32 devices in a mesh: dp: 2 (over x), row: 4 (over y, core), col: 4 (over z).
Axes of the slice: x: 2, y: 2, z: 4, core: 2. Of those that a mesh axis runs over, the one named last changes fastest.
Arguments:
- tokens: bfloat16 [4096, 4, 2048], P('col', 'dp', 'row'), may hold values from -6 to 6
- cotangent: bfloat16 [4096, 4, 2048], P('col', 'dp', 'row'), may hold values from -6 to 6
- block_labels: int32 [4, 4096], P('dp'), may hold values from 0 to 31, never falling along the last dimension, each value on 1 to 256 neighbouring positions
- adapter_selection: int32 [4], P('dp'), may hold values from 0 to 7
- adapter_scale: float32 [1], replicated, may hold values from 0.4 to 1.2
- attention_norm_gain: bfloat16 [2048], P('row'), may hold values from 0.099609375 to 1.8984375
- feedforward_norm_gain: bfloat16 [2048], P('row'), may hold values from 0.099609375 to 1.8984375
- query_weight: bfloat16 [2048, 2048], P('row', 'col'), may hold values from -0.125 to 0.125
- key_weight: bfloat16 [2048, 512], P('row', 'col'), may hold values from -0.125 to 0.125
- value_weight: bfloat16 [2048, 512], P('row', 'col'), may hold values from -0.125 to 0.125
- output_weight: bfloat16 [2048, 2048], P('col', 'row'), may hold values from -0.5 to 0.5
- gate_weight: bfloat16 [2048, 8192], P('row', 'col'), may hold values from -0.125 to 0.125
- up_weight: bfloat16 [2048, 8192], P('row', 'col'), may hold values from -0.125 to 0.125
- down_weight: bfloat16 [8192, 2048], P('col', 'row'), may hold values from -0.0625 to 0.0625
- query_first_factor: bfloat16 [2048, 128], P('row'), may hold values from -0.125 to 0.125
- query_second_factor: bfloat16 [128, 2048], P(None, 'col'), may hold values from -1.5 to 1.5
- key_first_factor: bfloat16 [2048, 128], P('row'), may hold values from -0.125 to 0.125
- key_second_factor: bfloat16 [128, 512], P(None, 'col'), may hold values from -1.5 to 1.5
- value_first_factor: bfloat16 [2048, 128], P('row'), may hold values from -0.125 to 0.125
- value_second_factor: bfloat16 [128, 512], P(None, 'col'), may hold values from -1.5 to 1.5
- output_first_factor: bfloat16 [2048, 128], P('col'), may hold values from -0.5 to 0.5
- output_second_factor: bfloat16 [128, 2048], P(None, 'row'), may hold values from -1.5 to 1.5
- gate_first_factor: bfloat16 [2048, 128], P('row'), may hold values from -0.125 to 0.125
- gate_second_factor: bfloat16 [128, 8192], P(None, 'col'), may hold values from -1.5 to 1.5
- up_first_factor: bfloat16 [2048, 128], P('row'), may hold values from -0.125 to 0.125
- up_second_factor: bfloat16 [128, 8192], P(None, 'col'), may hold values from -1.5 to 1.5
- down_first_factor: bfloat16 [8192, 128], P('col'), may hold values from -0.0625 to 0.0625
- down_second_factor: bfloat16 [128, 2048], P(None, 'row'), may hold values from -1.5 to 1.5
Outputs:
- mixed: bfloat16 [4096, 4, 2048], P('col', 'dp', 'row')
- grad_tokens: bfloat16 [4096, 4, 2048], P('col', 'dp', 'row')
- query_first_gradient: float32 [2048, 128], P('row')
- query_second_gradient: float32 [128, 2048], P(None, 'col')
- key_first_gradient: float32 [2048, 128], P('row')
- key_second_gradient: float32 [128, 512], P(None, 'col')
- value_first_gradient: float32 [2048, 128], P('row')
- value_second_gradient: float32 [128, 512], P(None, 'col')
- output_first_gradient: float32 [2048, 128], P('col')
- output_second_gradient: float32 [128, 2048], P(None, 'row')
- gate_first_gradient: float32 [2048, 128], P('row')
- gate_second_gradient: float32 [128, 8192], P(None, 'col')
- up_first_gradient: float32 [2048, 128], P('row')
- up_second_gradient: float32 [128, 8192], P(None, 'col')
- down_first_gradient: float32 [8192, 128], P('col')
- down_second_gradient: float32 [128, 2048], P(None, 'row')
The draws below stay inside these ranges and needn't reach their ends.
Inputs may be any that keep to these rules, and one draw needn't show every extreme that they name: `block_labels`: in each sequence block numbers never fall; each block holds 1 to 256 positions, one exactly 256.
All inputs are finite; a program needn't handle non-finite values.
Results may differ from the reference program's by a relative error of at most 0.035.
Values may be sent and summed in bfloat16 or wider, within the bound.
No kernel may reach another device: no remote copies, remote signals or barrier semaphores. Data moves between devices by JAX's collectives and lax.ppermute only.
A program may use at most 704 MiB of HBM per device.

```python
import math
import jax
import jax.numpy as jnp
import numpy as np
from jax import lax

D = 2048
HEADS = 32
KV_HEADS = 8
HEAD_DIM = 64
FF = 8192
ADAPTERS = 8
RANK = 16
LEN = 4096
BLOCK_MOST = 256
BLOCKS = 32
SEQS = 4
QD = 2048
KVD = 512
AR = 128


def touch_ends(entries, stream_key, least, top_value):
    index_at = [jax.random.randint(jax.random.fold_in(stream_key, axis), (), 0, length) for axis, length in enumerate(entries.shape)]
    main_axis = entries.shape.index(max(entries.shape))
    next_to = index_at[:main_axis] + [(index_at[main_axis] + 1) % entries.shape[main_axis]] + index_at[main_axis + 1:]
    return entries.at[tuple(index_at)].set(least).at[tuple(next_to)].set(top_value)


def levels(stream_key, shape, split, smallest, high):
    def one(axis_at, parts):
        draws = jax.random.uniform(jax.random.fold_in(jax.random.fold_in(stream_key, 6), axis_at), (parts,), jnp.float32, smallest / len(split), high / len(split))
        return jnp.repeat(jnp.exp(draws), shape[axis_at] // parts).reshape((-1,) + (1,) * (len(shape) - axis_at - 1))

    gain = one(*split[0])
    for cut in split[1:]:
        gain = gain * one(*cut)
    return gain


def profile(count, total, reach, lean):
    loads = [(1 << 20) // math.isqrt(rank ** lean) + 1 for rank in range(2, count + 1)]
    surplus, given = total - reach - (count - 1), [1] * (count - 1)
    while surplus > 0:
        movable = [i for i in range(count - 1) if given[i] < reach]
        mass, left = sum([loads[i] for i in movable]), surplus
        for i in movable:
            extra = min(reach - given[i], max(1, left * loads[i] // mass), surplus)
            given[i] = given[i] + extra
            surplus = surplus - extra
    return np.array([reach] + given)


def ragged_sizes(stream_key, number_of, total, most, slope):
    if number_of == 2:
        one = jax.random.randint(stream_key, (), max(1, total - most), min(most, total - 1) + 1)
        return jnp.stack([one, total - one])
    sizes = jnp.asarray(profile(number_of, total, most, slope), jnp.int32)
    pairs = (number_of - 1) // 2
    donor, taker = sizes[1:1 + 2 * pairs:2], sizes[2:2 + 2 * pairs:2]
    room = jnp.minimum(donor - 1, most - taker)
    shifted = jax.random.randint(jax.random.fold_in(stream_key, 1), (pairs,), 0, 1 << 20) % (room + 1)
    sizes = sizes.at[1:1 + 2 * pairs:2].set(donor - shifted).at[2:2 + 2 * pairs:2].set(taker + shifted)
    return sizes[jax.random.permutation(jax.random.fold_in(stream_key, 2), number_of)]


def normal_values(stream_key, extent, scale, reach, split=(), held_as=jnp.bfloat16):
    entries = jax.random.normal(stream_key, extent, jnp.float32) * scale
    if len(split) > 0:
        entries = levels(stream_key, extent, split, -0.22, 0.18) * entries
    return jnp.clip(entries, min=-reach, max=reach).astype(held_as)


def setup_inputs(seed: int = 0) -> dict:
    seeds = jax.random.split(jax.random.key(seed), 29)
    return {
        "tokens": normal_values(seeds[0], (LEN, SEQS, D), 1.0, 6.0, ((0, 4), (1, 2), (2, 4))),
        "cotangent": normal_values(seeds[1], (LEN, SEQS, D), 1.0, 6.0, ((0, 4), (1, 2), (2, 4))),
        "block_labels": jax.vmap(lambda own: jnp.searchsorted(jnp.cumsum(ragged_sizes(own, BLOCKS, LEN, BLOCK_MOST, 0)), jnp.arange(LEN), side="right"))(jax.random.split(seeds[2], SEQS)).reshape((SEQS, LEN)).astype(jnp.int32),
        "adapter_selection": touch_ends(jax.random.randint(seeds[3], (SEQS,), 0, ADAPTERS), jax.random.fold_in(seeds[3], 1), 0, ADAPTERS - 1).astype(jnp.int32),
        "adapter_scale": jnp.clip(jnp.exp(jax.random.uniform(seeds[4], (1,), jnp.float32, math.log(0.4), math.log(1.2))), 0.4, 1.2),
        "attention_norm_gain": jnp.clip(1.0 + 0.18 * jax.random.normal(seeds[5], (D,), jnp.float32), 0.099609375, 1.8984375).astype(jnp.bfloat16),
        "feedforward_norm_gain": jnp.clip(1.0 + 0.18 * jax.random.normal(seeds[6], (D,), jnp.float32), 0.099609375, 1.8984375).astype(jnp.bfloat16),
        "query_weight": normal_values(seeds[7], (D, QD), D ** -0.5, 0.125, ((0, 4), (1, 4))),
        "key_weight": normal_values(seeds[8], (D, KVD), D ** -0.5, 0.125, ((0, 4), (1, 4))),
        "value_weight": normal_values(seeds[9], (D, KVD), D ** -0.5, 0.125, ((0, 4), (1, 4))),
        "output_weight": normal_values(seeds[10], (QD, D), (QD // 16) ** -0.5, 0.5, ((0, 4), (1, 4))),
        "gate_weight": normal_values(seeds[11], (D, FF), D ** -0.5, 0.125, ((0, 4), (1, 4))),
        "up_weight": normal_values(seeds[12], (D, FF), D ** -0.5, 0.125, ((0, 4), (1, 4))),
        "down_weight": normal_values(seeds[13], (FF, D), FF ** -0.5, 0.0625, ((0, 4), (1, 4))),
        "query_first_factor": normal_values(seeds[14], (D, AR), D ** -0.5, 0.125, ((0, 4),)),
        "query_second_factor": normal_values(seeds[15], (AR, QD), RANK ** -0.5, 1.5, ((1, 4),)),
        "key_first_factor": normal_values(seeds[16], (D, AR), D ** -0.5, 0.125, ((0, 4),)),
        "key_second_factor": normal_values(seeds[17], (AR, KVD), RANK ** -0.5, 1.5, ((1, 4),)),
        "value_first_factor": normal_values(seeds[18], (D, AR), D ** -0.5, 0.125, ((0, 4),)),
        "value_second_factor": normal_values(seeds[19], (AR, KVD), RANK ** -0.5, 1.5, ((1, 4),)),
        "output_first_factor": normal_values(seeds[20], (QD, AR), (QD // 16) ** -0.5, 0.5, ((0, 4),)),
        "output_second_factor": normal_values(seeds[21], (AR, D), RANK ** -0.5, 1.5, ((1, 4),)),
        "gate_first_factor": normal_values(seeds[22], (D, AR), D ** -0.5, 0.125, ((0, 4),)),
        "gate_second_factor": normal_values(seeds[23], (AR, FF), RANK ** -0.5, 1.5, ((1, 4),)),
        "up_first_factor": normal_values(seeds[24], (D, AR), D ** -0.5, 0.125, ((0, 4),)),
        "up_second_factor": normal_values(seeds[25], (AR, FF), RANK ** -0.5, 1.5, ((1, 4),)),
        "down_first_factor": normal_values(seeds[26], (FF, AR), FF ** -0.5, 0.0625, ((0, 4),)),
        "down_second_factor": normal_values(seeds[27], (AR, D), RANK ** -0.5, 1.5, ((1, 4),)),
    }


EPS = 1e-05
ROPE_BASE = 500000.0
TOP_PRECISION = lax.Precision.HIGHEST

@jax.custom_vjp
def low(v):
    return lax.optimization_barrier(v.astype(jnp.bfloat16)).astype(jnp.float32)

@jax.custom_vjp
def low_back(v):
    return v

def low_keep(v):
    return (low(v), None)

def low_pass(kept, grad):
    return (grad,)

def back_keep(v):
    return (v, None)

def back_low(kept, grad):
    return (low(grad),)
low.defvjp(low_keep, low_pass)
low_back.defvjp(back_keep, back_low)

def rms_norm(values, norm_gain):
    inverse = lax.rsqrt(lax.optimization_barrier(jnp.mean(values * values, axis=-1, keepdims=True)) + EPS)
    return values * inverse * norm_gain

def rotate(values, positions):
    half_dim = values.shape[-1] // 2
    frequency = ROPE_BASE ** (-(jnp.arange(half_dim).astype(jnp.float32) * 2.0) / values.shape[-1])
    angles = positions.astype(jnp.float32)[:, None] * frequency[None, :]
    cosine = jnp.concatenate([jnp.cos(angles), jnp.cos(angles)], axis=-1)[:, None, :]
    sine_table = jnp.concatenate([jnp.sin(angles), jnp.sin(angles)], axis=-1)[:, None, :]
    turned = jnp.concatenate([-values[..., half_dim:], values[..., :half_dim]], axis=-1)
    return values * cosine + turned * sine_table

def attention(queries, key_rows, value_rows, block_list):
    seq_len, head_count, head_dim = queries.shape
    groups = key_rows.shape[1]
    repeat = head_count // groups
    query_rows = math.gcd(seq_len, 512)
    block_count = seq_len // query_rows
    grouped = queries.reshape(block_count, query_rows, groups, repeat, head_dim)
    query_blocks = block_list.reshape(block_count, query_rows)
    factor = head_dim ** (-0.5)

    def one_block(block_item):
        block_queries, query_ids = block_item
        scores = jnp.einsum('qgre,kge->grqk', block_queries, key_rows, precision=TOP_PRECISION) * factor
        scores = low_back(scores)
        allowed = block_list[None, :] <= query_ids[:, None]
        scores = jnp.where(allowed[None, None], scores, -1e+30)
        weight_set = low(jax.nn.softmax(scores, axis=-1))
        return jnp.einsum('grqk,kge->qgre', weight_set, value_rows, precision=TOP_PRECISION)
    mixed = lax.map(jax.checkpoint(one_block), (grouped, query_blocks))
    return mixed.reshape(seq_len, head_count * head_dim)

def layer_params(sequence_tokens, gain_vectors, weight_set, adapter_bundle, selection_mask, adapter_factor, block_list):
    seq_len = sequence_tokens.shape[0]
    positions = jnp.arange(seq_len)
    query_weight, key_weight, value_weight, output_weight, gate_weight, up_weight, down_weight = weight_set
    query_first_factor, query_second_factor, key_first_factor, key_second_factor, value_first_factor, value_second_factor, output_first_factor, output_second_factor, gate_first_factor, gate_second_factor, up_first_factor, up_second_factor, down_first_factor, down_second_factor = adapter_bundle

    def project(input_rows, weight_matrix, down_map, upward_mapping):
        reduced_rows = jnp.dot(input_rows, down_map, precision=TOP_PRECISION) * selection_mask
        return jnp.dot(input_rows, weight_matrix, precision=TOP_PRECISION) + adapter_factor * jnp.dot(reduced_rows, upward_mapping, precision=TOP_PRECISION)
    normed = low(rms_norm(sequence_tokens, gain_vectors[0]))
    query_raw = low_back(project(normed, query_weight, query_first_factor, query_second_factor))
    key_raw = low_back(project(normed, key_weight, key_first_factor, key_second_factor))
    value_raw = low_back(project(normed, value_weight, value_first_factor, value_second_factor))
    queries = low(rotate(query_raw.reshape(seq_len, HEADS, HEAD_DIM), positions))
    key_rows = low(rotate(key_raw.reshape(seq_len, KV_HEADS, HEAD_DIM), positions))
    value_rows = low(value_raw.reshape(seq_len, KV_HEADS, HEAD_DIM))
    heads_out = low_back(low(attention(queries, key_rows, value_rows, block_list)))
    attended = sequence_tokens + low_back(project(heads_out, output_weight, output_first_factor, output_second_factor))
    normed_mlp = low(rms_norm(attended, gain_vectors[1]))
    gate_raw = low_back(project(normed_mlp, gate_weight, gate_first_factor, gate_second_factor))
    upward = low_back(project(normed_mlp, up_weight, up_first_factor, up_second_factor))
    hidden = low(jax.nn.silu(gate_raw) * upward)
    return attended + low_back(project(hidden, down_weight, down_first_factor, down_second_factor))

def reference(tokens, cotangent, block_labels, adapter_selection, adapter_scale, attention_norm_gain, feedforward_norm_gain, query_weight, key_weight, value_weight, output_weight, gate_weight, up_weight, down_weight, query_first_factor, query_second_factor, key_first_factor, key_second_factor, value_first_factor, value_second_factor, output_first_factor, output_second_factor, gate_first_factor, gate_second_factor, up_first_factor, up_second_factor, down_first_factor, down_second_factor):
    weight_set = tuple((matrix.astype(jnp.float32) for matrix in (query_weight, key_weight, value_weight, output_weight, gate_weight, up_weight, down_weight)))
    adapter_bundle = tuple((matrix.astype(jnp.float32) for matrix in (query_first_factor, query_second_factor, key_first_factor, key_second_factor, value_first_factor, value_second_factor, output_first_factor, output_second_factor, gate_first_factor, gate_second_factor, up_first_factor, up_second_factor, down_first_factor, down_second_factor)))
    gain_vectors = (attention_norm_gain.astype(jnp.float32), feedforward_norm_gain.astype(jnp.float32))
    adapter_factor = adapter_scale[0]
    columns = jnp.arange(ADAPTERS * RANK).astype(jnp.int32) // RANK

    def per_sequence(totals, seq_item):
        token_seq, cot_seq, block_list, pick_one = seq_item
        selection_mask = (columns == pick_one).astype(jnp.float32)

        def forward(token_argument, adapter_arguments):
            return layer_params(token_argument, gain_vectors, weight_set, adapter_arguments, selection_mask, adapter_factor, block_list)
        outputs, pull_back = jax.vjp(forward, token_seq, adapter_bundle)
        token_grad, adapter_grads = pull_back(cot_seq)
        totals = tuple((total_now + grad_now for total_now, grad_now in zip(totals, adapter_grads)))
        return (totals, (outputs, token_grad))
    seq_tokens = jnp.moveaxis(tokens.astype(jnp.float32), 1, 0)
    seq_cotangents = jnp.moveaxis(cotangent.astype(jnp.float32), 1, 0)
    zero_grads = tuple((jnp.zeros(matrix.shape, jnp.float32) for matrix in adapter_bundle))
    grads_all, (outs_all, token_grads) = lax.scan(per_sequence, zero_grads, (seq_tokens, seq_cotangents, block_labels, adapter_selection))
    mixed = jnp.moveaxis(outs_all, 0, 1).astype(jnp.bfloat16)
    grad_tokens = jnp.moveaxis(token_grads, 0, 1).astype(jnp.bfloat16)
    return (mixed, grad_tokens, grads_all[0], grads_all[1], grads_all[2], grads_all[3], grads_all[4], grads_all[5], grads_all[6], grads_all[7], grads_all[8], grads_all[9], grads_all[10], grads_all[11], grads_all[12], grads_all[13])
```

```python
import functools, math
import jax, jax.numpy as jnp
from jax import lax
from jax.sharding import PartitionSpec as P
from jax.experimental import pallas as pl
from jax.experimental.pallas import tpu as pltpu

HEAD_DIM = 64
RANK = 16
BLOCKS = 32
EPS = 1e-05
ROPE_BASE = 500000.0
TILE = 512
REACH = 256
LOG2E = math.log2(math.e)
NEG = -1e30


def nt(a, b):
    return lax.dot_general(a, b, (((1,), (1,)), ((), ())), preferred_element_type=jnp.float32)


def nn(a, b):
    return lax.dot_general(a, b, (((1,), (0,)), ((), ())), preferred_element_type=jnp.float32)


def half_of(x, e):
    lane = lax.broadcasted_iota(jnp.int32, x.shape, 1)
    return jnp.where((lane < 64) if e == 0 else (lane >= 64), x, jnp.zeros_like(x))


def fwd_kernel(heads, factor, end_ref, q_ref, k2_ref, vt_ref, o_ref, lse_ref, acc_ref, m_ref, l_ref):
    i = pl.program_id(0)
    tq = q_ref.shape[0]
    q0 = i * tq
    c = factor * LOG2E
    ends = end_ref[...]
    m_ref[...] = jnp.full_like(m_ref, NEG)
    l_ref[...] = jnp.zeros_like(l_ref)
    acc_ref[...] = jnp.zeros_like(acc_ref)

    def tile(k0, size, masked):
        kk = k2_ref[pl.ds(k0, size), :]
        vv = vt_ref[:, pl.ds(k0, size)]
        if masked:
            allowed = (lax.broadcasted_iota(jnp.int32, (size, tq), 0) + k0) < ends
        for h in range(heads):
            qh = half_of(q_ref[:, (h // 2) * 128:(h // 2 + 1) * 128], h % 2)
            s = nt(kk, qh) * c
            if masked:
                s = jnp.where(allowed, s, NEG)
            m_old = m_ref[h:h + 1, :]
            m_new = jnp.maximum(m_old, jnp.max(s, axis=0, keepdims=True))
            p = jnp.exp2(s - m_new)
            alpha = jnp.exp2(m_old - m_new)
            l_ref[h:h + 1, :] = l_ref[h:h + 1, :] * alpha + jnp.sum(p, axis=0, keepdims=True)
            m_ref[h:h + 1, :] = m_new
            a = pl.ds(h * 64, 64)
            acc_ref[a, :] = acc_ref[a, :] * alpha + nn(vv, p.astype(jnp.bfloat16))

    def body(j, _):
        tile(pl.multiple_of(j * tq, tq), tq, False)
        return 0

    lax.fori_loop(0, i, body, 0)
    tile(pl.multiple_of(q0, tq), tq, True)

    @pl.when(i < pl.num_programs(0) - 1)
    def _():
        tile(pl.multiple_of(q0 + tq, REACH), REACH, True)

    lse_ref[...] = m_ref[...] + jnp.log2(l_ref[...])
    inv = 1.0 / l_ref[...]
    for p in range(o_ref.shape[1] // 128):
        parts = []
        for h in (2 * p, 2 * p + 1):
            if h < heads:
                parts.append(acc_ref[h * 64:(h + 1) * 64, :] * inv[h:h + 1, :])
            else:
                parts.append(jnp.zeros((64, tq), jnp.float32))
        o_ref[:, p * 128:(p + 1) * 128] = jnp.concatenate(parts, axis=0).T.astype(o_ref.dtype)


def attend(q, k2, vt, ends, heads, factor):
    length, width = q.shape
    tq = min(TILE, length)
    rows = 8
    return pl.pallas_call(
        functools.partial(fwd_kernel, heads, factor),
        grid=(length // tq,),
        in_specs=[
            pl.BlockSpec((1, tq), lambda i: (0, i)),
            pl.BlockSpec((tq, width), lambda i: (i, 0)),
            pl.BlockSpec((length, 128), lambda i: (0, 0)),
            pl.BlockSpec((64, length), lambda i: (0, 0)),
        ],
        out_specs=[
            pl.BlockSpec((tq, width), lambda i: (i, 0)),
            pl.BlockSpec((rows, tq), lambda i: (0, i)),
        ],
        out_shape=[
            jax.ShapeDtypeStruct((length, width), jnp.bfloat16),
            jax.ShapeDtypeStruct((rows, length), jnp.float32),
        ],
        scratch_shapes=[
            pltpu.VMEM((heads * 64, tq), jnp.float32),
            pltpu.VMEM((rows, tq), jnp.float32),
            pltpu.VMEM((rows, tq), jnp.float32),
        ],
        compiler_params=pltpu.CompilerParams(vmem_limit_bytes=48 * 2**20),
        cost_estimate=pl.CostEstimate(
            flops=2 * heads * length * length * 64, bytes_accessed=4 * length * width + length * 384, transcendentals=heads * length * length // 2
        ),
        name="attend_forward",
    )(ends, q, k2, vt)


def bwd_kernel(heads, factor, end_ref, q_ref, do_ref, o_ref, lse_ref, k2_ref, v2_ref, kt_ref, dq_ref, dkv_ref, dqt_ref, delta_ref, dk_ref, dv_ref):
    j = pl.program_id(0)
    n = pl.num_programs(0)
    tk = k2_ref.shape[0]
    length, width = q_ref.shape
    c = factor * LOG2E

    @pl.when(j == 0)
    def _():
        dqt_ref[...] = jnp.zeros_like(dqt_ref)
        delta_ref[...] = jnp.zeros_like(delta_ref)
        for t in range(length // tk):
            rows = slice(t * tk, (t + 1) * tk)
            for p in range(width // 128):
                prod = do_ref[rows, p * 128:(p + 1) * 128].astype(jnp.float32) * o_ref[rows, p * 128:(p + 1) * 128].astype(jnp.float32)
                turned = prod.T
                for h in (2 * p, 2 * p + 1):
                    if h < heads:
                        delta_ref[h:h + 1, rows] = jnp.sum(turned[(h % 2) * 64:(h % 2 + 1) * 64, :], axis=0, keepdims=True)

    dk_ref[...] = jnp.zeros_like(dk_ref)
    dv_ref[...] = jnp.zeros_like(dv_ref)

    def tile(q0, size, masked):
        rows = pl.ds(q0, tk)
        kk = k2_ref[:size, :]
        vv = v2_ref[:size, :]
        kt = kt_ref[:, :size]
        if masked:
            allowed = (lax.broadcasted_iota(jnp.int32, (size, tk), 0) + j * tk) < end_ref[:, rows]
        for h in range(heads):
            lanes = slice((h // 2) * 128, (h // 2 + 1) * 128)
            qh = half_of(q_ref[rows, lanes], h % 2)
            gh = half_of(do_ref[rows, lanes], h % 2)
            s = nt(kk, qh) * c - lse_ref[h:h + 1, rows]
            if masked:
                s = jnp.where(allowed, s, NEG)
            p = jnp.exp2(s)
            dp = nt(vv, gh)
            ds = (p * (dp - delta_ref[h:h + 1, rows])).astype(jnp.bfloat16)
            dv_ref[:size, :] += nn(p.astype(jnp.bfloat16), gh)
            dk_ref[:size, :] += nn(ds, qh)
            dqt_ref[h * 64:(h + 1) * 64, rows] += nn(kt, ds)

    @pl.when(j > 0)
    def _():
        tile(pl.multiple_of((j - 1) * tk, tk), REACH, True)

    tile(pl.multiple_of(j * tk, tk), tk, True)

    def body(i, _):
        tile(pl.multiple_of(i * tk, tk), tk, False)
        return 0

    lax.fori_loop(j + 1, n, body, 0)

    lane = lax.broadcasted_iota(jnp.int32, (tk, 128), 1)
    dk = dk_ref[...]
    dv = dv_ref[...]
    dk = (dk + pltpu.roll(dk, 64, 1)) * factor
    dv = dv + pltpu.roll(dv, 64, 1)
    dkv_ref[...] = jnp.where(lane < 64, dk, dv).astype(dkv_ref.dtype)

    @pl.when(j == n - 1)
    def _():
        for t in range(length // tk):
            rows = slice(t * tk, (t + 1) * tk)
            for p in range(width // 128):
                lo = 2 * p * 64
                if 2 * p + 1 < heads:
                    blk = dqt_ref[lo:lo + 128, rows]
                else:
                    blk = jnp.concatenate([dqt_ref[lo:lo + 64, rows], jnp.zeros((64, tk), jnp.float32)], axis=0)
                dq_ref[rows, p * 128:(p + 1) * 128] = (blk.T * factor).astype(dq_ref.dtype)


def attend_back(q, do, o, lse, k2, v2, kt, ends, heads, factor, out_dtype=jnp.bfloat16):
    length, width = q.shape
    tk = min(TILE, length)
    whole = lambda shape: pl.BlockSpec(shape, lambda j: (0, 0))
    return pl.pallas_call(
        functools.partial(bwd_kernel, heads, factor),
        grid=(length // tk,),
        in_specs=[
            whole((1, length)),
            whole((length, width)),
            whole((length, width)),
            whole((length, width)),
            whole((8, length)),
            pl.BlockSpec((tk, 128), lambda j: (j, 0)),
            pl.BlockSpec((tk, 128), lambda j: (j, 0)),
            pl.BlockSpec((64, tk), lambda j: (0, j)),
        ],
        out_specs=[
            whole((length, width)),
            pl.BlockSpec((tk, 128), lambda j: (j, 0)),
        ],
        out_shape=[
            jax.ShapeDtypeStruct((length, width), out_dtype),
            jax.ShapeDtypeStruct((length, 128), out_dtype),
        ],
        scratch_shapes=[
            pltpu.VMEM((heads * 64, length), jnp.float32),
            pltpu.VMEM((8, length), jnp.float32),
            pltpu.VMEM((tk, 128), jnp.float32),
            pltpu.VMEM((tk, 128), jnp.float32),
        ],
        compiler_params=pltpu.CompilerParams(vmem_limit_bytes=48 * 2**20),
        cost_estimate=pl.CostEstimate(
            flops=5 * heads * length * length * 64, bytes_accessed=8 * length * width + length * 512, transcendentals=heads * length * length // 2
        ),
        name="attend_backward",
    )(ends, q, do, o, lse, k2, v2, kt)


def dot(left, right):
    return lax.dot_general(left, right, (((1,), (0,)), ((), ())), preferred_element_type=jnp.float32)


def dot_turned(left, right):
    return lax.dot_general(left, right, (((1,), (1,)), ((), ())), preferred_element_type=jnp.float32)


def over_tokens(left, right):
    return lax.dot_general(left, right, (((0,), (0,)), ((), ())), preferred_element_type=jnp.float32)


def low(values):
    return values.astype(jnp.bfloat16)


def inverse_rms(values):
    return lax.rsqrt(jnp.mean(values * values, axis=-1, keepdims=True) + EPS)


def norm_back(values, gain, inverse, upstream):
    scaled = upstream * gain
    weighted = jnp.mean(scaled * values, axis=-1, keepdims=True)
    return inverse * scaled - values * (inverse * inverse * inverse) * weighted


def to_tokens(values):
    rows = lax.axis_size("row")
    part, seqs, features = values.shape
    cut = values.reshape(rows, part // rows, seqs, features).transpose(0, 2, 1, 3)
    moved = lax.all_to_all(cut, "row", 0, 0, tiled=True)
    return moved.transpose(1, 2, 0, 3).reshape(seqs * (part // rows), rows * features)


def to_features(values, seqs):
    rows = lax.axis_size("row")
    width = values.shape[1] // rows
    cut = values.reshape(seqs, -1, rows, width).transpose(2, 0, 1, 3)
    moved = lax.all_to_all(cut, "row", 0, 0, tiled=True)
    return moved.transpose(0, 2, 1, 3).reshape(-1, seqs, width)


def rope_tables(positions, lanes):
    half = HEAD_DIM // 2
    frequency = ROPE_BASE ** (-(jnp.arange(half).astype(jnp.float32) * 2.0) / HEAD_DIM)
    angles = positions.astype(jnp.float32)[:, None] * frequency[None, :]
    copies = (1, lanes // half)
    return lax.optimization_barrier((jnp.tile(jnp.cos(angles), copies), jnp.tile(jnp.sin(angles), copies)))


def spread(table, width):
    return jnp.concatenate([table] * pl.cdiv(width, table.shape[1]), axis=1)[:, :width]


def turn(values, sign):
    half = HEAD_DIM // 2
    ahead = jnp.concatenate([values[:, half:], values[:, :half]], axis=1)
    behind = jnp.concatenate([values[:, -half:], values[:, :-half]], axis=1)
    lane = lax.broadcasted_iota(jnp.int32, values.shape, 1)
    return jnp.where(lane % HEAD_DIM < half, sign * ahead, -sign * behind)


def rope(values, cosine, sine):
    width = values.shape[1]
    return values * spread(cosine, width) + turn(values, -1.0) * spread(sine, width)


def rope_back(values, cosine, sine):
    width = values.shape[1]
    return values * spread(cosine, width) + turn(values * spread(sine, width), 1.0)


def diagonal(blocks):
    total = sum(b.shape[1] for b in blocks)
    out, at = [], 0
    for b in blocks:
        out.append(jnp.pad(b, ((0, 0), (at, total - at - b.shape[1]))))
        at += b.shape[1]
    return jnp.concatenate(out, axis=0)


def local(
    tokens,
    cotangent,
    block_labels,
    adapter_selection,
    adapter_scale,
    attention_norm_gain,
    feedforward_norm_gain,
    query_weight,
    key_weight,
    value_weight,
    output_weight,
    gate_weight,
    up_weight,
    down_weight,
    query_first_factor,
    query_second_factor,
    key_first_factor,
    key_second_factor,
    value_first_factor,
    value_second_factor,
    output_first_factor,
    output_second_factor,
    gate_first_factor,
    gate_second_factor,
    up_first_factor,
    up_second_factor,
    down_first_factor,
    down_second_factor,
):
    copies, rows, cols = lax.axis_size("dp"), lax.axis_size("row"), lax.axis_size("col")
    me = lax.axis_index("dp")
    units = rows * cols
    both, turned_both = ("row", "col"), ("col", "row")
    seqs = tokens.shape[1]
    part = tokens.shape[0] // rows
    length = part * units
    features = tokens.shape[2] * rows
    scale = adapter_scale[0]
    width_q, width_kv = query_weight.shape[1], key_weight.shape[1]
    width_qkv = width_q + 2 * width_kv
    width_ff = gate_weight.shape[1] // copies
    kv_heads = width_kv * cols // HEAD_DIM
    heads = width_q * cols // HEAD_DIM * seqs // units
    kv_copies = max(1, units // (seqs * kv_heads))
    adapter_cols = query_first_factor.shape[1]
    rank = seqs * RANK
    factor = HEAD_DIM ** (-0.5)

    picked = lax.all_gather(adapter_selection, "dp", axis=0, tiled=True)
    owner = jnp.arange(adapter_cols)
    slot = jnp.arange(copies * rank)
    choose = (owner[:, None] // RANK == picked[slot // RANK][None, :]) & (owner[:, None] % RANK == slot[None, :] % RANK)
    choose_low = choose.astype(jnp.bfloat16)
    choose_wide = choose.astype(jnp.float32)
    choose_own = lax.dynamic_slice_in_dim(choose_low, me * rank, rank, 1)

    def first_of(matrix, chosen):
        return low(dot(matrix, chosen))

    def second_of(matrix, chosen):
        return low(over_tokens(chosen, matrix))

    half = me * width_ff
    gate_half = lax.dynamic_slice_in_dim(gate_weight, half, width_ff, 1)
    up_half = lax.dynamic_slice_in_dim(up_weight, half, width_ff, 1)
    down_half = lax.dynamic_slice_in_dim(down_weight, half, width_ff, 0)
    gate_second_half = lax.dynamic_slice_in_dim(gate_second_factor, half, width_ff, 1)
    up_second_half = lax.dynamic_slice_in_dim(up_second_factor, half, width_ff, 1)
    down_first_half = lax.dynamic_slice_in_dim(down_first_factor, half, width_ff, 0)

    first_parts = [first_of(m, choose_own) for m in (query_first_factor, key_first_factor, value_first_factor)]
    first_parts += [first_of(m, choose_low) for m in (gate_first_factor, up_first_factor)]
    first_parts += [attention_norm_gain[:, None], feedforward_norm_gain[:, None]]
    first_rows = lax.all_gather(jnp.concatenate(first_parts, axis=1), "row", axis=0, tiled=True)
    qkv_weight = lax.all_gather(
        jnp.concatenate([query_weight, key_weight, value_weight], axis=1), turned_both, axis=0, tiled=True
    ).reshape(cols, features, width_qkv)
    qkv_second = lax.all_gather(
        diagonal([second_of(m, choose_own) for m in (query_second_factor, key_second_factor, value_second_factor)]),
        "col",
    )
    out_weight = lax.all_gather(output_weight, both, axis=0, tiled=True).reshape(rows, -1, output_weight.shape[1])
    second_rows = lax.all_gather(
        jnp.concatenate([second_of(output_second_factor, choose_own), second_of(down_second_factor, choose_low)], axis=0),
        "row",
    )
    out_first = lax.all_gather(first_of(output_first_factor, choose_own), "col", axis=0, tiled=True)
    front_weight = lax.all_gather(
        jnp.concatenate([gate_half, up_half], axis=1), turned_both, axis=0, tiled=True
    ).reshape(cols, features, 2 * width_ff)
    gate_second = second_of(gate_second_half, choose_low)
    up_second = second_of(up_second_half, choose_low)
    front_second = lax.all_gather(
        jnp.concatenate(
            [diagonal([gate_second[g * rank : (g + 1) * rank], up_second[g * rank : (g + 1) * rank]]) for g in range(copies)],
            axis=0,
        ),
        "col",
    )
    back_weight = lax.all_gather(down_half, both, axis=0, tiled=True).reshape(rows, -1, down_half.shape[1])
    down_first = lax.all_gather(first_of(down_first_half, choose_low), "col", axis=0, tiled=True)

    qkv_first = first_rows[:, : 3 * rank]
    gate_first = first_rows[:, 3 * rank : (3 + copies) * rank]
    up_first = first_rows[:, (3 + copies) * rank : (3 + 2 * copies) * rank]
    gains = first_rows[:, (3 + 2 * copies) * rank :].astype(jnp.float32).T
    out_second = second_rows[:, :rank]
    down_second = second_rows[:, rank:]

    row_seq = jnp.arange(seqs * part) // part
    mask = (row_seq[:, None] == jnp.arange(rank)[None, :] // RANK).astype(jnp.float32) * scale

    def masked(values):
        return low(values * jnp.tile(mask, (1, values.shape[1] // rank)))

    residual = to_tokens(tokens).astype(jnp.float32)
    upstream = to_tokens(cotangent)
    inverse_attn = inverse_rms(residual)
    normed = low(residual * inverse_attn * gains[0:1])
    low_qkv = masked(dot(normed, qkv_first))
    positions = (lax.axis_index("col") * rows + lax.axis_index("row")) * part + jnp.arange(part)
    cosine, sine = rope_tables(jnp.tile(positions, seqs), 2 * HEAD_DIM)
    query_parts, key_parts, value_parts = [], [], []
    for c in range(cols):
        raw = dot(normed, qkv_weight[c]) + dot(low_qkv, qkv_second[c])
        turned = low(rope(raw[:, : width_q + width_kv], cosine, sine))
        query_parts.append(turned[:, :width_q])
        key_parts.append(turned[:, width_q:])
        value_parts.append(low(raw[:, width_q + width_kv :]))

    def to_units(values, groups):
        return values.reshape(seqs, part, groups, -1).transpose(0, 2, 1, 3)

    def from_units(values):
        return values.transpose(0, 2, 1, 3).reshape(seqs * part, -1)

    def exchange(values):
        return lax.all_to_all(values.reshape(units, part, -1), turned_both, 0, 0, tiled=True)

    unit_width = heads * HEAD_DIM
    sent_queries = to_units(jnp.concatenate(query_parts, axis=1), units // seqs)
    sent_kv = jnp.concatenate(
        [to_units(jnp.concatenate(key_parts, axis=1), kv_heads), to_units(jnp.concatenate(value_parts, axis=1), kv_heads)],
        axis=-1,
    )
    sent_kv = jnp.repeat(sent_kv, kv_copies, axis=1)
    unit_in = exchange(jnp.concatenate([sent_queries, sent_kv], axis=-1)).reshape(length, -1)
    pad_width = -unit_width % 128
    unit_queries = jnp.pad(unit_in[:, :unit_width], ((0, 0), (0, pad_width)))
    unit_keys = unit_in[:, unit_width : unit_width + HEAD_DIM]
    unit_values = unit_in[:, unit_width + HEAD_DIM :]
    keys_twice = jnp.concatenate([unit_keys, unit_keys], axis=1)
    values_twice = jnp.concatenate([unit_values, unit_values], axis=1)
    unit_seq = (lax.axis_index("col") * rows + lax.axis_index("row")) * seqs // units
    labels = lax.dynamic_index_in_dim(block_labels, unit_seq, 0, keepdims=True)
    numbers = jnp.arange(BLOCKS)[:, None]
    ends_of = jnp.sum((labels <= numbers).astype(jnp.int32), axis=1, keepdims=True)
    ends = jnp.sum(jnp.where(labels == numbers, ends_of, 0), axis=0, keepdims=True)
    unit_out, log_sums = attend(unit_queries, keys_twice, unit_values.T, ends, heads, factor)
    heads_out = from_units(exchange(unit_out[:, :unit_width]).reshape(seqs, units // seqs, part, -1))
    low_out = masked(dot(heads_out, out_first))
    attended = residual + jnp.concatenate(
        [dot(heads_out, out_weight[r]) + dot(low_out, out_second[r]) for r in range(rows)], axis=1
    )
    inverse_mlp = inverse_rms(attended)
    normed_mlp = low(attended * inverse_mlp * gains[1:2])

    def swap(values, step):
        return lax.ppermute(values, "dp", [(i, (i + step) % copies) for i in range(copies)])

    mixed_part, grad_part = None, None
    row_sums, col_sums = [], []
    for step in range(copies):
        group = (me - step) % copies
        h = normed_mlp if step == 0 else swap(normed_mlp, step)
        e = upstream if step == 0 else swap(upstream, step)

        def of_group(values, axis):
            return lax.dynamic_slice_in_dim(values, group * rank, rank, axis)

        front_first = jnp.concatenate([of_group(gate_first, 1), of_group(up_first, 1)], axis=1)
        front_second_now = lax.dynamic_slice_in_dim(front_second, group * 2 * rank, 2 * rank, 1)
        down_first_now = of_group(down_first, 1)
        down_second_now = of_group(down_second, 1)
        low_front = masked(dot(h, front_first))
        lowered_down = masked(
            sum(dot_turned(e[:, r * features // rows : (r + 1) * features // rows], down_second_now[r]) for r in range(rows))
        )
        hidden_grad = jnp.einsum(
            "mrn,rfn->mf", e.reshape(e.shape[0], rows, -1), back_weight, preferred_element_type=jnp.float32
        ) + dot_turned(lowered_down, down_first_now)
        hidden_parts, front_parts = [], []
        for c in range(cols):
            raw = dot(h, front_weight[c]) + dot(low_front, front_second_now[c])
            gate, up = raw[:, :width_ff], raw[:, width_ff:]
            upstream_now = hidden_grad[:, c * width_ff : (c + 1) * width_ff]
            sigmoid = jax.nn.sigmoid(gate)
            hidden_parts.append(low(gate * sigmoid * up))
            front_parts.append(
                jnp.concatenate(
                    [low(upstream_now * up * sigmoid * (1.0 + gate * (1.0 - sigmoid))), low(upstream_now * gate * sigmoid)],
                    axis=1,
                )
            )
        hidden = jnp.concatenate(hidden_parts, axis=1)
        lowered_front = masked(sum(dot_turned(front_parts[c], front_second_now[c]) for c in range(cols)))
        grad = sum(dot_turned(front_parts[c], front_weight[c]) for c in range(cols)) + dot_turned(lowered_front, front_first)
        low_down = masked(dot(hidden, down_first_now))
        mixed = jnp.concatenate(
            [dot(hidden, back_weight[r]) + dot(low_down, down_second_now[r]) for r in range(rows)], axis=1
        )
        row_sums.append(jnp.concatenate([over_tokens(lowered_front, h), over_tokens(low_down, e)], axis=0))
        gate_up_sums = [over_tokens(low_front, front_parts[c]) for c in range(cols)]
        col_sums.append(
            jnp.concatenate(
                [
                    jnp.concatenate([g[:rank, :width_ff] for g in gate_up_sums], axis=1),
                    jnp.concatenate([g[rank:, width_ff:] for g in gate_up_sums], axis=1),
                    over_tokens(lowered_down, hidden),
                ],
                axis=0,
            )
        )
        if step == 0:
            mixed_part, grad_part = mixed, grad
        else:
            grad_part = grad_part + swap(low(grad), -step).astype(jnp.float32)
            mixed_part = mixed_part + swap(low(mixed), -step).astype(jnp.float32)

    def by_group(values):
        stacked = jnp.stack(values)
        return jnp.concatenate(
            [lax.dynamic_index_in_dim(stacked, (me - g) % copies, 0, keepdims=False) for g in range(copies)], axis=0
        )

    def own_group(values):
        return jnp.concatenate([jnp.where(me == g, values, 0.0) for g in range(copies)], axis=0)

    def sum_rows(values):
        cut = values.reshape(values.shape[0], rows, -1).transpose(1, 0, 2)
        return lax.psum(lax.psum_scatter(cut, "row", scatter_dimension=0), ("col", "dp"))

    def sum_cols(values, axes):
        cut = values.reshape(values.shape[0], cols, -1).transpose(1, 0, 2)
        return lax.psum(lax.psum_scatter(cut, "col", scatter_dimension=0), axes)

    def slots(values, count, at):
        return values.reshape(copies, count, rank, -1)[:, at].reshape(copies * rank, -1)

    def wide_second(values):
        return lax.dot_general(
            choose_wide, values, (((1,), (0,)), ((), ())), precision=lax.Precision.HIGHEST, preferred_element_type=jnp.float32
        )

    def wide_first(values):
        return lax.dot_general(
            values, choose_wide, (((0,), (1,)), ((), ())), precision=lax.Precision.HIGHEST, preferred_element_type=jnp.float32
        )

    mlp_rows = sum_rows(by_group(row_sums))
    gate_first_gradient, up_first_gradient = (wide_first(slots(mlp_rows, 3, i)) for i in range(2))
    down_second_gradient = wide_second(slots(mlp_rows, 3, 2))
    mlp_cols = lax.all_gather(sum_cols(by_group(col_sums), "row"), "dp", axis=1, tiled=True)
    gate_second_gradient, up_second_gradient = (wide_second(slots(mlp_cols, 3, i)) for i in range(2))
    down_first_gradient = wide_first(slots(mlp_cols, 3, 2))

    mixed_tokens = low(attended + mixed_part)
    attended_grad = upstream.astype(jnp.float32) + norm_back(attended, gains[1:2], inverse_mlp, grad_part)

    out_grad = low(attended_grad)
    row_width = features // rows
    lowered_out = masked(
        sum(dot_turned(out_grad[:, r * row_width : (r + 1) * row_width], out_second[r]) for r in range(rows))
    )
    heads_grad = low(
        sum(dot_turned(out_grad[:, r * row_width : (r + 1) * row_width], out_weight[r]) for r in range(rows))
        + dot_turned(lowered_out, out_first)
    )
    unit_grad = exchange(to_units(heads_grad, units // seqs)).reshape(length, -1)
    unit_grad = jnp.pad(unit_grad, ((0, 0), (0, pad_width)))
    query_grad, kv_grad = attend_back(
        unit_queries, unit_grad, unit_out, log_sums, keys_twice, values_twice, unit_keys.T, ends, heads, factor
    )
    moved = exchange(jnp.concatenate([query_grad[:, :unit_width], kv_grad], axis=1))
    moved = moved.reshape(seqs, units // seqs, part, -1)
    query_moved = from_units(moved[..., :unit_width]).astype(jnp.float32)
    kv_moved = moved[..., unit_width:].astype(jnp.float32).reshape(seqs, kv_heads, kv_copies, part, -1).sum(axis=2)
    key_moved = from_units(kv_moved[..., :HEAD_DIM])
    value_moved = from_units(kv_moved[..., HEAD_DIM:])
    query_back = low(rope_back(query_moved, cosine, sine))
    key_back = low(rope_back(key_moved, cosine, sine))
    value_back = low(value_moved)
    qkv_grad = [
        jnp.concatenate(
            [
                query_back[:, c * width_q : (c + 1) * width_q],
                key_back[:, c * width_kv : (c + 1) * width_kv],
                value_back[:, c * width_kv : (c + 1) * width_kv],
            ],
            axis=1,
        )
        for c in range(cols)
    ]
    lowered_qkv = masked(sum(dot_turned(qkv_grad[c], qkv_second[c]) for c in range(cols)))
    normed_grad = sum(dot_turned(qkv_grad[c], qkv_weight[c]) for c in range(cols)) + dot_turned(lowered_qkv, qkv_first)
    token_grad = low(attended_grad + norm_back(residual, gains[0:1], inverse_attn, normed_grad))

    attn_rows = sum_rows(own_group(jnp.concatenate([over_tokens(lowered_qkv, normed), over_tokens(low_out, out_grad)], axis=0)))
    query_first_gradient, key_first_gradient, value_first_gradient = (
        wide_first(slots(attn_rows, 4, i)) for i in range(3)
    )
    output_second_gradient = wide_second(slots(attn_rows, 4, 3))
    qkv_sums = [over_tokens(low_qkv, qkv_grad[c]) for c in range(cols)]
    out_sums = over_tokens(lowered_out, heads_out).reshape(rank, cols, -1)
    attn_cols = sum_cols(
        own_group(
            jnp.concatenate(
                [
                    jnp.concatenate(
                        [
                            qkv_sums[c][:rank, :width_q],
                            out_sums[:, c],
                            qkv_sums[c][rank : 2 * rank, width_q : width_q + width_kv],
                            qkv_sums[c][2 * rank :, width_q + width_kv :],
                        ],
                        axis=1,
                    )
                    for c in range(cols)
                ],
                axis=1,
            )
        ),
        ("row", "dp"),
    )
    query_second_gradient = wide_second(attn_cols[:, :width_q])
    output_first_gradient = wide_first(attn_cols[:, width_q : 2 * width_q])
    key_second_gradient = wide_second(attn_cols[:, 2 * width_q : 2 * width_q + width_kv])
    value_second_gradient = wide_second(attn_cols[:, 2 * width_q + width_kv :])

    return (
        to_features(mixed_tokens, seqs),
        to_features(token_grad, seqs),
        query_first_gradient,
        query_second_gradient,
        key_first_gradient,
        key_second_gradient,
        value_first_gradient,
        value_second_gradient,
        output_first_gradient,
        output_second_gradient,
        gate_first_gradient,
        gate_second_gradient,
        up_first_gradient,
        up_second_gradient,
        down_first_gradient,
        down_second_gradient,
    )


def solution(mesh):
    in_specs = (
        P("col", "dp", "row"),
        P("col", "dp", "row"),
        P("dp", None),
        P("dp"),
        P(),
        P("row"),
        P("row"),
        P("row", "col"),
        P("row", "col"),
        P("row", "col"),
        P("col", "row"),
        P("row", "col"),
        P("row", "col"),
        P("col", "row"),
        P("row", None),
        P(None, "col"),
        P("row", None),
        P(None, "col"),
        P("row", None),
        P(None, "col"),
        P("col", None),
        P(None, "row"),
        P("row", None),
        P(None, "col"),
        P("row", None),
        P(None, "col"),
        P("col", None),
        P(None, "row"),
    )
    out_specs = (
        P("col", "dp", "row"),
        P("col", "dp", "row"),
        P("row", None),
        P(None, "col"),
        P("row", None),
        P(None, "col"),
        P("row", None),
        P(None, "col"),
        P("col", None),
        P(None, "row"),
        P("row", None),
        P(None, "col"),
        P("row", None),
        P(None, "col"),
        P("col", None),
        P(None, "row"),
    )
    return jax.shard_map(local, mesh=mesh, in_specs=in_specs, out_specs=out_specs, check_vma=False)
```

```python
import functools, math
import jax, jax.numpy as jnp
from jax import lax
from jax.sharding import PartitionSpec as P
from jax.experimental import pallas as pl
from jax.experimental.pallas import tpu as pltpu

HEAD_DIM = 64
RANK = 16
BLOCKS = 32
EPS = 1e-05
ROPE_BASE = 500000.0
TILE = 512
REACH = 256
LOG2E = math.log2(math.e)
NEG = -1e30


def nt(a, b):
    return lax.dot_general(a, b, (((1,), (1,)), ((), ())), preferred_element_type=jnp.float32)


def nn(a, b):
    return lax.dot_general(a, b, (((1,), (0,)), ((), ())), preferred_element_type=jnp.float32)


def half_of(x, e):
    lane = lax.broadcasted_iota(jnp.int32, x.shape, 1)
    return jnp.where((lane < 64) if e == 0 else (lane >= 64), x, jnp.zeros_like(x))


def fwd_kernel(heads, factor, end_ref, q_ref, k2_ref, vt_ref, o_ref, lse_ref, acc_ref, m_ref, l_ref):
    i = pl.program_id(0)
    tq = q_ref.shape[0]
    q0 = i * tq
    c = factor * LOG2E
    ends = end_ref[...]
    m_ref[...] = jnp.full_like(m_ref, NEG)
    l_ref[...] = jnp.zeros_like(l_ref)
    acc_ref[...] = jnp.zeros_like(acc_ref)

    def tile(k0, size, masked):
        kk = k2_ref[pl.ds(k0, size), :]
        vv = vt_ref[:, pl.ds(k0, size)]
        if masked:
            allowed = (lax.broadcasted_iota(jnp.int32, (size, tq), 0) + k0) < ends
        for h in range(heads):
            qh = half_of(q_ref[:, (h // 2) * 128:(h // 2 + 1) * 128], h % 2)
            s = nt(kk, qh) * c
            if masked:
                s = jnp.where(allowed, s, NEG)
            m_old = m_ref[h:h + 1, :]
            m_new = jnp.maximum(m_old, jnp.max(s, axis=0, keepdims=True))
            p = jnp.exp2(s - m_new)
            alpha = jnp.exp2(m_old - m_new)
            l_ref[h:h + 1, :] = l_ref[h:h + 1, :] * alpha + jnp.sum(p, axis=0, keepdims=True)
            m_ref[h:h + 1, :] = m_new
            a = pl.ds(h * 64, 64)
            acc_ref[a, :] = acc_ref[a, :] * alpha + nn(vv, p.astype(jnp.bfloat16))

    def body(j, _):
        tile(pl.multiple_of(j * tq, tq), tq, False)
        return 0

    lax.fori_loop(0, i, body, 0)
    tile(pl.multiple_of(q0, tq), tq, True)

    @pl.when(i < pl.num_programs(0) - 1)
    def _():
        tile(pl.multiple_of(q0 + tq, REACH), REACH, True)

    lse_ref[...] = m_ref[...] + jnp.log2(l_ref[...])
    inv = 1.0 / l_ref[...]
    for p in range(o_ref.shape[1] // 128):
        parts = []
        for h in (2 * p, 2 * p + 1):
            if h < heads:
                parts.append(acc_ref[h * 64:(h + 1) * 64, :] * inv[h:h + 1, :])
            else:
                parts.append(jnp.zeros((64, tq), jnp.float32))
        o_ref[:, p * 128:(p + 1) * 128] = jnp.concatenate(parts, axis=0).T.astype(o_ref.dtype)


def attend(q, k2, vt, ends, heads, factor):
    length, width = q.shape
    tq = min(TILE, length)
    rows = 8
    return pl.pallas_call(
        functools.partial(fwd_kernel, heads, factor),
        grid=(length // tq,),
        in_specs=[
            pl.BlockSpec((1, tq), lambda i: (0, i)),
            pl.BlockSpec((tq, width), lambda i: (i, 0)),
            pl.BlockSpec((length, 128), lambda i: (0, 0)),
            pl.BlockSpec((64, length), lambda i: (0, 0)),
        ],
        out_specs=[
            pl.BlockSpec((tq, width), lambda i: (i, 0)),
            pl.BlockSpec((rows, tq), lambda i: (0, i)),
        ],
        out_shape=[
            jax.ShapeDtypeStruct((length, width), jnp.bfloat16),
            jax.ShapeDtypeStruct((rows, length), jnp.float32),
        ],
        scratch_shapes=[
            pltpu.VMEM((heads * 64, tq), jnp.float32),
            pltpu.VMEM((rows, tq), jnp.float32),
            pltpu.VMEM((rows, tq), jnp.float32),
        ],
        compiler_params=pltpu.CompilerParams(vmem_limit_bytes=48 * 2**20),
        cost_estimate=pl.CostEstimate(
            flops=2 * heads * length * length * 64, bytes_accessed=4 * length * width + length * 384, transcendentals=heads * length * length // 2
        ),
        name="attend_forward",
    )(ends, q, k2, vt)


def turn_back(values, cosine, sine):
    high, rest = values[:32, :], values[32:, :]
    return jnp.concatenate([high * cosine + rest * sine, rest * cosine - high * sine], axis=0)


def bwd_kernel(heads, factor, end_ref, cos_ref, sin_ref, q_ref, do_ref, o_ref, lse_ref, k2_ref, v2_ref, kt_ref, dq_ref, dkv_ref, dqt_ref, delta_ref, dk_ref, dv_ref):
    j = pl.program_id(0)
    n = pl.num_programs(0)
    tk = k2_ref.shape[0]
    length, width = q_ref.shape
    c = factor * LOG2E

    @pl.when(j == 0)
    def _():
        dqt_ref[...] = jnp.zeros_like(dqt_ref)
        delta_ref[...] = jnp.zeros_like(delta_ref)
        for t in range(length // tk):
            rows = slice(t * tk, (t + 1) * tk)
            for p in range(width // 128):
                prod = do_ref[rows, p * 128:(p + 1) * 128].astype(jnp.float32) * o_ref[rows, p * 128:(p + 1) * 128].astype(jnp.float32)
                turned = prod.T
                for h in (2 * p, 2 * p + 1):
                    if h < heads:
                        delta_ref[h:h + 1, rows] = jnp.sum(turned[(h % 2) * 64:(h % 2 + 1) * 64, :], axis=0, keepdims=True)

    dk_ref[...] = jnp.zeros_like(dk_ref)
    dv_ref[...] = jnp.zeros_like(dv_ref)

    def tile(q0, size, masked):
        rows = pl.ds(q0, tk)
        kk = k2_ref[:size, :]
        vv = v2_ref[:size, :]
        kt = kt_ref[:, :size]
        if masked:
            allowed = (lax.broadcasted_iota(jnp.int32, (size, tk), 0) + j * tk) < end_ref[:, rows]
        for h in range(heads):
            lanes = slice((h // 2) * 128, (h // 2 + 1) * 128)
            qh = half_of(q_ref[rows, lanes], h % 2)
            gh = half_of(do_ref[rows, lanes], h % 2)
            s = nt(kk, qh) * c - lse_ref[h:h + 1, rows]
            if masked:
                s = jnp.where(allowed, s, NEG)
            p = jnp.exp2(s)
            dp = nt(vv, gh)
            ds = (p * (dp - delta_ref[h:h + 1, rows])).astype(jnp.bfloat16)
            dv_ref[:size, :] += nn(p.astype(jnp.bfloat16), gh)
            dk_ref[:size, :] += nn(ds, qh)
            dqt_ref[h * 64:(h + 1) * 64, rows] += nn(kt, ds)

    @pl.when(j > 0)
    def _():
        tile(pl.multiple_of((j - 1) * tk, tk), REACH, True)

    tile(pl.multiple_of(j * tk, tk), tk, True)

    def body(i, _):
        tile(pl.multiple_of(i * tk, tk), tk, False)
        return 0

    lax.fori_loop(j + 1, n, body, 0)

    own = pl.ds(pl.multiple_of(j * tk, tk), tk)
    dk = dk_ref[...].T
    dv = dv_ref[...].T
    dk = turn_back(dk[:64] + dk[64:], cos_ref[:, own], sin_ref[:, own]) * factor
    dkv_ref[...] = jnp.concatenate([dk, dv[:64] + dv[64:]], axis=0).T.astype(dkv_ref.dtype)

    @pl.when(j == n - 1)
    def _():
        for t in range(length // tk):
            rows = slice(t * tk, (t + 1) * tk)
            for p in range(width // 128):
                parts = []
                for h in (2 * p, 2 * p + 1):
                    if h < heads:
                        parts.append(turn_back(dqt_ref[h * 64:(h + 1) * 64, rows], cos_ref[:, rows], sin_ref[:, rows]) * factor)
                    else:
                        parts.append(jnp.zeros((64, tk), jnp.float32))
                dq_ref[rows, p * 128:(p + 1) * 128] = jnp.concatenate(parts, axis=0).T.astype(dq_ref.dtype)


def attend_back(q, do, o, lse, k2, v2, kt, ends, cosine, sine, heads, factor):
    length, width = q.shape
    tk = min(TILE, length)
    whole = lambda shape: pl.BlockSpec(shape, lambda j: (0, 0))
    return pl.pallas_call(
        functools.partial(bwd_kernel, heads, factor),
        grid=(length // tk,),
        in_specs=[
            whole((1, length)),
            whole((32, length)),
            whole((32, length)),
            whole((length, width)),
            whole((length, width)),
            whole((length, width)),
            whole((8, length)),
            pl.BlockSpec((tk, 128), lambda j: (j, 0)),
            pl.BlockSpec((tk, 128), lambda j: (j, 0)),
            pl.BlockSpec((64, tk), lambda j: (0, j)),
        ],
        out_specs=[
            whole((length, width)),
            pl.BlockSpec((tk, 128), lambda j: (j, 0)),
        ],
        out_shape=[
            jax.ShapeDtypeStruct((length, width), jnp.bfloat16),
            jax.ShapeDtypeStruct((length, 128), jnp.float32),
        ],
        scratch_shapes=[
            pltpu.VMEM((heads * 64, length), jnp.float32),
            pltpu.VMEM((8, length), jnp.float32),
            pltpu.VMEM((tk, 128), jnp.float32),
            pltpu.VMEM((tk, 128), jnp.float32),
        ],
        compiler_params=pltpu.CompilerParams(vmem_limit_bytes=48 * 2**20),
        cost_estimate=pl.CostEstimate(
            flops=5 * heads * length * length * 64, bytes_accessed=8 * length * width + length * 512, transcendentals=heads * length * length // 2
        ),
        name="attend_backward",
    )(ends, cosine, sine, q, do, o, lse, k2, v2, kt)


def buffered_once(shape, index_map):
    return pl.BlockSpec(shape, index_map, pipeline_mode=pl.Buffered(1))


def normalized(values, gain):
    inverse = lax.rsqrt(jnp.mean(values * values, axis=-1, keepdims=True) + EPS)
    return inverse, (values * inverse * gain).astype(jnp.bfloat16)


def norm_back(values, inverse, gain, upstream):
    scaled = upstream * gain
    weighted = jnp.mean(scaled * values, axis=-1, keepdims=True)
    return inverse * scaled - values * (inverse * inverse * inverse * weighted)


def qkv_kernel(pairs, kv_heads, token_ref, gain_ref, mask_ref, first_ref, second_ref, cos_ref, sin_ref, *refs):
    weight_refs, refs = refs[:3], refs[3:]
    message_refs, low_ref, normed_ref = refs[:pairs], refs[pairs], refs[pairs + 1]
    rows, lanes, chunk = weight_refs[0].shape[1:]
    count = token_ref.shape[0]
    seqs, _, units, part, _ = message_refs[0].shape
    pair_width = message_refs[0].shape[4] - 2 * HEAD_DIM

    @pl.when(pl.program_id(0) == 0)
    def _():
        _, normed = normalized(token_ref[...].astype(jnp.float32), gain_ref[...])
        normed_ref[...] = normed
        low_ref[...] = (nt(normed, first_ref[...]) * mask_ref[...]).astype(jnp.bfloat16)

    raw = jnp.concatenate(
        [nn(normed_ref[...], w[0].reshape(rows * lanes, chunk)) for w in weight_refs], axis=1
    ) + nn(low_ref[...], second_ref[0])
    width = raw.shape[1]
    lane = lax.broadcasted_iota(jnp.int32, raw.shape, 1)
    turned = jnp.where(lane % HEAD_DIM < HEAD_DIM // 2, -pltpu.roll(raw, width - HEAD_DIM // 2, 1), pltpu.roll(raw, HEAD_DIM // 2, 1))
    out = (raw * cos_ref[...] + turned * sin_ref[...]).astype(jnp.bfloat16)
    head_width = width // kv_heads
    for s in range(seqs):
        at = slice(s * part, (s + 1) * part)
        for u in range(units):
            base = u * kv_heads // units * head_width
            inside = u % (units // kv_heads) * pairs * pair_width
            kv = out[at, base + head_width - 2 * HEAD_DIM : base + head_width]
            for p in range(pairs):
                begin = base + inside + p * pair_width
                queries = out[at, begin : begin + pair_width]
                message_refs[p][s, 0, u] = jnp.concatenate([queries, kv], axis=1) if p == 0 else queries


def project_qkv(tokens, gain, mask, first, second, cosine, sine, weight, seqs, units, pairs, pair_width, kv_heads):
    count, features = tokens.shape
    cols, rows, lanes, _ = weight.shape
    width = second.shape[2]
    chunk = width // 3
    part = count // seqs
    ahead = lanes // chunk
    whole = lambda shape: pl.BlockSpec(shape, lambda c: (0,) * len(shape))
    message = lambda wide: (seqs, cols, units // (seqs * cols), part, wide)
    widths = [pair_width + 2 * HEAD_DIM] + [pair_width] * (pairs - 1)
    block = lambda wide: pl.BlockSpec((seqs, 1) + message(wide)[2:], lambda c: (0, c, 0, 0, 0))
    weights = lambda at: pl.BlockSpec((1, rows, lanes, chunk), lambda c: (c, 0, 0, ahead + at))
    return pl.pallas_call(
        functools.partial(qkv_kernel, pairs, kv_heads),
        grid=(cols,),
        in_specs=[
            whole((count, features)),
            whole((1, features)),
            whole(mask.shape),
            whole(first.shape),
            pl.BlockSpec((1,) + second.shape[1:], lambda c: (c, 0, 0)),
            whole((count, width)),
            whole((count, width)),
            weights(0),
            weights(1),
            weights(2),
        ],
        out_specs=[block(w) for w in widths] + [whole(mask.shape)],
        out_shape=[jax.ShapeDtypeStruct(message(w), jnp.bfloat16) for w in widths]
        + [jax.ShapeDtypeStruct(mask.shape, jnp.bfloat16)],
        scratch_shapes=[pltpu.VMEM((count, features), jnp.bfloat16)],
        compiler_params=pltpu.CompilerParams(vmem_limit_bytes=48 * 2**20),
        cost_estimate=pl.CostEstimate(
            flops=2 * count * features * cols * width,
            bytes_accessed=2 * features * cols * width + 4 * count * features,
            transcendentals=count,
        ),
        name="project_qkv",
    )(tokens, gain, mask, first, second, cosine, sine, weight, weight, weight)


def qkv_back_kernel(
    pairs, token_ref, attended_ref, gain_ref, mask_ref, first_ref, second_ref, low_ref, kv_ref, *refs
):
    query_refs, refs = refs[:pairs], refs[pairs:]
    weight_refs, refs = refs[:3], refs[3:]
    out_ref, rows_ref, cols_ref, grad_ref, lowered_ref, low_turned_ref = refs
    c = pl.program_id(0)
    rows, lanes, chunk = weight_refs[0].shape[1:]
    seqs, _, kv_heads, part, _ = kv_ref.shape
    units = query_refs[0].shape[2]
    rank = mask_ref.shape[1] // 3

    @pl.when(c == 0)
    def _():
        grad_ref[...] = jnp.zeros_like(grad_ref)
        lowered_ref[...] = jnp.zeros_like(lowered_ref)
        low_turned_ref[...] = low_ref[...].astype(jnp.float32).T.astype(jnp.bfloat16)

    parts = []
    for j in range(kv_heads):
        for u in range(j * units // kv_heads, (j + 1) * units // kv_heads):
            parts += [jnp.concatenate([q[s, 0, u] for s in range(seqs)], axis=0) for q in query_refs]
        parts.append(jnp.concatenate([kv_ref[s, 0, j] for s in range(seqs)], axis=0))
    e = jnp.concatenate(parts, axis=1)
    for r in range(rows):
        total = nt(e[:, :chunk], weight_refs[0][0, r])
        for i in (1, 2):
            total += nt(e[:, i * chunk : (i + 1) * chunk], weight_refs[i][0, r])
        grad_ref[:, r * lanes : (r + 1) * lanes] += total
    lowered_ref[...] += nt(e, second_ref[0])
    sums = nn(low_turned_ref[...], e)
    lane = lax.broadcasted_iota(jnp.int32, (rank, sums.shape[1]), 1) % (sums.shape[1] // kv_heads)
    query_lanes = sums.shape[1] // kv_heads - 2 * HEAD_DIM
    cols_ref[0] = jnp.where(
        lane < query_lanes,
        sums[:rank],
        jnp.where(lane < query_lanes + HEAD_DIM, sums[rank : 2 * rank], sums[2 * rank :]),
    ).astype(cols_ref.dtype)

    @pl.when(c == pl.num_programs(0) - 1)
    def _():
        lowered = lowered_ref[...] * mask_ref[...]
        grad = grad_ref[...] + nn(lowered.astype(jnp.bfloat16), first_ref[...])
        values = token_ref[...].astype(jnp.float32)
        inverse, normed = normalized(values, gain_ref[...])
        turned = nn(lowered.T.astype(jnp.bfloat16), normed)
        out = (attended_ref[...] + norm_back(values, inverse, gain_ref[...], grad)).astype(jnp.bfloat16)
        for r in range(rows):
            at = slice(r * lanes, (r + 1) * lanes)
            out_ref[r] = out[:, at]
            rows_ref[r] = turned[:, at].astype(rows_ref.dtype)


def project_qkv_back(tokens, attended_grad, gain, mask, first, second, low_qkv, kv, queries, weight):
    count, features = tokens.shape
    cols, rows, lanes, _ = weight.shape
    width = second.shape[2]
    chunk = width // 3
    ahead = lanes // chunk
    rank = mask.shape[1] // 3
    pairs = len(queries)
    whole = lambda shape: buffered_once(shape, lambda c: (0,) * len(shape))
    by_unit = lambda v: pl.BlockSpec((v.shape[0], 1) + v.shape[2:], lambda c: (0, c, 0, 0, 0))
    weights = lambda at: pl.BlockSpec((1, rows, lanes, chunk), lambda c: (c, 0, 0, ahead + at))
    return pl.pallas_call(
        functools.partial(qkv_back_kernel, pairs),
        grid=(cols,),
        in_specs=[
            whole((count, features)),
            whole((count, features)),
            whole((1, features)),
            whole(mask.shape),
            whole(first.shape),
            pl.BlockSpec((1,) + second.shape[1:], lambda c: (c, 0, 0)),
            whole(low_qkv.shape),
            by_unit(kv),
        ]
        + [by_unit(q) for q in queries]
        + [weights(0), weights(1), weights(2)],
        out_specs=[
            pl.BlockSpec((rows, count, lanes), lambda c: (0, 0, 0)),
            pl.BlockSpec((rows, 3 * rank, lanes), lambda c: (0, 0, 0)),
            pl.BlockSpec((1, rank, width), lambda c: (c, 0, 0)),
        ],
        out_shape=[
            jax.ShapeDtypeStruct((rows, count, lanes), jnp.bfloat16),
            jax.ShapeDtypeStruct((rows, 3 * rank, lanes), jnp.bfloat16),
            jax.ShapeDtypeStruct((cols, rank, width), jnp.bfloat16),
        ],
        scratch_shapes=[
            pltpu.VMEM((count, features), jnp.float32),
            pltpu.VMEM((count, 3 * rank), jnp.float32),
            pltpu.VMEM((3 * rank, count), jnp.bfloat16),
        ],
        compiler_params=pltpu.CompilerParams(vmem_limit_bytes=60 * 2**20),
        cost_estimate=pl.CostEstimate(
            flops=2 * count * features * cols * width,
            bytes_accessed=2 * features * cols * width + 10 * count * features,
            transcendentals=count,
        ),
        name="project_qkv_back",
    )(tokens, attended_grad, gain, mask, first, second, low_qkv, kv, *queries, weight, weight, weight)


def mlp_kernel(goes_on, group_ref, h_ref, e_ref, mask_ref, first_ref, second_ref, gate_ref, up_ref, down_ref, mids_ref, *refs):
    if goes_on:
        rows_in_ref, _, grad_in_ref, mixed_in_ref = refs[:4]
        refs = refs[4:]
    else:
        refs = refs[2:]
    rows_ref, cols_ref, grad_out_ref, mixed_out_ref = refs[:4]
    low_ref, low_turned_ref, lowered_ref, lowered_turned_ref, sum_front_ref, sum_down_ref = refs[4:10]
    grad_ref, mixed_ref = refs[10:] if len(refs) > 10 else (grad_out_ref, mixed_out_ref)
    c = pl.program_id(0)
    rows, lanes = gate_ref.shape[1], gate_ref.shape[3]
    rank = second_ref.shape[0]

    @pl.when(c == 0)
    def _():
        low_now = nt(h_ref[...], first_ref[...]) * mask_ref[...]
        low_ref[...] = low_now.astype(jnp.bfloat16)
        low_turned_ref[...] = low_now.T.astype(jnp.bfloat16)
        lowered_now = nt(e_ref[...], second_ref[...]) * mask_ref[:, :rank]
        lowered_ref[...] = lowered_now.astype(jnp.bfloat16)
        lowered_turned_ref[...] = lowered_now.T.astype(jnp.bfloat16)
        sum_front_ref[...] = jnp.zeros_like(sum_front_ref)
        sum_down_ref[...] = jnp.zeros_like(sum_down_ref)
        if goes_on:
            grad_ref[...] = grad_in_ref[...]
            mixed_ref[...] = mixed_in_ref[...]
        else:
            grad_ref[...] = jnp.zeros_like(grad_ref)
            mixed_ref[...] = jnp.zeros_like(mixed_ref)

    h = h_ref[...]
    gate_second, up_second, down_first = mids_ref[0, 0, 0], mids_ref[0, 0, 1], mids_ref[0, 0, 2, :rank]
    gate = nn(h, gate_ref[0].reshape(rows * lanes, lanes)) + nn(low_ref[...], gate_second)
    up = nn(h, up_ref[0].reshape(rows * lanes, lanes)) + nn(low_ref[...], up_second)
    upstream = nn(lowered_ref[...], down_first)
    for r in range(rows):
        upstream += nt(e_ref[:, r * lanes : (r + 1) * lanes], down_ref[0, r])
    sigmoid = 1.0 / (1.0 + jnp.exp(-gate))
    swish = gate * sigmoid
    hidden = (swish * up).astype(jnp.bfloat16)
    gate_grad = (upstream * up * (sigmoid + swish * (1.0 - sigmoid))).astype(jnp.bfloat16)
    up_grad = (upstream * swish).astype(jnp.bfloat16)
    for r in range(rows):
        at = slice(r * lanes, (r + 1) * lanes)
        grad_ref[:, at] += nt(gate_grad, gate_ref[0, r]) + nt(up_grad, up_ref[0, r])
        mixed_ref[:, at] += nn(hidden, down_ref[0, r])
    sum_front_ref[...] += nt(gate_grad, gate_second) + nt(up_grad, up_second)
    sum_down_ref[...] += nt(hidden, down_first)
    cols_ref[0, :rank] = nn(low_turned_ref[:rank], gate_grad)
    cols_ref[0, rank : 2 * rank] = nn(low_turned_ref[rank:], up_grad)
    cols_ref[0, 2 * rank :] = nn(lowered_turned_ref[...], hidden)

    @pl.when(c == pl.num_programs(0) - 1)
    def _():
        front_now = sum_front_ref[...] * mask_ref[...]
        grad_out_ref[...] = (grad_ref[...] + nn(front_now.astype(jnp.bfloat16), first_ref[...])).astype(grad_out_ref.dtype)
        down_now = sum_down_ref[...] * mask_ref[:, :rank]
        mixed_out_ref[...] = (mixed_ref[...] + nn(down_now.astype(jnp.bfloat16), second_ref[...])).astype(mixed_out_ref.dtype)
        front_sum = nn(front_now.T.astype(jnp.bfloat16), h_ref[...])
        down_sum = nn(down_now.T.astype(jnp.bfloat16), e_ref[...])
        for r in range(rows):
            at = slice(r * lanes, (r + 1) * lanes)
            now = jnp.concatenate([front_sum[:, at], down_sum[:, at]], axis=0)
            rows_ref[r] = now + rows_in_ref[r] if goes_on else now


def feed_forward(group, block, h, e, mask, first, second, weight, mids, row_sums, col_sums, earlier, dtype):
    count, features = h.shape
    cols, rows, _, lanes = weight.shape
    rank = mids.shape[3] // 2
    groups = mids.shape[1]
    blocks = col_sums.shape[1] // (groups * 3 * rank)
    goes_on = earlier is not None
    whole = lambda shape: buffered_once(shape, lambda c, g: (0,) * len(shape))
    weights = lambda at: pl.BlockSpec((1, rows, lanes, lanes), lambda c, g: (c, 0, at, 0))
    row_spec = pl.BlockSpec((rows, 3 * rank, lanes), lambda c, g: (0, g[0], 0))
    anywhere = pl.BlockSpec(memory_space=pl.ANY)
    scratch = [
        pltpu.VMEM((count, 2 * rank), jnp.bfloat16),
        pltpu.VMEM((2 * rank, count), jnp.bfloat16),
        pltpu.VMEM((count, rank), jnp.bfloat16),
        pltpu.VMEM((rank, count), jnp.bfloat16),
        pltpu.VMEM((count, 2 * rank), jnp.float32),
        pltpu.VMEM((count, rank), jnp.float32),
    ]
    if dtype != jnp.float32:
        scratch += [pltpu.VMEM((count, features), jnp.float32)] * 2
    return pl.pallas_call(
        functools.partial(mlp_kernel, goes_on),
        grid_spec=pltpu.PrefetchScalarGridSpec(
            num_scalar_prefetch=1,
            grid=(cols,),
            in_specs=[
                whole((count, features)),
                whole((count, features)),
                whole((count, 2 * rank)),
                pl.BlockSpec((2 * rank, features), lambda c, g: (g[0], 0)),
                pl.BlockSpec((rank, features), lambda c, g: (g[0], 0)),
                weights(0),
                weights(1),
                weights(2),
                pl.BlockSpec((1, 1, 3, 2 * rank, lanes), lambda c, g: (c, g[0], 0, 0, 0)),
                row_spec if goes_on else anywhere,
                anywhere,
            ]
            + ([whole((count, features))] * 2 if goes_on else []),
            out_specs=[
                row_spec,
                pl.BlockSpec((1, 3 * rank, lanes), lambda c, g: (c, g[0] * blocks + block, 0)),
                pl.BlockSpec((count, features), lambda c, g: (0, 0)),
                pl.BlockSpec((count, features), lambda c, g: (0, 0)),
            ],
            scratch_shapes=scratch,
        ),
        out_shape=[
            jax.ShapeDtypeStruct(row_sums.shape, jnp.float32),
            jax.ShapeDtypeStruct(col_sums.shape, jnp.float32),
            jax.ShapeDtypeStruct((count, features), dtype),
            jax.ShapeDtypeStruct((count, features), dtype),
        ],
        input_output_aliases={10: 0, 11: 1},
        compiler_params=pltpu.CompilerParams(vmem_limit_bytes=60 * 2**20),
        cost_estimate=pl.CostEstimate(
            flops=12 * count * features * cols * lanes,
            bytes_accessed=6 * features * cols * lanes + 12 * count * features,
            transcendentals=count * cols * lanes,
        ),
        name="feed_forward",
    )(group, h, e, mask, first, second, weight, weight, weight, mids, row_sums, col_sums, *(earlier or ()))


def out_kernel(heads_ref, residual_ref, gain_ref, mask_ref, first_ref, second_ref, weight_ref, attended_ref, normed_ref, low_ref):
    r = pl.program_id(0)
    cols, lanes = weight_ref.shape[0], weight_ref.shape[3]

    @pl.when(r == 0)
    def _():
        low_ref[...] = (nt(heads_ref[...], first_ref[...]) * mask_ref[...]).astype(jnp.bfloat16)

    at = pl.ds(pl.multiple_of(r * lanes, lanes), lanes)
    attended_ref[:, at] = (
        residual_ref[...].astype(jnp.float32)
        + nn(heads_ref[...], weight_ref[:, 0].reshape(cols * lanes, lanes))
        + nn(low_ref[...], second_ref[0])
    )

    @pl.when(r == pl.num_programs(0) - 1)
    def _():
        normed_ref[...] = normalized(attended_ref[...], gain_ref[...])[1]


def project_out(heads, residual, gain, mask, first, second, weight):
    count, features = residual.shape
    cols, rows, lanes, _ = weight.shape
    rank = mask.shape[1]
    whole = lambda shape: pl.BlockSpec(shape, lambda r: (0,) * len(shape))
    return pl.pallas_call(
        out_kernel,
        grid=(rows,),
        in_specs=[
            whole(heads.shape),
            pl.BlockSpec((count, lanes), lambda r: (0, r)),
            whole((1, features)),
            whole((count, rank)),
            whole(first.shape),
            pl.BlockSpec((1, rank, lanes), lambda r: (r, 0, 0)),
            pl.BlockSpec((cols, 1, lanes, lanes), lambda r: (0, r, 0, 0)),
        ],
        out_specs=[whole((count, features)), whole((count, features)), whole((count, rank))],
        out_shape=[
            jax.ShapeDtypeStruct((count, features), jnp.float32),
            jax.ShapeDtypeStruct((count, features), jnp.bfloat16),
            jax.ShapeDtypeStruct((count, rank), jnp.bfloat16),
        ],
        compiler_params=pltpu.CompilerParams(vmem_limit_bytes=48 * 2**20),
        cost_estimate=pl.CostEstimate(
            flops=2 * count * features * heads.shape[1],
            bytes_accessed=2 * features * heads.shape[1] + 10 * count * features,
            transcendentals=count,
        ),
        name="project_out",
    )(heads, residual, gain, mask, first, second, weight)


def out_back_kernel(
    pairs, pair_width, own_ref, other_ref, upstream_ref, attended_ref, gain_ref, mask_ref, first_ref, second_ref, heads_ref, low_ref, weight_ref,
    attended_grad_ref, rows_ref, cols_ref, *refs,
):
    message_refs = refs[:pairs]
    e_ref, lowered_ref, lowered_turned_ref = refs[pairs:]
    c = pl.program_id(0)
    rows, lanes = weight_ref.shape[1], weight_ref.shape[3]
    seqs, _, units, part, _ = message_refs[0].shape

    @pl.when(c == 0)
    def _():
        values = attended_ref[...]
        inverse = lax.rsqrt(jnp.mean(values * values, axis=-1, keepdims=True) + EPS)
        upstream = own_ref[...] + other_ref[...].astype(jnp.float32)
        total = upstream_ref[...].astype(jnp.float32) + norm_back(values, inverse, gain_ref[...], upstream)
        attended_grad_ref[...] = total
        e = total.astype(jnp.bfloat16)
        e_ref[...] = e
        lowered = nt(e, second_ref[...]) * mask_ref[...]
        lowered_ref[...] = lowered.astype(jnp.bfloat16)
        lowered_turned_ref[...] = lowered.T.astype(jnp.bfloat16)
        turned = nn(low_ref[...].astype(jnp.float32).T.astype(jnp.bfloat16), e)
        for r in range(rows):
            rows_ref[r] = turned[:, r * lanes : (r + 1) * lanes].astype(rows_ref.dtype)

    grad = nn(lowered_ref[...], first_ref[...])
    for r in range(rows):
        grad += nt(e_ref[:, r * lanes : (r + 1) * lanes], weight_ref[0, r])
    grad = grad.astype(jnp.bfloat16)
    for s in range(seqs):
        for u in range(units):
            for p in range(pairs):
                begin = (u * pairs + p) * pair_width
                message_refs[p][s, 0, u] = grad[s * part : (s + 1) * part, begin : begin + pair_width]
    cols_ref[0] = nn(lowered_turned_ref[...], heads_ref[...]).astype(cols_ref.dtype)


def project_out_back(own, other, upstream, attended, gain, mask, first, second, heads, low_out, weight, seqs, units, pairs, pair_width):
    count, features = attended.shape
    cols, rows, lanes, _ = weight.shape
    rank = mask.shape[1]
    whole = lambda shape: buffered_once(shape, lambda c: (0,) * len(shape))
    message = (seqs, cols, units // (seqs * cols), count // seqs, pair_width)
    return pl.pallas_call(
        functools.partial(out_back_kernel, pairs, pair_width),
        grid=(cols,),
        in_specs=[whole((count, features))] * 4
        + [
            whole((1, features)),
            whole((count, rank)),
            pl.BlockSpec((rank, lanes), lambda c: (0, c)),
            whole((rank, features)),
            pl.BlockSpec((count, lanes), lambda c: (0, c)),
            whole((count, rank)),
            pl.BlockSpec((1, rows, lanes, lanes), lambda c: (c, 0, 0, 0)),
        ],
        out_specs=[
            pl.BlockSpec((count, features), lambda c: (0, 0)),
            pl.BlockSpec((rows, rank, lanes), lambda c: (0, 0, 0)),
            pl.BlockSpec((1, rank, lanes), lambda c: (c, 0, 0)),
        ]
        + [pl.BlockSpec((seqs, 1) + message[2:], lambda c: (0, c, 0, 0, 0))] * pairs,
        out_shape=[
            jax.ShapeDtypeStruct((count, features), jnp.float32),
            jax.ShapeDtypeStruct((rows, rank, lanes), jnp.bfloat16),
            jax.ShapeDtypeStruct((cols, rank, lanes), jnp.bfloat16),
        ]
        + [jax.ShapeDtypeStruct(message, jnp.bfloat16)] * pairs,
        scratch_shapes=[
            pltpu.VMEM((count, features), jnp.bfloat16),
            pltpu.VMEM((count, rank), jnp.bfloat16),
            pltpu.VMEM((rank, count), jnp.bfloat16),
        ],
        compiler_params=pltpu.CompilerParams(vmem_limit_bytes=60 * 2**20),
        cost_estimate=pl.CostEstimate(
            flops=2 * count * features * cols * lanes,
            bytes_accessed=2 * features * cols * lanes + 18 * count * features,
            transcendentals=count,
        ),
        name="project_out_back",
    )(own, other, upstream, attended, gain, mask, first, second, heads, low_out, weight)


def dot(left, right):
    return lax.dot_general(left, right, (((1,), (0,)), ((), ())), preferred_element_type=jnp.float32)


def over_tokens(left, right):
    return lax.dot_general(left, right, (((0,), (0,)), ((), ())), preferred_element_type=jnp.float32)


def low(values):
    return values.astype(jnp.bfloat16)


def after(values, earlier):
    return lax.optimization_barrier((values, earlier))[0]


def to_tokens(values):
    rows = lax.axis_size("row")
    part, seqs, features = values.shape
    cut = values.reshape(rows, part // rows, seqs, features).transpose(0, 2, 1, 3)
    moved = lax.all_to_all(cut, "row", 0, 0, tiled=True)
    return moved.transpose(1, 2, 0, 3).reshape(seqs * (part // rows), rows * features)


def to_features(blocks, seqs):
    rows, _, width = blocks.shape
    me = lax.axis_index("row")
    parts = []
    for step in range(rows):
        block = lax.dynamic_index_in_dim(blocks, (me + step) % rows, 0, keepdims=False)
        if step:
            block = lax.ppermute(block, "row", [(i, (i + step) % rows) for i in range(rows)])
        parts.append(block)
    stacked = jnp.stack(parts)
    moved = jnp.stack(
        [lax.dynamic_index_in_dim(stacked, (me - source) % rows, 0, keepdims=False) for source in range(rows)]
    ).reshape(rows, seqs, -1, width)
    return moved.transpose(0, 2, 1, 3).reshape(-1, seqs, width)


def rope_tables(positions):
    half = HEAD_DIM // 2
    frequency = ROPE_BASE ** (-(jnp.arange(half).astype(jnp.float32) * 2.0) / HEAD_DIM)
    angles = positions.astype(jnp.float32)[:, None] * frequency[None, :]
    return lax.optimization_barrier((jnp.cos(angles), jnp.sin(angles)))


def diagonal(blocks):
    total = sum(b.shape[1] for b in blocks)
    out, at = [], 0
    for b in blocks:
        out.append(jnp.pad(b, ((0, 0), (at, total - at - b.shape[1]))))
        at += b.shape[1]
    return jnp.concatenate(out, axis=0)


def local(
    tokens,
    cotangent,
    block_labels,
    adapter_selection,
    adapter_scale,
    attention_norm_gain,
    feedforward_norm_gain,
    query_weight,
    key_weight,
    value_weight,
    output_weight,
    gate_weight,
    up_weight,
    down_weight,
    query_first_factor,
    query_second_factor,
    key_first_factor,
    key_second_factor,
    value_first_factor,
    value_second_factor,
    output_first_factor,
    output_second_factor,
    gate_first_factor,
    gate_second_factor,
    up_first_factor,
    up_second_factor,
    down_first_factor,
    down_second_factor,
):
    copies, rows, cols = lax.axis_size("dp"), lax.axis_size("row"), lax.axis_size("col")
    me = lax.axis_index("dp")
    units = rows * cols
    both, turned_both = ("row", "col"), ("col", "row")
    seqs = tokens.shape[1]
    part = tokens.shape[0] // rows
    length = part * units
    lanes = tokens.shape[2]
    scale = adapter_scale[0]
    width_q, width_kv = query_weight.shape[1], key_weight.shape[1]
    width_ff = gate_weight.shape[1] // copies
    blocks_ff = width_ff // lanes
    kv_heads = width_kv // HEAD_DIM
    heads = width_q * cols // HEAD_DIM * seqs // units
    pairs = -(-heads // 2)
    pair_heads = heads // pairs
    pair_width = pair_heads * HEAD_DIM
    pair_pad = -pair_width % 128
    kv_copies = max(1, units // (seqs * kv_heads * cols))
    adapter_cols = query_first_factor.shape[1]
    rank = seqs * RANK
    factor = HEAD_DIM ** (-0.5)
    head_q = width_q // kv_heads

    picked = lax.all_gather(adapter_selection, "dp", axis=0, tiled=True)
    owner = jnp.arange(adapter_cols)
    slot = jnp.arange(copies * rank)
    choose = (owner[:, None] // RANK == picked[slot // RANK][None, :]) & (owner[:, None] % RANK == slot[None, :] % RANK)
    choose_low = choose.astype(jnp.bfloat16)
    choose_wide = choose.astype(jnp.float32)
    choose_own = lax.dynamic_slice_in_dim(choose_low, me * rank, rank, 1)

    def first_of(matrix, chosen):
        return low(lax.dot_general(chosen, matrix, (((0,), (1,)), ((), ())), preferred_element_type=jnp.float32))

    def second_of(matrix, chosen):
        return low(over_tokens(chosen, matrix))

    def pack(by_row, by_col):
        shares = []
        for group, count, at in zip((by_row, by_col), (cols, rows), ("col", "row")):
            if not group:
                shares.append(jnp.zeros((0, lanes), jnp.bfloat16))
                continue
            joined = jnp.concatenate([v.reshape(-1, lanes) for v in group], axis=0)
            joined = jnp.pad(joined, ((0, -joined.shape[0] % count), (0, 0)))
            piece = joined.shape[0] // count
            shares.append(lax.dynamic_slice_in_dim(joined, lax.axis_index(at) * piece, piece, 0))
        return jnp.concatenate(shares, axis=0), shares[0].shape[0]

    def unpack(moved, share, by_row, by_col):
        of_rows = moved[:, :, :share].transpose(1, 0, 2, 3).reshape(rows, -1, lanes)
        of_cols = moved[:, :, share:].reshape(cols, -1, lanes)
        outs = []
        for group, source in zip((by_row, by_col), (of_rows, of_cols)):
            at, out = 0, []
            for v in group:
                size = v.size // lanes
                out.append(source[:, at : at + size].reshape((source.shape[0],) + v.shape))
                at += size
            outs.append(out)
        return outs

    def joined_rows(values):
        return values.transpose(1, 0, 2).reshape(values.shape[1], -1)

    def by_head(query, key, value):
        parts = []
        for j in range(kv_heads):
            at = slice(j * HEAD_DIM, (j + 1) * HEAD_DIM)
            parts += [query[:, j * head_q : (j + 1) * head_q], key[:, at], value[:, at]]
        return jnp.concatenate(parts, axis=1)

    half = me * width_ff
    gate_half = lax.dynamic_slice_in_dim(gate_weight, half, width_ff, 1)
    up_half = lax.dynamic_slice_in_dim(up_weight, half, width_ff, 1)
    down_half = lax.dynamic_slice_in_dim(down_weight, half, width_ff, 0)
    gate_second_half = lax.dynamic_slice_in_dim(gate_second_factor, half, width_ff, 1)
    up_second_half = lax.dynamic_slice_in_dim(up_second_factor, half, width_ff, 1)
    down_first_half = lax.dynamic_slice_in_dim(down_first_factor, half, width_ff, 0)

    attn_weight = lax.all_gather(
        jnp.concatenate([output_weight, by_head(query_weight, key_weight, value_weight)], axis=1),
        turned_both,
        axis=0,
        tiled=True,
    ).reshape(cols, rows, lanes, -1)
    attn_small = (
        [
            jnp.concatenate([first_of(m, choose_own) for m in (query_first_factor, key_first_factor, value_first_factor)]),
            jnp.stack([attention_norm_gain, feedforward_norm_gain]),
            second_of(output_second_factor, choose_own),
        ],
        [
            second_of(query_second_factor, choose_own),
            second_of(key_second_factor, choose_own),
            second_of(value_second_factor, choose_own),
            first_of(output_first_factor, choose_own),
        ],
    )
    packed, share = pack(*attn_small)
    (qkv_first, gains, out_second), (query_second, key_second, value_second, out_first) = unpack(
        lax.all_gather(packed, turned_both).reshape(cols, rows, -1, lanes), share, *attn_small
    )
    qkv_first = joined_rows(qkv_first)
    gains = joined_rows(gains).astype(jnp.float32)
    out_first = joined_rows(out_first)
    nothing = lambda m: jnp.zeros_like(m)
    qkv_second = jnp.stack(
        [
            jnp.concatenate(
                [
                    by_head(query_second[c], nothing(key_second[c]), nothing(value_second[c])),
                    by_head(nothing(query_second[c]), key_second[c], nothing(value_second[c])),
                    by_head(nothing(query_second[c]), nothing(key_second[c]), value_second[c]),
                ],
                axis=0,
            )
            for c in range(cols)
        ]
    )

    first_parts = [first_of(m, choose_low) for m in (gate_first_factor, up_first_factor)]
    hidden_parts = [
        second_of(gate_second_half, choose_low),
        second_of(up_second_half, choose_low),
        first_of(down_first_half, choose_low),
    ]
    of_group = lambda values, g: values[g * rank : (g + 1) * rank]
    mlp_small = [
        jnp.concatenate([of_group(m, g) for g in range(copies) for m in first_parts]),
        second_of(down_second_factor, choose_low),
    ]

    def middle(n):
        at = slice(n * lanes, (n + 1) * lanes)
        return jnp.stack(
            [
                jnp.stack(
                    [
                        jnp.pad(of_group(m, g)[:, at], ((rank, 0), (0, 0)) if i == 1 else ((0, rank), (0, 0)))
                        for i, m in enumerate(hidden_parts)
                    ]
                )
                for g in range(copies)
            ]
        )

    packs = [pack(mlp_small if n == 0 else [], [middle(n)]) for n in range(blocks_ff)]
    mlp_shards = [
        jnp.concatenate(
            [
                gate_half[:, n * lanes : (n + 1) * lanes],
                up_half[:, n * lanes : (n + 1) * lanes],
                down_half[n * lanes : (n + 1) * lanes],
                packs[n][0],
            ],
            axis=0,
        )
        for n in range(blocks_ff)
    ]

    row_seq = jnp.arange(seqs * part) // part
    mask = (row_seq[:, None] == jnp.arange(rank)[None, :] // RANK).astype(jnp.float32) * scale
    mask_twice, mask_thrice = jnp.tile(mask, (1, 2)), jnp.tile(mask, (1, 3))

    residual = to_tokens(tokens)
    upstream = to_tokens(after(cotangent, residual))
    residual, upstream = lax.optimization_barrier((residual, upstream))
    positions = (lax.axis_index("col") * rows + lax.axis_index("row")) * part + jnp.arange(part)
    cosine, sine = rope_tables(jnp.tile(positions, seqs))
    flat, none = jnp.ones((seqs * part, HEAD_DIM), jnp.float32), jnp.zeros((seqs * part, HEAD_DIM), jnp.float32)
    turning = head_q // HEAD_DIM + 1
    cosine, sine = (
        jnp.tile(jnp.concatenate([jnp.tile(table, (1, 2 * turning)), rest], axis=1), (1, kv_heads))
        for table, rest in ((cosine, flat), (sine, none))
    )
    *messages, low_qkv = project_qkv(
        residual, gains[0:1], mask_thrice, qkv_first, qkv_second, cosine, sine, attn_weight, seqs, units, pairs, pair_width, kv_heads
    )

    def exchange(values):
        return lax.all_to_all(values.reshape(units, part, -1), turned_both, 0, 0, tiled=True)

    def from_pairs(parts):
        split = jnp.stack([v.reshape(seqs, units // seqs, part, pair_width) for v in parts])
        return split.transpose(1, 3, 2, 0, 4).reshape(seqs * part, -1)

    def padded(values):
        return jnp.pad(values, ((0, 0), (0, pair_pad)))

    mlp_weights, earlier = [], residual
    for n in range(blocks_ff):
        shard = after(mlp_shards[n], earlier)
        mlp_weights.append(lax.all_gather(shard, turned_both).reshape(cols, rows, -1, lanes))
        earlier = messages[0]
    first_in = exchange(messages[0]).reshape(length, -1)
    unit_queries = [first_in[:, :pair_width]] + [exchange(v).reshape(length, -1) for v in messages[1:]]
    unit_queries = [padded(v) for v in unit_queries]
    unit_keys = first_in[:, pair_width : pair_width + HEAD_DIM]
    unit_values = first_in[:, pair_width + HEAD_DIM :]
    keys_twice = jnp.concatenate([unit_keys, unit_keys], axis=1)
    values_twice = jnp.concatenate([unit_values, unit_values], axis=1)
    keys_turned, values_turned = unit_keys.T, unit_values.T
    unit_seq = (lax.axis_index("col") * rows + lax.axis_index("row")) * seqs // units
    labels = lax.dynamic_index_in_dim(block_labels, unit_seq, 0, keepdims=True)
    numbers = jnp.arange(BLOCKS)[:, None]
    ends_of = jnp.sum((labels <= numbers).astype(jnp.int32), axis=1, keepdims=True)
    ends = jnp.sum(jnp.where(labels == numbers, ends_of, 0), axis=0, keepdims=True)
    unit_outs, log_sums = [], []
    for p in range(pairs):
        out, log_sum = attend(unit_queries[p], keys_twice, values_turned, ends, pair_heads, factor)
        unit_outs.append(out)
        log_sums.append(log_sum)
    heads_out = from_pairs([exchange(v[:, :pair_width]) for v in unit_outs])
    attended, normed_mlp, low_out = project_out(
        heads_out, residual, gains[1:2], mask, out_first, out_second, attn_weight
    )

    unpacked = [
        unpack(mlp_weights[n][:, :, 3 * lanes :], packs[n][1], mlp_small if n == 0 else [], [middle(n)])
        for n in range(blocks_ff)
    ]
    front_first, down_second = (joined_rows(v) for v in unpacked[0][0])

    def swap(values, step):
        return lax.ppermute(values, "dp", [(i, (i + step) % copies) for i in range(copies)])

    tokens_of = [(normed_mlp, upstream)]
    for step in range(1, copies):
        tokens_of.append((swap(normed_mlp, step), swap(upstream, step)))
    row_sums = jnp.zeros((rows, copies * 3 * rank, lanes), jnp.float32)
    col_sums = jnp.zeros((cols, copies * blocks_ff * 3 * rank, lanes), jnp.float32)
    sums = [None] * copies
    for n in range(blocks_ff):
        order = list(range(copies))
        for step in order if n < blocks_ff - 1 else order[1:] + order[:1]:
            row_sums, col_sums, *sums[step] = feed_forward(
                ((me - step) % copies).reshape(1),
                n,
                *tokens_of[step],
                mask_twice,
                front_first,
                down_second,
                mlp_weights[n],
                unpacked[n][1][0],
                row_sums,
                col_sums,
                sums[step],
                jnp.float32 if n < blocks_ff - 1 or step == 0 else jnp.bfloat16,
            )
    grad_part, mixed_part = sums[0]
    mixed_backs = []
    for step in range(1, copies):
        grad_back, mixed_back = (swap(v, -step) for v in sums[step])
        grad_other = grad_back if step == 1 else grad_other + grad_back
        mixed_backs.append(mixed_back)

    attended_grad, out_rows, out_cols, *grad_messages = project_out_back(
        grad_part,
        grad_other,
        upstream,
        attended,
        gains[1:2],
        mask,
        out_first,
        joined_rows(out_second),
        heads_out,
        low_out,
        attn_weight,
        seqs,
        units,
        pairs,
        pair_width,
    )
    row_sums, col_sums, _ = lax.optimization_barrier((row_sums, col_sums, grad_messages))
    row_shares = lax.psum_scatter(row_sums.reshape(units, -1, lanes), both, scatter_dimension=0)
    col_shares = lax.psum_scatter(col_sums.reshape(units, -1, lanes), turned_both, scatter_dimension=0)
    unit_grads = [padded(exchange(v).reshape(length, -1)) for v in grad_messages]
    full_cosine, full_sine = (table.T for table in rope_tables(jnp.arange(length)))
    query_moved, kv_grad = [], None
    for p in range(pairs):
        if p == pairs - 1 and p > 0:
            mixed_backs, _ = lax.optimization_barrier((mixed_backs, kv_now))
            mixed_part = sum((v.astype(jnp.float32) for v in mixed_backs), mixed_part)
            mixed_out = low(attended + mixed_part).reshape(seqs * part, rows, lanes).transpose(1, 0, 2)
            ends, mixed_out = lax.optimization_barrier((ends, mixed_out))
        query_now, kv_now = attend_back(
            unit_queries[p],
            unit_grads[p],
            unit_outs[p],
            log_sums[p],
            keys_twice,
            values_twice,
            keys_turned,
            ends,
            full_cosine,
            full_sine,
            pair_heads,
            factor,
        )
        kv_grad = kv_now if kv_grad is None else kv_grad + kv_now
        if p == pairs - 1:
            query_now = jnp.concatenate([query_now[:, :pair_width], low(kv_grad)], axis=1)
            if pairs == 1:
                mixed_part = sum((v.astype(jnp.float32) for v in mixed_backs), mixed_part)
                mixed_out = low(attended + mixed_part).reshape(seqs * part, rows, lanes).transpose(1, 0, 2)
            mixed_out = to_features(mixed_out, seqs)
            query_now, mixed_out, row_shares, col_shares, query_moved = lax.optimization_barrier(
                (query_now, mixed_out, row_shares, col_shares, query_moved)
            )
        query_moved.append(exchange(query_now[:, : query_now.shape[1] if p == pairs - 1 else pair_width]))
    row_height = row_shares.shape[0]
    row_total = lax.all_gather(jnp.pad(row_shares, ((0, -row_height % 64), (0, 0))), ("dp", "col"))[..., :row_height, :]
    col_total = lax.all_gather(col_shares, ("dp", "row"))
    kv_moved = query_moved[-1][..., pair_width:].reshape(seqs, cols, kv_heads, kv_copies, part, -1)
    kv_moved = low(kv_moved.astype(jnp.float32).sum(axis=3)) if kv_copies > 1 else kv_moved[:, :, :, 0]
    query_moved[-1] = query_moved[-1][..., :pair_width]
    query_moved = [v.reshape(seqs, cols, -1, part, pair_width) for v in query_moved]
    token_grad, qkv_rows, qkv_cols = project_qkv_back(
        residual, attended_grad, gains[0:1], mask_thrice, qkv_first, qkv_second, low_qkv, kv_moved, query_moved, attn_weight
    )

    row_total, col_total, _ = lax.optimization_barrier((row_total, col_total, token_grad))

    def everywhere(values, axes, count):
        copied = jnp.broadcast_to(values[None], (count,) + values.shape)
        return lax.all_to_all(copied, axes, 0, 0, tiled=True).reshape(copies, -1, lanes)

    def wide_second(values):
        return lax.dot_general(
            choose_wide, values, (((1,), (0,)), ((), ())), precision=lax.Precision.HIGHEST, preferred_element_type=jnp.float32
        )

    def wide_first(values):
        return lax.dot_general(
            values, choose_wide, (((0,), (1,)), ((), ())), precision=lax.Precision.HIGHEST, preferred_element_type=jnp.float32
        )

    row_total = row_total.reshape(copies, copies, 3, rank, lanes).sum(axis=0)
    gate_first_gradient, up_first_gradient = (wide_first(row_total[:, i].reshape(-1, lanes)) for i in range(2))
    down_second_gradient = wide_second(row_total[:, 2].reshape(-1, lanes))
    col_total = col_total.reshape(copies, copies, blocks_ff, 3, rank, lanes)
    pieces = [
        [col_total[x, :, n, i].reshape(-1, lanes) for x in range(copies) for n in range(blocks_ff)] for i in range(3)
    ]
    gate_second_gradient, up_second_gradient = (
        jnp.concatenate([wide_second(v) for v in pieces[i]], axis=1) for i in range(2)
    )
    down_first_gradient = jnp.concatenate([wide_first(v) for v in pieces[2]], axis=0)

    row_cut = jnp.concatenate([qkv_rows, out_rows], axis=1).reshape(rows, cols, -1, lanes)
    col_cut = jnp.concatenate([qkv_cols.reshape(cols, -1, lanes), out_cols], axis=1)
    col_cut = col_cut.reshape(cols, rows, -1, lanes).transpose(1, 0, 2, 3)
    cut = row_cut.shape[2]
    attn_shares = jnp.concatenate([row_cut, col_cut], axis=2).reshape(units, -1, lanes)
    attn_sums = jnp.sum(lax.all_to_all(attn_shares, both, 0, 0, tiled=True).astype(jnp.float32), axis=0)
    attn_rows = everywhere(attn_sums[:cut], ("dp", "col"), copies * cols).reshape(copies, 4, rank, lanes)
    attn_cols = everywhere(attn_sums[cut:], ("dp", "row"), copies * rows)
    query_first_gradient, key_first_gradient, value_first_gradient = (
        wide_first(attn_rows[:, i].reshape(-1, lanes)) for i in range(3)
    )
    output_second_gradient = wide_second(attn_rows[:, 3].reshape(-1, lanes))
    output_first_gradient = wide_first(attn_cols[:, -rank:].reshape(-1, lanes))
    qkv_second_gradient = wide_second(attn_cols[:, :-rank].reshape(copies * rank, -1)).reshape(
        adapter_cols, kv_heads, -1
    )
    query_second_gradient = qkv_second_gradient[..., :head_q].reshape(adapter_cols, -1)
    key_second_gradient = qkv_second_gradient[..., head_q : head_q + HEAD_DIM].reshape(adapter_cols, -1)
    value_second_gradient = qkv_second_gradient[..., head_q + HEAD_DIM :].reshape(adapter_cols, -1)

    return (
        mixed_out,
        to_features(token_grad, seqs),
        query_first_gradient,
        query_second_gradient,
        key_first_gradient,
        key_second_gradient,
        value_first_gradient,
        value_second_gradient,
        output_first_gradient,
        output_second_gradient,
        gate_first_gradient,
        gate_second_gradient,
        up_first_gradient,
        up_second_gradient,
        down_first_gradient,
        down_second_gradient,
    )


def solution(mesh):
    in_specs = (
        P("col", "dp", "row"),
        P("col", "dp", "row"),
        P("dp", None),
        P("dp"),
        P(),
        P("row"),
        P("row"),
        P("row", "col"),
        P("row", "col"),
        P("row", "col"),
        P("col", "row"),
        P("row", "col"),
        P("row", "col"),
        P("col", "row"),
        P("row", None),
        P(None, "col"),
        P("row", None),
        P(None, "col"),
        P("row", None),
        P(None, "col"),
        P("col", None),
        P(None, "row"),
        P("row", None),
        P(None, "col"),
        P("row", None),
        P(None, "col"),
        P("col", None),
        P(None, "row"),
    )
    out_specs = (
        P("col", "dp", "row"),
        P("col", "dp", "row"),
        P("row", None),
        P(None, "col"),
        P("row", None),
        P(None, "col"),
        P("row", None),
        P(None, "col"),
        P("col", None),
        P(None, "row"),
        P("row", None),
        P(None, "col"),
        P("row", None),
        P(None, "col"),
        P("col", None),
        P(None, "row"),
    )
    return jax.shard_map(local, mesh=mesh, in_specs=in_specs, out_specs=out_specs, check_vma=False)
```

```python
import functools, math
import jax, jax.numpy as jnp
from jax import lax
from jax.sharding import PartitionSpec as P
from jax.experimental import pallas as pl
from jax.experimental.pallas import tpu as pltpu

HEAD_DIM = 64
RANK = 16
BLOCKS = 32
EPS = 1e-05
ROPE_BASE = 500000.0
GATHER_ROWS = 128
TILE = 512
REACH = 256
LOG2E = math.log2(math.e)
NEG = -1e30


def nt(a, b):
    return lax.dot_general(a, b, (((1,), (1,)), ((), ())), preferred_element_type=jnp.float32)


def nn(a, b):
    return lax.dot_general(a, b, (((1,), (0,)), ((), ())), preferred_element_type=jnp.float32)


def half_of(x, e):
    lane = lax.broadcasted_iota(jnp.int32, x.shape, 1)
    return jnp.where((lane < 64) if e == 0 else (lane >= 64), x, jnp.zeros_like(x))


def doubled(kv):
    wide = kv.astype(jnp.float32)
    turned = pltpu.roll(wide, 64, 1)
    lane = lax.broadcasted_iota(jnp.int32, wide.shape, 1)
    return jnp.where(lane < 64, wide, turned).astype(jnp.bfloat16), jnp.where(lane < 64, turned, wide).astype(jnp.bfloat16)


def fwd_kernel(heads, factor, end_ref, q_ref, kv_ref, o_ref, lse_ref, acc_ref, m_ref, l_ref, k2_ref, vt_ref):
    i = pl.program_id(0)
    tq = q_ref.shape[0]
    q0 = i * tq
    c = factor * LOG2E

    @pl.when(i == 0)
    def _():
        for t in range(kv_ref.shape[0] // tq):
            rows = slice(t * tq, (t + 1) * tq)
            k2_ref[rows, :] = doubled(kv_ref[rows, :])[0]
            vt_ref[:, rows] = kv_ref[rows, :].astype(jnp.float32).T[64:, :].astype(jnp.bfloat16)

    ends = end_ref[...]
    m_ref[...] = jnp.full_like(m_ref, NEG)
    l_ref[...] = jnp.zeros_like(l_ref)
    acc_ref[...] = jnp.zeros_like(acc_ref)

    def tile(k0, size, masked):
        kk = k2_ref[pl.ds(k0, size), :]
        vv = vt_ref[:, pl.ds(k0, size)]
        if masked:
            allowed = (lax.broadcasted_iota(jnp.int32, (size, tq), 0) + k0) < ends
        for h in range(heads):
            qh = half_of(q_ref[:, (h // 2) * 128:(h // 2 + 1) * 128], h % 2)
            s = nt(kk, qh) * c
            if masked:
                s = jnp.where(allowed, s, NEG)
            m_old = m_ref[h:h + 1, :]
            m_new = jnp.maximum(m_old, jnp.max(s, axis=0, keepdims=True))
            p = jnp.exp2(s - m_new)
            alpha = jnp.exp2(m_old - m_new)
            l_ref[h:h + 1, :] = l_ref[h:h + 1, :] * alpha + jnp.sum(p, axis=0, keepdims=True)
            m_ref[h:h + 1, :] = m_new
            a = pl.ds(h * 64, 64)
            acc_ref[a, :] = acc_ref[a, :] * alpha + nn(vv, p.astype(jnp.bfloat16))

    def body(j, _):
        tile(pl.multiple_of(j * 2 * tq, tq), 2 * tq, False)
        return 0

    lax.fori_loop(0, i // 2, body, 0)
    last = pl.num_programs(0) - 1

    for odd in (False, True):
        for reach in (REACH, 0):

            @pl.when((i % 2 == int(odd)) & ((i < last) if reach else (i == last)))
            def _():
                before = tq if odd else 0
                tile(pl.multiple_of(q0 - before, tq), before + tq + reach, True)

    lse_ref[...] = m_ref[...] + jnp.log2(l_ref[...])
    inv = 1.0 / l_ref[...]
    for p in range(o_ref.shape[1] // 128):
        parts = []
        for h in (2 * p, 2 * p + 1):
            if h < heads:
                parts.append(acc_ref[h * 64:(h + 1) * 64, :] * inv[h:h + 1, :])
            else:
                parts.append(jnp.zeros((64, tq), jnp.float32))
        o_ref[:, p * 128:(p + 1) * 128] = jnp.concatenate(parts, axis=0).T.astype(o_ref.dtype)


def attend(q, kv, ends, heads, factor):
    (q, q_at), (kv, kv_at) = q, kv
    length, width = q.shape[0], 128
    tq = min(TILE, length)
    rows = 8
    return pl.pallas_call(
        functools.partial(fwd_kernel, heads, factor),
        grid=(length // tq,),
        in_specs=[
            pl.BlockSpec((1, tq), lambda i: (0, i)),
            pl.BlockSpec((tq, width), lambda i: (i, q_at)),
            pl.BlockSpec((length, 128), lambda i: (0, kv_at)),
        ],
        out_specs=[
            pl.BlockSpec((tq, width), lambda i: (i, 0)),
            pl.BlockSpec((rows, tq), lambda i: (0, i)),
        ],
        out_shape=[
            jax.ShapeDtypeStruct((length, width), jnp.bfloat16),
            jax.ShapeDtypeStruct((rows, length), jnp.float32),
        ],
        scratch_shapes=[
            pltpu.VMEM((heads * 64, tq), jnp.float32),
            pltpu.VMEM((rows, tq), jnp.float32),
            pltpu.VMEM((rows, tq), jnp.float32),
            pltpu.VMEM((length, 128), jnp.bfloat16),
            pltpu.VMEM((64, length), jnp.bfloat16),
        ],
        compiler_params=pltpu.CompilerParams(vmem_limit_bytes=48 * 2**20),
        cost_estimate=pl.CostEstimate(
            flops=2 * heads * length * length * 64, bytes_accessed=4 * length * width + length * 384, transcendentals=heads * length * length // 2
        ),
        name="attend_forward",
    )(ends, q, kv)


def turn_back(values, cosine, sine):
    high, rest = values[:32, :], values[32:, :]
    return jnp.concatenate([high * cosine + rest * sine, rest * cosine - high * sine], axis=0)


def bwd_kernel(heads, factor, last, end_ref, cos_ref, sin_ref, q_ref, do_ref, o_ref, lse_ref, kv_ref, *refs):
    if last:
        earlier_ref, dq_ref, *refs = refs
    else:
        dq_ref, dkv_ref, *refs = refs
    dqt_ref, delta_ref, dk_ref, dv_ref, k2_ref, v2_ref, kt_ref = refs
    j = pl.program_id(0)
    n = pl.num_programs(0)
    tk = kv_ref.shape[0]
    length, width = q_ref.shape
    c = factor * LOG2E
    k2_ref[...], v2_ref[...] = doubled(kv_ref[...])
    kt_ref[...] = kv_ref[...].astype(jnp.float32).T[:64, :].astype(jnp.bfloat16)

    @pl.when(j == 0)
    def _():
        dqt_ref[...] = jnp.zeros_like(dqt_ref)
        delta_ref[...] = jnp.zeros_like(delta_ref)
        for t in range(length // tk):
            rows = slice(t * tk, (t + 1) * tk)
            for p in range(width // 128):
                prod = do_ref[rows, p * 128:(p + 1) * 128].astype(jnp.float32) * o_ref[rows, p * 128:(p + 1) * 128].astype(jnp.float32)
                turned = prod.T
                for h in (2 * p, 2 * p + 1):
                    if h < heads:
                        delta_ref[h:h + 1, rows] = jnp.sum(turned[(h % 2) * 64:(h % 2 + 1) * 64, :], axis=0, keepdims=True)

    dk_ref[...] = jnp.zeros_like(dk_ref)
    dv_ref[...] = jnp.zeros_like(dv_ref)

    def tile(q0, count, size, masked):
        rows = pl.ds(q0, count)
        kk = k2_ref[:size, :]
        vv = v2_ref[:size, :]
        kt = kt_ref[:, :size]
        if masked:
            allowed = (lax.broadcasted_iota(jnp.int32, (size, count), 0) + j * tk) < end_ref[:, rows]
        for h in range(heads):
            lanes = slice((h // 2) * 128, (h // 2 + 1) * 128)
            qh = half_of(q_ref[rows, lanes], h % 2)
            gh = half_of(do_ref[rows, lanes], h % 2)
            s = nt(kk, qh) * c - lse_ref[h:h + 1, rows]
            if masked:
                s = jnp.where(allowed, s, NEG)
            p = jnp.exp2(s)
            dp = nt(vv, gh)
            ds = (p * (dp - delta_ref[h:h + 1, rows])).astype(jnp.bfloat16)
            dv_ref[:size, :] += nn(p.astype(jnp.bfloat16), gh)
            dk_ref[:size, :] += nn(ds, qh)
            dqt_ref[h * 64:(h + 1) * 64, rows] += nn(kt, ds)

    @pl.when(j > 0)
    def _():
        tile(pl.multiple_of((j - 1) * tk, tk), tk, REACH, True)

    rest = n - 1 - j
    for odd in (False, True):

        @pl.when(rest % 2 == int(odd))
        def _():
            tile(pl.multiple_of(j * tk, tk), 2 * tk if odd else tk, tk, True)

    def body(i, _):
        tile(pl.multiple_of((j + 1 + rest % 2 + 2 * i) * tk, tk), 2 * tk, tk, False)
        return 0

    lax.fori_loop(0, rest // 2, body, 0)

    own = pl.ds(pl.multiple_of(j * tk, tk), tk)
    dk = dk_ref[...].T
    dv = dv_ref[...].T
    dk = turn_back(dk[:64] + dk[64:], cos_ref[:, own], sin_ref[:, own]) * factor
    dkv = jnp.concatenate([dk, dv[:64] + dv[64:]], axis=0).T
    if last:
        dq_ref[own, width:] = (dkv if earlier_ref is None else dkv + earlier_ref[...]).astype(dq_ref.dtype)
    else:
        dkv_ref[...] = dkv

    @pl.when(j == n - 1)
    def _():
        for t in range(length // tk):
            rows = slice(t * tk, (t + 1) * tk)
            for p in range(width // 128):
                parts = []
                for h in (2 * p, 2 * p + 1):
                    if h < heads:
                        parts.append(turn_back(dqt_ref[h * 64:(h + 1) * 64, rows], cos_ref[:, rows], sin_ref[:, rows]) * factor)
                    else:
                        parts.append(jnp.zeros((64, tk), jnp.float32))
                dq_ref[rows, p * 128:(p + 1) * 128] = jnp.concatenate(parts, axis=0).T.astype(dq_ref.dtype)


def attend_back(q, do, o, lse, kv, ends, cosine, sine, heads, factor, earlier=None, last=True):
    (q, q_at), (kv, kv_at) = q, kv
    length, width = o.shape
    tk = min(TILE, length)
    whole = lambda shape, at=0: pl.BlockSpec(shape, lambda j: (0, at))
    by_block = lambda at=0: pl.BlockSpec((tk, 128), lambda j: (j, at))
    if last and earlier is None:
        earlier = jnp.zeros((length, 128), jnp.float32)
    return pl.pallas_call(
        functools.partial(bwd_kernel, heads, factor, last),
        grid=(length // tk,),
        in_specs=[
            whole((1, length)),
            whole((32, length)),
            whole((32, length)),
            whole((length, width), q_at),
            whole((length, width)),
            whole((length, width)),
            whole((8, length)),
            by_block(kv_at),
        ]
        + ([by_block()] if last else []),
        out_specs=[whole((length, width + 128))] if last else [whole((length, width)), by_block()],
        out_shape=[jax.ShapeDtypeStruct((length, width + 128), jnp.bfloat16)]
        if last
        else [jax.ShapeDtypeStruct((length, width), jnp.bfloat16), jax.ShapeDtypeStruct((length, 128), jnp.float32)],
        scratch_shapes=[
            pltpu.VMEM((heads * 64, length), jnp.float32),
            pltpu.VMEM((8, length), jnp.float32),
            pltpu.VMEM((tk, 128), jnp.float32),
            pltpu.VMEM((tk, 128), jnp.float32),
            pltpu.VMEM((tk, 128), jnp.bfloat16),
            pltpu.VMEM((tk, 128), jnp.bfloat16),
            pltpu.VMEM((64, tk), jnp.bfloat16),
        ],
        compiler_params=pltpu.CompilerParams(vmem_limit_bytes=48 * 2**20),
        cost_estimate=pl.CostEstimate(
            flops=5 * heads * length * length * 64,
            bytes_accessed=8 * length * width + length * 512,
            transcendentals=heads * length * length // 2,
        ),
        name="attend_backward",
    )(ends, cosine, sine, q, do, o, lse, kv, *([earlier] if last else []))


def buffered_once(shape, index_map):
    return pl.BlockSpec(shape, index_map, pipeline_mode=pl.Buffered(1))


def normalized(values, gain):
    inverse = lax.rsqrt(jnp.mean(values * values, axis=-1, keepdims=True) + EPS)
    return inverse, (values * inverse * gain).astype(jnp.bfloat16)


def norm_back(values, inverse, gain, upstream):
    scaled = upstream * gain
    weighted = jnp.mean(scaled * values, axis=-1, keepdims=True)
    return inverse * scaled - values * (inverse * inverse * inverse * weighted)


def qkv_kernel(pairs, kv_heads, token_ref, gain_ref, mask_ref, first_ref, second_ref, cos_ref, sin_ref, *refs):
    weight_refs, refs = refs[:3], refs[3:]
    message_refs, low_ref, normed_ref = refs[:pairs], refs[pairs], refs[pairs + 1]
    rows, lanes, chunk = weight_refs[0].shape[1:]
    count = token_ref.shape[0]
    seqs, _, units, part, _ = message_refs[0].shape
    pair_width = message_refs[0].shape[4] - 2 * HEAD_DIM

    @pl.when(pl.program_id(0) == 0)
    def _():
        _, normed = normalized(token_ref[...].astype(jnp.float32), gain_ref[...])
        normed_ref[...] = normed
        low_ref[...] = (nt(normed, first_ref[...]) * mask_ref[...]).astype(jnp.bfloat16)

    raw = jnp.concatenate(
        [nn(normed_ref[...], w[0].reshape(rows * lanes, chunk)) for w in weight_refs], axis=1
    ) + nn(low_ref[...], second_ref[0])
    width = raw.shape[1]
    lane = lax.broadcasted_iota(jnp.int32, raw.shape, 1)
    turned = jnp.where(lane % HEAD_DIM < HEAD_DIM // 2, -pltpu.roll(raw, width - HEAD_DIM // 2, 1), pltpu.roll(raw, HEAD_DIM // 2, 1))
    out = (raw * cos_ref[...] + turned * sin_ref[...]).astype(jnp.bfloat16)
    head_width = width // kv_heads
    for s in range(seqs):
        at = slice(s * part, (s + 1) * part)
        for u in range(units):
            base = u * kv_heads // units * head_width
            inside = u % (units // kv_heads) * pairs * pair_width
            kv = out[at, base + head_width - 2 * HEAD_DIM : base + head_width]
            for p in range(pairs):
                begin = base + inside + p * pair_width
                queries = out[at, begin : begin + pair_width]
                message_refs[p][s, 0, u] = jnp.concatenate([queries, kv], axis=1) if p == 0 else queries


def project_qkv(tokens, gain, mask, first, second, cosine, sine, weight, seqs, units, pairs, pair_width, kv_heads):
    count, features = tokens.shape
    cols, rows, lanes, _ = weight.shape
    width = second.shape[2]
    chunk = width // 3
    part = count // seqs
    ahead = lanes // chunk
    whole = lambda shape: pl.BlockSpec(shape, lambda c: (0,) * len(shape))
    message = lambda wide: (seqs, cols, units // (seqs * cols), part, wide)
    widths = [pair_width + 2 * HEAD_DIM] + [pair_width] * (pairs - 1)
    block = lambda wide: pl.BlockSpec((seqs, 1) + message(wide)[2:], lambda c: (0, c, 0, 0, 0))
    weights = lambda at: pl.BlockSpec((1, rows, lanes, chunk), lambda c: (c, 0, 0, ahead + at))
    return pl.pallas_call(
        functools.partial(qkv_kernel, pairs, kv_heads),
        grid=(cols,),
        in_specs=[
            whole((count, features)),
            whole((1, features)),
            whole(mask.shape),
            whole(first.shape),
            pl.BlockSpec((1,) + second.shape[1:], lambda c: (c, 0, 0)),
            whole((count, width)),
            whole((count, width)),
            weights(0),
            weights(1),
            weights(2),
        ],
        out_specs=[block(w) for w in widths] + [whole(mask.shape)],
        out_shape=[jax.ShapeDtypeStruct(message(w), jnp.bfloat16) for w in widths]
        + [jax.ShapeDtypeStruct(mask.shape, jnp.bfloat16)],
        scratch_shapes=[pltpu.VMEM((count, features), jnp.bfloat16)],
        compiler_params=pltpu.CompilerParams(vmem_limit_bytes=48 * 2**20),
        cost_estimate=pl.CostEstimate(
            flops=2 * count * features * cols * width,
            bytes_accessed=2 * features * cols * width + 4 * count * features,
            transcendentals=count,
        ),
        name="project_qkv",
    )(tokens, gain, mask, first, second, cosine, sine, weight, weight, weight)


def joined_messages(query_refs, kv_ref):
    seqs, _, kv_heads = kv_ref.shape[:3]
    units = query_refs[0].shape[2]
    parts = []
    for j in range(kv_heads):
        for u in range(j * units // kv_heads, (j + 1) * units // kv_heads):
            parts += [jnp.concatenate([q[s, 0, u] for s in range(seqs)], axis=0) for q in query_refs]
        parts.append(jnp.concatenate([kv_ref[s, 0, j] for s in range(seqs)], axis=0))
    return jnp.concatenate(parts, axis=1)


def qkv_sums_kernel(token_ref, gain_ref, mask_ref, second_ref, low_ref, kv_ref, *refs):
    query_refs, refs = refs[:-5], refs[-5:]
    lowered_out_ref, rows_ref, cols_ref, lowered_ref, low_turned_ref = refs
    c = pl.program_id(0)
    rows, _, lanes = rows_ref.shape
    kv_heads = kv_ref.shape[2]
    rank = mask_ref.shape[1] // 3

    @pl.when(c == 0)
    def _():
        lowered_ref[...] = jnp.zeros_like(lowered_ref)
        low_turned_ref[...] = low_ref[...].astype(jnp.float32).T.astype(jnp.bfloat16)

    e = joined_messages(query_refs, kv_ref)
    lowered_ref[...] += nt(e, second_ref[0])
    sums = nn(low_turned_ref[...], e)
    lane = lax.broadcasted_iota(jnp.int32, (rank, sums.shape[1]), 1) % (sums.shape[1] // kv_heads)
    query_lanes = sums.shape[1] // kv_heads - 2 * HEAD_DIM
    cols_ref[0] = jnp.where(
        lane < query_lanes,
        sums[:rank],
        jnp.where(lane < query_lanes + HEAD_DIM, sums[rank : 2 * rank], sums[2 * rank :]),
    ).astype(cols_ref.dtype)

    @pl.when(c == pl.num_programs(0) - 1)
    def _():
        lowered = lowered_ref[...] * mask_ref[...]
        lowered_out_ref[...] = lowered.astype(jnp.bfloat16)
        _, normed = normalized(token_ref[...].astype(jnp.float32), gain_ref[...])
        turned = nn(lowered.T.astype(jnp.bfloat16), normed)
        for r in range(rows):
            rows_ref[r] = turned[:, r * lanes : (r + 1) * lanes].astype(rows_ref.dtype)


def qkv_grad_sums(tokens, gain, mask, second, low_qkv, kv, queries, rows):
    count, features = tokens.shape
    cols, _, width = second.shape
    rank = mask.shape[1] // 3
    lanes = features // rows
    whole = lambda shape: buffered_once(shape, lambda c: (0,) * len(shape))
    by_unit = lambda v: pl.BlockSpec((v.shape[0], 1) + v.shape[2:], lambda c: (0, c, 0, 0, 0))
    return pl.pallas_call(
        qkv_sums_kernel,
        grid=(cols,),
        in_specs=[
            whole((count, features)),
            whole((1, features)),
            whole(mask.shape),
            pl.BlockSpec((1,) + second.shape[1:], lambda c: (c, 0, 0)),
            whole(low_qkv.shape),
            by_unit(kv),
        ]
        + [by_unit(q) for q in queries],
        out_specs=[
            pl.BlockSpec(mask.shape, lambda c: (0, 0)),
            pl.BlockSpec((rows, 3 * rank, lanes), lambda c: (0, 0, 0)),
            pl.BlockSpec((1, rank, width), lambda c: (c, 0, 0)),
        ],
        out_shape=[
            jax.ShapeDtypeStruct(mask.shape, jnp.bfloat16),
            jax.ShapeDtypeStruct((rows, 3 * rank, lanes), jnp.bfloat16),
            jax.ShapeDtypeStruct((cols, rank, width), jnp.bfloat16),
        ],
        scratch_shapes=[
            pltpu.VMEM((count, 3 * rank), jnp.float32),
            pltpu.VMEM((3 * rank, count), jnp.bfloat16),
        ],
        compiler_params=pltpu.CompilerParams(vmem_limit_bytes=48 * 2**20),
        cost_estimate=pl.CostEstimate(
            flops=2 * count * features * cols * width,
            bytes_accessed=2 * count * cols * width + 2 * count * features,
            transcendentals=count,
        ),
        name="qkv_grad_sums",
    )(tokens, gain, mask, second, low_qkv, kv, *queries)


def qkv_back_kernel(token_ref, attended_ref, gain_ref, first_ref, lowered_ref, kv_ref, *refs):
    query_refs, refs = refs[:-5], refs[-5:]
    weight_refs, (out_ref, grad_ref) = refs[:3], refs[3:]
    c = pl.program_id(0)
    rows, lanes, chunk = weight_refs[0].shape[1:]

    @pl.when(c == 0)
    def _():
        grad_ref[...] = nn(lowered_ref[...], first_ref[...])

    e = joined_messages(query_refs, kv_ref)
    for r in range(rows):
        total = nt(e[:, :chunk], weight_refs[0][0, r])
        for i in (1, 2):
            total += nt(e[:, i * chunk : (i + 1) * chunk], weight_refs[i][0, r])
        grad_ref[:, r * lanes : (r + 1) * lanes] += total

    @pl.when(c == pl.num_programs(0) - 1)
    def _():
        values = token_ref[...].astype(jnp.float32)
        inverse = lax.rsqrt(jnp.mean(values * values, axis=-1, keepdims=True) + EPS)
        out = (attended_ref[...] + norm_back(values, inverse, gain_ref[...], grad_ref[...])).astype(jnp.bfloat16)
        for r in range(rows):
            out_ref[r] = out[:, r * lanes : (r + 1) * lanes]


def project_qkv_back(tokens, attended_grad, gain, first, lowered, kv, queries, weight):
    count, features = tokens.shape
    cols, rows, lanes, wide = weight.shape
    width = wide - lanes
    chunk = width // 3
    ahead = lanes // chunk
    whole = lambda shape: buffered_once(shape, lambda c: (0,) * len(shape))
    by_unit = lambda v: pl.BlockSpec((v.shape[0], 1) + v.shape[2:], lambda c: (0, c, 0, 0, 0))
    weights = lambda at: pl.BlockSpec((1, rows, lanes, chunk), lambda c: (c, 0, 0, ahead + at))
    return pl.pallas_call(
        qkv_back_kernel,
        grid=(cols,),
        in_specs=[
            whole((count, features)),
            whole((count, features)),
            whole((1, features)),
            whole(first.shape),
            whole(lowered.shape),
            by_unit(kv),
        ]
        + [by_unit(q) for q in queries]
        + [weights(0), weights(1), weights(2)],
        out_specs=pl.BlockSpec((rows, count, lanes), lambda c: (0, 0, 0)),
        out_shape=jax.ShapeDtypeStruct((rows, count, lanes), jnp.bfloat16),
        scratch_shapes=[pltpu.VMEM((count, features), jnp.float32)],
        compiler_params=pltpu.CompilerParams(vmem_limit_bytes=60 * 2**20),
        cost_estimate=pl.CostEstimate(
            flops=8 * count * features * cols * width,
            bytes_accessed=2 * features * cols * width + 10 * count * features,
            transcendentals=count,
        ),
        name="project_qkv_back",
    )(tokens, attended_grad, gain, first, lowered, kv, *queries, weight, weight, weight)


def mlp_kernel(fresh, goes_on, block, group_ref, h_ref, e_ref, mask_ref, first_ref, second_ref, gate_ref, up_ref, down_ref, mids_ref, *refs):
    if goes_on:
        sums_in_ref, grad_in_ref = refs[:2]
        refs = refs[2:]
    elif not fresh:
        refs = refs[1:]
    sums_ref, grad_out_ref, hidden_ref, low_down_ref = refs[:4]
    low_ref, low_turned_ref, lowered_ref, lowered_turned_ref, sum_front_ref, sum_down_ref = refs[4:10]
    grad_ref = refs[10] if len(refs) > 10 else grad_out_ref
    c = pl.program_id(0)
    rows, lanes = gate_ref.shape[1], gate_ref.shape[3]
    rank = second_ref.shape[0]

    @pl.when(c == 0)
    def _():
        low_now = nt(h_ref[...], first_ref[...]) * mask_ref[...]
        low_ref[...] = low_now.astype(jnp.bfloat16)
        low_turned_ref[...] = low_now.T.astype(jnp.bfloat16)
        lowered_now = nt(e_ref[...], second_ref[...]) * mask_ref[:, :rank]
        lowered_ref[...] = lowered_now.astype(jnp.bfloat16)
        lowered_turned_ref[...] = lowered_now.T.astype(jnp.bfloat16)
        sum_front_ref[...] = jnp.zeros_like(sum_front_ref)
        sum_down_ref[...] = jnp.zeros_like(sum_down_ref)
        if goes_on:
            grad_ref[...] = grad_in_ref[...]
            sums_ref[...] = sums_in_ref[...]
        else:
            grad_ref[...] = jnp.zeros_like(grad_ref)
            sums_ref[...] = jnp.zeros_like(sums_ref)

    h = h_ref[...]
    gate_second, up_second, down_first = mids_ref[0, 0, 0], mids_ref[0, 0, 1], mids_ref[0, 0, 2, :rank]
    gate = nn(h, gate_ref[0].reshape(rows * lanes, lanes)) + nn(low_ref[...], gate_second)
    up = nn(h, up_ref[0].reshape(rows * lanes, lanes)) + nn(low_ref[...], up_second)
    upstream = nn(lowered_ref[...], down_first)
    for r in range(rows):
        upstream += nt(e_ref[:, r * lanes : (r + 1) * lanes], down_ref[0, r])
    sigmoid = 1.0 / (1.0 + jnp.exp(-gate))
    swish = gate * sigmoid
    hidden = (swish * up).astype(jnp.bfloat16)
    gate_grad = (upstream * up * (sigmoid + swish * (1.0 - sigmoid))).astype(jnp.bfloat16)
    up_grad = (upstream * swish).astype(jnp.bfloat16)
    for r in range(rows):
        at = slice(r * lanes, (r + 1) * lanes)
        grad_ref[:, at] += nt(gate_grad, gate_ref[0, r]) + nt(up_grad, up_ref[0, r])
    hidden_ref[...] = hidden
    sum_front_ref[...] += nt(gate_grad, gate_second) + nt(up_grad, up_second)
    sum_down_ref[...] += nt(hidden, down_first)
    col_sum = jnp.concatenate(
        [nn(low_turned_ref[:rank], gate_grad), nn(low_turned_ref[rank:], up_grad), nn(lowered_turned_ref[...], hidden)],
        axis=0,
    )
    row_share, col_share = 3 * rank // sums_ref.shape[1], 3 * rank // rows
    begin = share_height(row_share) + block * share_height(col_share)
    for r in range(rows):
        sums_ref[r, c, begin : begin + col_share] = col_sum[r * col_share : (r + 1) * col_share]

    @pl.when(c == pl.num_programs(0) - 1)
    def _():
        front_now = sum_front_ref[...] * mask_ref[...]
        grad_out_ref[...] = (grad_ref[...] + nn(front_now.astype(jnp.bfloat16), first_ref[...])).astype(grad_out_ref.dtype)
        down_now = sum_down_ref[...] * mask_ref[:, :rank]
        low_down_ref[...] = down_now.astype(jnp.bfloat16)
        front_sum = nn(front_now.T.astype(jnp.bfloat16), h_ref[...])
        down_sum = nn(down_now.T.astype(jnp.bfloat16), e_ref[...])
        for r in range(rows):
            at = slice(r * lanes, (r + 1) * lanes)
            now = jnp.concatenate([front_sum[:, at], down_sum[:, at]], axis=0)
            for to in range(sums_ref.shape[1]):
                sums_ref[r, to, :row_share] += now[to * row_share : (to + 1) * row_share]


def share_height(count):
    return -(-count // 8) * 8


def feed_forward(group, block, blocks, h, e, mask, first, second, weight, mids, sums, earlier, dtype):
    count, features = h.shape
    cols, rows, _, lanes = weight.shape
    rank = mids.shape[3] // 2
    groups = mids.shape[1]
    goes_on = earlier is not None
    fresh = sums is None
    whole = lambda shape: buffered_once(shape, lambda c, g: (0,) * len(shape))
    weights = lambda at: pl.BlockSpec((1, rows, lanes, lanes), lambda c, g: (c, 0, at, 0))
    height = share_height(3 * rank // cols) + blocks * share_height(3 * rank // rows)
    sums_shape = (rows, cols, height, lanes)
    anywhere = pl.BlockSpec(memory_space=pl.ANY)
    scratch = [
        pltpu.VMEM((count, 2 * rank), jnp.bfloat16),
        pltpu.VMEM((2 * rank, count), jnp.bfloat16),
        pltpu.VMEM((count, rank), jnp.bfloat16),
        pltpu.VMEM((rank, count), jnp.bfloat16),
        pltpu.VMEM((count, 2 * rank), jnp.float32),
        pltpu.VMEM((count, rank), jnp.float32),
    ]
    if dtype != jnp.float32:
        scratch += [pltpu.VMEM((count, features), jnp.float32)]
    return pl.pallas_call(
        functools.partial(mlp_kernel, fresh, goes_on, block),
        grid_spec=pltpu.PrefetchScalarGridSpec(
            num_scalar_prefetch=1,
            grid=(cols,),
            in_specs=[
                whole((count, features)),
                whole((count, features)),
                whole((count, 2 * rank)),
                pl.BlockSpec((2 * rank, features), lambda c, g: (g[0], 0)),
                pl.BlockSpec((rank, features), lambda c, g: (g[0], 0)),
                weights(0),
                weights(1),
                weights(2),
                pl.BlockSpec((1, 1, 3, 2 * rank, lanes), lambda c, g: (c, g[0], 0, 0, 0)),
            ]
            + ([] if fresh else [buffered_once(sums_shape, lambda c, g: (0, 0, g[0], 0)) if goes_on else anywhere])
            + ([whole((count, features))] if goes_on else []),
            out_specs=[
                pl.BlockSpec(sums_shape, lambda c, g: (0, 0, g[0], 0)),
                pl.BlockSpec((count, features), lambda c, g: (0, 0)),
                pl.BlockSpec((count, lanes), lambda c, g: (0, c)),
                pl.BlockSpec((count, rank), lambda c, g: (0, 0)),
            ],
            scratch_shapes=scratch,
        ),
        out_shape=[
            jax.ShapeDtypeStruct((rows, cols, groups * height, lanes), jnp.float32),
            jax.ShapeDtypeStruct((count, features), dtype),
            jax.ShapeDtypeStruct((count, cols * lanes), jnp.bfloat16),
            jax.ShapeDtypeStruct((count, rank), jnp.bfloat16),
        ],
        input_output_aliases={} if fresh else {10: 0},
        compiler_params=pltpu.CompilerParams(vmem_limit_bytes=60 * 2**20),
        cost_estimate=pl.CostEstimate(
            flops=10 * count * features * cols * lanes,
            bytes_accessed=6 * features * cols * lanes + 12 * count * features,
            transcendentals=count * cols * lanes,
        ),
        name="feed_forward",
    )(group, h, e, mask, first, second, weight, weight, weight, mids, *([] if fresh else [sums]), *([earlier] if goes_on else []))


def down_kernel(second_ref, hidden_ref, low_ref, weight_ref, *refs):
    kept_refs, out_ref = refs[:-1], refs[-1]
    cols, lanes = weight_ref.shape[0], weight_ref.shape[3]
    total = nn(low_ref[...], second_ref[...]) + nn(hidden_ref[...], weight_ref[:, 0].reshape(cols * lanes, lanes))
    for v in kept_refs:
        total += (v[0] if len(v.shape) == 3 else v[...]).astype(jnp.float32)
    out_ref[0] = total.astype(out_ref.dtype)


def project_down(second, hidden, low_down, weight, kept, dtype):
    count = hidden.shape[0]
    cols, rows, _, lanes = weight.shape
    rank = low_down.shape[1]
    whole = lambda v: buffered_once(v.shape, lambda r: (0, 0))
    by_block = pl.BlockSpec((1, count, lanes), lambda r: (r, 0, 0))
    return pl.pallas_call(
        down_kernel,
        grid=(rows,),
        in_specs=[
            pl.BlockSpec((rank, lanes), lambda r: (0, r)),
            whole(hidden),
            whole(low_down),
            pl.BlockSpec((cols, 1, lanes, lanes), lambda r: (0, r, 2, 0)),
        ]
        + [by_block if v.ndim == 3 else pl.BlockSpec((count, lanes), lambda r: (0, r)) for v in kept],
        out_specs=by_block,
        out_shape=jax.ShapeDtypeStruct((rows, count, lanes), dtype),
        compiler_params=pltpu.CompilerParams(vmem_limit_bytes=48 * 2**20),
        cost_estimate=pl.CostEstimate(
            flops=2 * count * rows * lanes * cols * lanes,
            bytes_accessed=2 * rows * lanes * cols * lanes + 8 * count * rows * lanes,
            transcendentals=0,
        ),
        name="project_down",
    )(second, hidden, low_down, weight, *kept)


def out_kernel(pairs, *refs):
    message_refs, refs = refs[:pairs], refs[pairs:]
    residual_ref, gain_ref, mask_ref, first_ref, second_ref, weight_ref, attended_ref, normed_ref, low_ref, heads_ref = refs
    r = pl.program_id(0)
    cols, lanes = weight_ref.shape[0], weight_ref.shape[3]

    @pl.when(r == 0)
    def _():
        seqs, _, units, part, width = message_refs[0].shape
        for s in range(seqs):
            for u in range(cols * units):
                for p in range(pairs):
                    begin = (u * pairs + p) * width
                    heads_ref[s * part : (s + 1) * part, begin : begin + width] = message_refs[p][s, u // units, u % units]
        low_ref[...] = (nt(heads_ref[...], first_ref[...]) * mask_ref[...]).astype(jnp.bfloat16)

    at = pl.ds(pl.multiple_of(r * lanes, lanes), lanes)
    attended_ref[:, at] = (
        residual_ref[...].astype(jnp.float32)
        + nn(heads_ref[...], weight_ref[:, 0].reshape(cols * lanes, lanes))
        + nn(low_ref[...], second_ref[0])
    )

    @pl.when(r == pl.num_programs(0) - 1)
    def _():
        normed_ref[...] = normalized(attended_ref[...], gain_ref[...])[1]


def project_out(messages, residual, gain, mask, first, second, weight):
    count, features = residual.shape
    cols, rows, lanes, _ = weight.shape
    rank = mask.shape[1]
    whole = lambda shape: pl.BlockSpec(shape, lambda r: (0,) * len(shape))
    return pl.pallas_call(
        functools.partial(out_kernel, len(messages)),
        grid=(rows,),
        in_specs=[buffered_once(m.shape, lambda r: (0,) * 5) for m in messages]
        + [
            pl.BlockSpec((count, lanes), lambda r: (0, r)),
            whole((1, features)),
            whole((count, rank)),
            whole(first.shape),
            pl.BlockSpec((1, rank, lanes), lambda r: (r, 0, 0)),
            pl.BlockSpec((cols, 1, lanes, lanes), lambda r: (0, r, 0, 0)),
        ],
        out_specs=[whole((count, features)), whole((count, features)), whole((count, rank))],
        out_shape=[
            jax.ShapeDtypeStruct((count, features), jnp.float32),
            jax.ShapeDtypeStruct((count, features), jnp.bfloat16),
            jax.ShapeDtypeStruct((count, rank), jnp.bfloat16),
        ],
        scratch_shapes=[pltpu.VMEM((count, cols * lanes), jnp.bfloat16)],
        compiler_params=pltpu.CompilerParams(vmem_limit_bytes=48 * 2**20),
        cost_estimate=pl.CostEstimate(
            flops=2 * count * features * cols * lanes,
            bytes_accessed=2 * features * cols * lanes + 10 * count * features,
            transcendentals=count,
        ),
        name="project_out",
    )(*messages, residual, gain, mask, first, second, weight)


def out_back_kernel(
    pairs, pair_width, own_ref, other_ref, upstream_ref, attended_ref, gain_ref, mask_ref, first_ref, second_ref, low_ref, weight_ref, *refs
):
    heads_refs, refs = refs[:pairs], refs[pairs:]
    attended_grad_ref, rows_ref, cols_ref, *refs = refs
    message_refs = refs[:pairs]
    e_ref, lowered_ref, lowered_turned_ref = refs[pairs:]
    c = pl.program_id(0)
    rows, lanes = weight_ref.shape[1], weight_ref.shape[3]
    seqs, _, units, part, _ = message_refs[0].shape

    @pl.when(c == 0)
    def _():
        values = attended_ref[...]
        inverse = lax.rsqrt(jnp.mean(values * values, axis=-1, keepdims=True) + EPS)
        upstream = own_ref[...] + other_ref[...].astype(jnp.float32)
        total = upstream_ref[...].astype(jnp.float32) + norm_back(values, inverse, gain_ref[...], upstream)
        attended_grad_ref[...] = total
        e = total.astype(jnp.bfloat16)
        e_ref[...] = e
        lowered = nt(e, second_ref[...]) * mask_ref[...]
        lowered_ref[...] = lowered.astype(jnp.bfloat16)
        lowered_turned_ref[...] = lowered.T.astype(jnp.bfloat16)
        turned = nn(low_ref[...].astype(jnp.float32).T.astype(jnp.bfloat16), e)
        for r in range(rows):
            rows_ref[r] = turned[:, r * lanes : (r + 1) * lanes].astype(rows_ref.dtype)

    grad = nn(lowered_ref[...], first_ref[...])
    for r in range(rows):
        grad += nt(e_ref[:, r * lanes : (r + 1) * lanes], weight_ref[0, r])
    grad = grad.astype(jnp.bfloat16)
    for s in range(seqs):
        for u in range(units):
            for p in range(pairs):
                begin = (u * pairs + p) * pair_width
                message_refs[p][s, 0, u] = grad[s * part : (s + 1) * part, begin : begin + pair_width]
    heads = [jnp.concatenate([h[s, 0, u] for s in range(seqs)], axis=0) for u in range(units) for h in heads_refs]
    cols_ref[0] = nn(lowered_turned_ref[...], jnp.concatenate(heads, axis=1)).astype(cols_ref.dtype)


def project_out_back(own, other, upstream, attended, gain, mask, first, second, heads, low_out, weight, seqs, units, pairs, pair_width):
    count, features = attended.shape
    cols, rows, lanes, _ = weight.shape
    rank = mask.shape[1]
    whole = lambda shape: buffered_once(shape, lambda c: (0,) * len(shape))
    message = (seqs, cols, units // (seqs * cols), count // seqs, pair_width)
    return pl.pallas_call(
        functools.partial(out_back_kernel, pairs, pair_width),
        grid=(cols,),
        in_specs=[whole((count, features))] * 4
        + [
            whole((1, features)),
            whole((count, rank)),
            pl.BlockSpec((rank, lanes), lambda c: (0, c)),
            whole((rank, features)),
            whole((count, rank)),
            pl.BlockSpec((1, rows, lanes, lanes), lambda c: (c, 0, 0, 0)),
        ]
        + [pl.BlockSpec((seqs, 1) + message[2:], lambda c: (0, c, 0, 0, 0))] * pairs,
        out_specs=[
            pl.BlockSpec((count, features), lambda c: (0, 0)),
            pl.BlockSpec((rows, rank, lanes), lambda c: (0, 0, 0)),
            pl.BlockSpec((1, rank, lanes), lambda c: (c, 0, 0)),
        ]
        + [pl.BlockSpec((seqs, 1) + message[2:], lambda c: (0, c, 0, 0, 0))] * pairs,
        out_shape=[
            jax.ShapeDtypeStruct((count, features), jnp.float32),
            jax.ShapeDtypeStruct((rows, rank, lanes), jnp.bfloat16),
            jax.ShapeDtypeStruct((cols, rank, lanes), jnp.bfloat16),
        ]
        + [jax.ShapeDtypeStruct(message, jnp.bfloat16)] * pairs,
        scratch_shapes=[
            pltpu.VMEM((count, features), jnp.bfloat16),
            pltpu.VMEM((count, rank), jnp.bfloat16),
            pltpu.VMEM((rank, count), jnp.bfloat16),
        ],
        compiler_params=pltpu.CompilerParams(vmem_limit_bytes=60 * 2**20),
        cost_estimate=pl.CostEstimate(
            flops=2 * count * features * cols * lanes,
            bytes_accessed=2 * features * cols * lanes + 18 * count * features,
            transcendentals=count,
        ),
        name="project_out_back",
    )(own, other, upstream, attended, gain, mask, first, second, low_out, weight, *heads)


def dot(left, right):
    return lax.dot_general(left, right, (((1,), (0,)), ((), ())), preferred_element_type=jnp.float32)


def over_tokens(left, right):
    return lax.dot_general(left, right, (((0,), (0,)), ((), ())), preferred_element_type=jnp.float32)


def low(values):
    return values.astype(jnp.bfloat16)


ordered = lax.optimization_barrier


def to_tokens(values):
    rows = lax.axis_size("row")
    part, seqs, features = values.shape
    cut = values.reshape(rows, part // rows, seqs, features).transpose(0, 2, 1, 3)
    moved = lax.all_to_all(cut, "row", 0, 0, tiled=True)
    return moved.transpose(1, 2, 0, 3).reshape(seqs * (part // rows), rows * features)


def send_features(*terms):
    rows = terms[0].shape[0]
    me = lax.axis_index("row")
    parts = []
    for step in range(rows):
        blocks = [lax.dynamic_index_in_dim(v, (me + step) % rows, 0, keepdims=False) for v in terms]
        block = low(sum(v.astype(jnp.float32) for v in blocks)) if len(blocks) > 1 else blocks[0]
        if step:
            block = lax.ppermute(block, "row", [(i, (i + step) % rows) for i in range(rows)])
        parts.append(block)
    return parts


def join_features(parts, seqs):
    rows, width = len(parts), parts[0].shape[1]
    me = lax.axis_index("row")
    stacked = jnp.stack(parts)
    moved = jnp.stack(
        [lax.dynamic_index_in_dim(stacked, (me - source) % rows, 0, keepdims=False) for source in range(rows)]
    ).reshape(rows, seqs, -1, width)
    return moved.transpose(0, 2, 1, 3).reshape(-1, seqs, width)


def rope_tables(positions):
    half = HEAD_DIM // 2
    frequency = ROPE_BASE ** (-(jnp.arange(half).astype(jnp.float32) * 2.0) / HEAD_DIM)
    angles = positions.astype(jnp.float32)[:, None] * frequency[None, :]
    return lax.optimization_barrier((jnp.cos(angles), jnp.sin(angles)))


def diagonal(blocks):
    total = sum(b.shape[1] for b in blocks)
    out, at = [], 0
    for b in blocks:
        out.append(jnp.pad(b, ((0, 0), (at, total - at - b.shape[1]))))
        at += b.shape[1]
    return jnp.concatenate(out, axis=0)


def local(
    tokens,
    cotangent,
    block_labels,
    adapter_selection,
    adapter_scale,
    attention_norm_gain,
    feedforward_norm_gain,
    query_weight,
    key_weight,
    value_weight,
    output_weight,
    gate_weight,
    up_weight,
    down_weight,
    query_first_factor,
    query_second_factor,
    key_first_factor,
    key_second_factor,
    value_first_factor,
    value_second_factor,
    output_first_factor,
    output_second_factor,
    gate_first_factor,
    gate_second_factor,
    up_first_factor,
    up_second_factor,
    down_first_factor,
    down_second_factor,
):
    copies, rows, cols = lax.axis_size("dp"), lax.axis_size("row"), lax.axis_size("col")
    me = lax.axis_index("dp")
    units = rows * cols
    both, turned_both = ("row", "col"), ("col", "row")
    seqs = tokens.shape[1]
    part = tokens.shape[0] // rows
    length = part * units
    lanes = tokens.shape[2]
    scale = adapter_scale[0]
    width_q, width_kv = query_weight.shape[1], key_weight.shape[1]
    width_ff = gate_weight.shape[1] // copies
    blocks_ff = width_ff // lanes
    kv_heads = width_kv // HEAD_DIM
    heads = width_q * cols // HEAD_DIM * seqs // units
    pairs = -(-heads // 2)
    pair_heads = heads // pairs
    pair_width = pair_heads * HEAD_DIM
    pair_pad = -pair_width % 128
    kv_copies = max(1, units // (seqs * kv_heads * cols))
    adapter_cols = query_first_factor.shape[1]
    rank = seqs * RANK
    factor = HEAD_DIM ** (-0.5)
    head_q = width_q // kv_heads

    picked = lax.all_gather(adapter_selection, "dp", axis=0, tiled=True)
    owner = jnp.arange(adapter_cols)
    slot = jnp.arange(copies * rank)
    choose = (owner[:, None] // RANK == picked[slot // RANK][None, :]) & (owner[:, None] % RANK == slot[None, :] % RANK)
    choose_low = choose.astype(jnp.bfloat16)
    choose_wide = choose.astype(jnp.float32)
    choose_own = lax.dynamic_slice_in_dim(choose_low, me * rank, rank, 1)

    def first_of(matrix, chosen):
        return low(lax.dot_general(chosen, matrix, (((0,), (1,)), ((), ())), preferred_element_type=jnp.float32))

    def second_of(matrix, chosen):
        return low(over_tokens(chosen, matrix))

    def pack(by_row, by_col):
        shares = []
        for group, count, at in zip((by_row, by_col), (cols, rows), ("col", "row")):
            if not group:
                shares.append(jnp.zeros((0, lanes), jnp.bfloat16))
                continue
            joined = jnp.concatenate([v.reshape(-1, lanes) for v in group], axis=0)
            joined = jnp.pad(joined, ((0, -joined.shape[0] % count), (0, 0)))
            piece = joined.shape[0] // count
            shares.append(lax.dynamic_slice_in_dim(joined, lax.axis_index(at) * piece, piece, 0))
        return jnp.concatenate(shares, axis=0), shares[0].shape[0]

    def unpack(moved, share, by_row, by_col):
        of_rows = moved[:, :, :share].transpose(1, 0, 2, 3).reshape(rows, -1, lanes)
        of_cols = moved[:, :, share:].reshape(cols, -1, lanes)
        outs = []
        for group, source in zip((by_row, by_col), (of_rows, of_cols)):
            at, out = 0, []
            for v in group:
                size = v.size // lanes
                out.append(source[:, at : at + size].reshape((source.shape[0],) + v.shape))
                at += size
            outs.append(out)
        return outs

    def joined_rows(values):
        return values.transpose(1, 0, 2).reshape(values.shape[1], -1)

    def by_head(query, key, value):
        parts = []
        for j in range(kv_heads):
            at = slice(j * HEAD_DIM, (j + 1) * HEAD_DIM)
            parts += [query[:, j * head_q : (j + 1) * head_q], key[:, at], value[:, at]]
        return jnp.concatenate(parts, axis=1)

    half = me * width_ff
    gate_half = lax.dynamic_slice_in_dim(gate_weight, half, width_ff, 1)
    up_half = lax.dynamic_slice_in_dim(up_weight, half, width_ff, 1)
    down_half = lax.dynamic_slice_in_dim(down_weight, half, width_ff, 0)
    gate_second_half = lax.dynamic_slice_in_dim(gate_second_factor, half, width_ff, 1)
    up_second_half = lax.dynamic_slice_in_dim(up_second_factor, half, width_ff, 1)
    down_first_half = lax.dynamic_slice_in_dim(down_first_factor, half, width_ff, 0)

    attn_weight = lax.all_gather(
        jnp.concatenate([output_weight, by_head(query_weight, key_weight, value_weight)], axis=1),
        turned_both,
        axis=0,
        tiled=True,
    ).reshape(cols, rows, lanes, -1)
    attn_small = (
        [
            jnp.concatenate([first_of(m, choose_own) for m in (query_first_factor, key_first_factor, value_first_factor)]),
            jnp.stack([attention_norm_gain, feedforward_norm_gain]),
            second_of(output_second_factor, choose_own),
        ],
        [
            second_of(query_second_factor, choose_own),
            second_of(key_second_factor, choose_own),
            second_of(value_second_factor, choose_own),
            first_of(output_first_factor, choose_own),
        ],
    )
    packed, share = pack(*attn_small)
    (qkv_first, gains, out_second), (query_second, key_second, value_second, out_first) = unpack(
        lax.all_gather(packed, turned_both).reshape(cols, rows, -1, lanes), share, *attn_small
    )
    qkv_first = joined_rows(qkv_first)
    gains = joined_rows(gains).astype(jnp.float32)
    out_first = joined_rows(out_first)
    nothing = lambda m: jnp.zeros_like(m)
    qkv_second = jnp.stack(
        [
            jnp.concatenate(
                [
                    by_head(query_second[c], nothing(key_second[c]), nothing(value_second[c])),
                    by_head(nothing(query_second[c]), key_second[c], nothing(value_second[c])),
                    by_head(nothing(query_second[c]), nothing(key_second[c]), value_second[c]),
                ],
                axis=0,
            )
            for c in range(cols)
        ]
    )

    first_parts = [first_of(m, choose_low) for m in (gate_first_factor, up_first_factor)]
    hidden_parts = [
        second_of(gate_second_half, choose_low),
        second_of(up_second_half, choose_low),
        first_of(down_first_half, choose_low),
    ]
    of_group = lambda values, g: values[g * rank : (g + 1) * rank]
    mlp_small = [
        jnp.concatenate([of_group(m, g) for g in range(copies) for m in first_parts]),
        second_of(down_second_factor, choose_low),
    ]

    def middle(n):
        at = slice(n * lanes, (n + 1) * lanes)
        return jnp.stack(
            [
                jnp.stack(
                    [
                        jnp.pad(of_group(m, g)[:, at], ((rank, 0), (0, 0)) if i == 1 else ((0, rank), (0, 0)))
                        for i, m in enumerate(hidden_parts)
                    ]
                )
                for g in range(copies)
            ]
        )

    packs = [pack(mlp_small if n == 0 else [], [middle(n)]) for n in range(blocks_ff)]
    mlp_shards = [
        jnp.concatenate(
            [
                gate_half[:, n * lanes : (n + 1) * lanes],
                up_half[:, n * lanes : (n + 1) * lanes],
                down_half[n * lanes : (n + 1) * lanes],
                packs[n][0],
            ],
            axis=0,
        )
        for n in range(blocks_ff)
    ]

    row_seq = jnp.arange(seqs * part) // part
    mask = (row_seq[:, None] == jnp.arange(rank)[None, :] // RANK).astype(jnp.float32) * scale
    mask_twice, mask_thrice = jnp.tile(mask, (1, 2)), jnp.tile(mask, (1, 3))

    positions = (lax.axis_index("col") * rows + lax.axis_index("row")) * part + jnp.arange(part)
    cosine, sine = rope_tables(jnp.tile(positions, seqs))
    flat, none = jnp.ones((seqs * part, HEAD_DIM), jnp.float32), jnp.zeros((seqs * part, HEAD_DIM), jnp.float32)
    turning = head_q // HEAD_DIM + 1
    cosine, sine = (
        jnp.tile(jnp.concatenate([jnp.tile(table, (1, 2 * turning)), rest], axis=1), (1, kv_heads))
        for table, rest in ((cosine, flat), (sine, none))
    )
    tokens, gains = ordered((tokens, gains))
    residual = to_tokens(tokens)
    cotangent, residual, mlp_shards, qkv_first, qkv_second, cosine, sine, mask_thrice, gains = ordered(
        (cotangent, residual, mlp_shards, qkv_first, qkv_second, cosine, sine, mask_thrice, gains)
    )
    upstream = to_tokens(cotangent)
    residual, upstream, mlp_shards[0] = ordered((residual, upstream, mlp_shards[0]))
    *messages, low_qkv = project_qkv(
        residual, gains[0:1], mask_thrice, qkv_first, qkv_second, cosine, sine, attn_weight, seqs, units, pairs, pair_width, kv_heads
    )

    def exchange(values):
        return lax.all_to_all(values.reshape(units, part, -1), turned_both, 0, 0, tiled=True)

    def to_messages(parts):
        return [v.reshape(seqs, cols, -1, part, pair_width) for v in parts]

    def padded(values):
        return jnp.pad(values, ((0, 0), (0, pair_pad)))

    first_in = exchange(messages[0]).reshape(length, -1)
    first_in, messages[1:], mlp_shards[1:] = ordered((first_in, messages[1:], mlp_shards[1:]))
    mlp_weights = [lax.all_gather(v, turned_both).reshape(cols, rows, -1, lanes) for v in mlp_shards]
    if pair_pad:
        unit_kv = (first_in[:, pair_width:], 0)
        unit_queries = [(padded(first_in[:, :pair_width]), 0)]
    else:
        unit_kv = (first_in, 1)
        unit_queries = [(first_in, 0)]
    unit_queries += [(padded(exchange(v).reshape(length, -1)), 0) for v in messages[1:]]
    unit_seq = (lax.axis_index("col") * rows + lax.axis_index("row")) * seqs // units
    labels = lax.dynamic_index_in_dim(block_labels, unit_seq, 0, keepdims=True)
    numbers = jnp.arange(BLOCKS)[:, None]
    ends_of = jnp.sum((labels <= numbers).astype(jnp.int32), axis=1, keepdims=True)
    ends = jnp.sum(jnp.where(labels == numbers, ends_of, 0), axis=0, keepdims=True)
    unit_outs, log_sums = [], []
    for p in range(pairs):
        out, log_sum = attend(unit_queries[p], unit_kv, ends, pair_heads, factor)
        unit_outs.append(out)
        log_sums.append(log_sum)
    heads_out = to_messages([exchange(v[:, :pair_width]) for v in unit_outs])
    unpacked = [
        unpack(mlp_weights[n][:, :, 3 * lanes :], packs[n][1], mlp_small if n == 0 else [], [middle(n)])
        for n in range(blocks_ff)
    ]
    front_first, down_second = (joined_rows(v) for v in unpacked[0][0])
    heads_out, front_first, down_second, unpacked[0][1][0] = ordered(
        (heads_out, front_first, down_second, unpacked[0][1][0])
    )
    attended, normed_mlp, low_out = project_out(
        heads_out, residual, gains[1:2], mask, out_first, out_second, attn_weight
    )

    def swap(values, step):
        return lax.ppermute(values, "dp", [(i, (i + step) % copies) for i in range(copies)])

    tokens_of = [(normed_mlp, upstream)]
    for step in range(1, copies):
        tokens_of.append((swap(normed_mlp, step), swap(upstream, step)))
    def second_of_group(step):
        return lax.dynamic_slice_in_dim(down_second, (me - step) % copies * rank, rank, 0)

    adapter_sums, grads, mixed = None, [None] * copies, [()] * copies
    for n in range(blocks_ff):
        last = n == blocks_ff - 1
        order = list(range(copies))
        hidden, low_down = [None] * copies, [None] * copies
        for step in order[1:] + order[:1] if last else order:
            adapter_sums, grads[step], hidden[step], low_down[step] = feed_forward(
                ((me - step) % copies).reshape(1),
                n,
                blocks_ff,
                *tokens_of[step],
                mask_twice,
                front_first,
                down_second,
                mlp_weights[n],
                unpacked[n][1][0],
                adapter_sums,
                grads[step],
                jnp.float32 if not last or step == 0 else jnp.bfloat16,
            )
        if not last:
            mixed = [
                (project_down(second_of_group(step), hidden[step], low_down[step], mlp_weights[n], mixed[step], jnp.float32),)
                for step in range(copies)
            ]
            mlp_weights[n + 1], mixed = ordered((mlp_weights[n + 1], mixed))
    grad_part = grads[0]
    for step in range(1, copies):
        grad_back = swap(grads[step], -step)
        grad_other = grad_back if step == 1 else grad_other + grad_back

    attended_grad, out_rows, out_cols, *grad_messages = project_out_back(
        grad_part,
        grad_other,
        upstream,
        attended,
        gains[1:2],
        mask,
        out_first,
        joined_rows(out_second),
        heads_out,
        low_out,
        attn_weight,
        seqs,
        units,
        pairs,
        pair_width,
    )
    shares = low(adapter_sums)
    row_share, col_share = 3 * rank // cols, 3 * rank // rows
    row_height, col_height = share_height(row_share), share_height(col_share)
    grad_messages, hidden = ordered((grad_messages, hidden))
    mixed_own, *mixed_others = [
        project_down(
            second_of_group(step),
            hidden[step],
            low_down[step],
            mlp_weights[-1],
            mixed[step] + (() if step else (attended,)),
            jnp.bfloat16 if step else jnp.float32,
        )
        for step in range(copies)
    ]
    unit_grads = [padded(exchange(grad_messages[0]).reshape(length, -1))]
    ends, mixed_own, mixed_others, shares, unit_grads[0] = ordered((ends, mixed_own, mixed_others, shares, unit_grads[0]))
    shares = lax.psum_scatter(shares.reshape(units, -1, lanes), both, scatter_dimension=0)
    mixed_backs = [swap(v, -step) for step, v in enumerate(mixed_others, 1)]
    unit_grads[0], grad_messages[1:] = ordered((unit_grads[0], grad_messages[1:]))
    unit_grads += [padded(exchange(v).reshape(length, -1)) for v in grad_messages[1:]]
    full_cosine, full_sine = (table.T for table in rope_tables(jnp.arange(length)))
    query_moved, kv_grad = [], None
    for p in range(pairs):
        last = p == pairs - 1
        if last:
            if p > 0:
                shares, mixed_backs, kv_grad = ordered((shares, mixed_backs, kv_grad))
            mixed_parts = send_features(mixed_own, *mixed_backs)
            shares = shares.reshape(copies, -1, lanes)
            parts = (
                shares[:, :row_share].reshape(-1, lanes),
                shares[:, row_height:].reshape(copies, blocks_ff, col_height, lanes)[:, :, :col_share].reshape(-1, lanes),
            )
            counts = [v.shape[0] for v in parts]
            parts = [jnp.pad(low(v), ((0, -v.shape[0] % GATHER_ROWS), (0, 0))) for v in parts]
            row_total = lax.all_gather(parts[0], ("dp", "col"))[..., : counts[0], :]
            col_total = lax.all_gather(parts[1], ("dp", "row"))[..., : counts[1], :]
        query_now, *kv_now = attend_back(
            unit_queries[p],
            unit_grads[p],
            unit_outs[p],
            log_sums[p],
            unit_kv,
            ends,
            full_cosine,
            full_sine,
            pair_heads,
            factor,
            kv_grad,
            last,
        )
        if last:
            query_now, mixed_parts, row_total, col_total, query_moved = ordered(
                (query_now, mixed_parts, row_total, col_total, query_moved)
            )
            if pair_pad:
                query_now = jnp.concatenate([query_now[:, :pair_width], query_now[:, -2 * HEAD_DIM :]], axis=1)
        else:
            kv_grad = kv_now[0]
            query_now = query_now[:, :pair_width]
        query_moved.append(exchange(query_now))
    mixed_out = join_features(mixed_parts, seqs)
    kv_moved = query_moved[-1][..., pair_width:].reshape(seqs, cols, kv_heads, kv_copies, part, -1)
    kv_moved = low(kv_moved.astype(jnp.float32).sum(axis=3)) if kv_copies > 1 else kv_moved[:, :, :, 0]
    query_moved[-1] = query_moved[-1][..., :pair_width]
    query_moved = to_messages(query_moved)
    lowered_qkv, qkv_rows, qkv_cols = qkv_grad_sums(
        residual, gains[0:1], mask_thrice, qkv_second, low_qkv, kv_moved, query_moved, rows
    )

    def everywhere(values, axes, count):
        copied = jnp.broadcast_to(values[None], (count,) + values.shape)
        return lax.all_to_all(copied, axes, 0, 0, tiled=True).reshape(copies, -1, lanes)

    def wide_second(values):
        return lax.dot_general(
            choose_wide, values, (((1,), (0,)), ((), ())), precision=lax.Precision.HIGHEST, preferred_element_type=jnp.float32
        )

    def wide_first(values):
        return lax.dot_general(
            values, choose_wide, (((0,), (1,)), ((), ())), precision=lax.Precision.HIGHEST, preferred_element_type=jnp.float32
        )

    row_total = row_total.astype(jnp.float32).reshape(copies, cols, copies, row_share, lanes).sum(axis=0)
    row_total = row_total.transpose(1, 0, 2, 3).reshape(copies, 3, rank, lanes)
    gate_first_gradient, up_first_gradient = (wide_first(row_total[:, i].reshape(-1, lanes)) for i in range(2))
    down_second_gradient = wide_second(row_total[:, 2].reshape(-1, lanes))
    col_total = col_total.astype(jnp.float32).reshape(copies, rows, copies, blocks_ff, col_share, lanes)
    col_total = col_total.transpose(0, 2, 3, 1, 4, 5).reshape(copies, copies, blocks_ff, 3, rank, lanes)
    pieces = [
        [col_total[x, :, n, i].reshape(-1, lanes) for x in range(copies) for n in range(blocks_ff)] for i in range(3)
    ]
    gate_second_gradient, up_second_gradient = (
        jnp.concatenate([wide_second(v) for v in pieces[i]], axis=1) for i in range(2)
    )
    down_first_gradient = jnp.concatenate([wide_first(v) for v in pieces[2]], axis=0)

    row_cut = jnp.concatenate([qkv_rows, out_rows], axis=1).reshape(rows, cols, -1, lanes)
    col_cut = jnp.concatenate([qkv_cols.reshape(cols, -1, lanes), out_cols], axis=1)
    col_cut = col_cut.reshape(cols, rows, -1, lanes).transpose(1, 0, 2, 3)
    cut = row_cut.shape[2]
    attn_shares = jnp.concatenate([row_cut, col_cut], axis=2).reshape(units, -1, lanes)
    attn_shares, lowered_qkv = ordered((attn_shares, lowered_qkv))
    token_grad = project_qkv_back(
        residual, attended_grad, gains[0:1], qkv_first, lowered_qkv, kv_moved, query_moved, attn_weight
    )
    attn_sums = jnp.sum(lax.all_to_all(attn_shares, both, 0, 0, tiled=True).astype(jnp.float32), axis=0)
    token_parts = send_features(token_grad)
    attn_rows, token_parts[0] = ordered((attn_sums[:cut], token_parts[0]))
    attn_rows = everywhere(attn_rows, ("dp", "col"), copies * cols)
    attn_cols, attn_rows = ordered((attn_sums[cut:], attn_rows))
    attn_rows = attn_rows.reshape(copies, 4, rank, lanes)
    attn_cols = everywhere(attn_cols, ("dp", "row"), copies * rows)
    query_first_gradient, key_first_gradient, value_first_gradient = (
        wide_first(attn_rows[:, i].reshape(-1, lanes)) for i in range(3)
    )
    output_second_gradient = wide_second(attn_rows[:, 3].reshape(-1, lanes))
    output_first_gradient = wide_first(attn_cols[:, -rank:].reshape(-1, lanes))
    qkv_second_gradient = wide_second(attn_cols[:, :-rank].reshape(copies * rank, -1)).reshape(
        adapter_cols, kv_heads, -1
    )
    query_second_gradient = qkv_second_gradient[..., :head_q].reshape(adapter_cols, -1)
    key_second_gradient = qkv_second_gradient[..., head_q : head_q + HEAD_DIM].reshape(adapter_cols, -1)
    value_second_gradient = qkv_second_gradient[..., head_q + HEAD_DIM :].reshape(adapter_cols, -1)

    return (
        mixed_out,
        join_features(token_parts, seqs),
        query_first_gradient,
        query_second_gradient,
        key_first_gradient,
        key_second_gradient,
        value_first_gradient,
        value_second_gradient,
        output_first_gradient,
        output_second_gradient,
        gate_first_gradient,
        gate_second_gradient,
        up_first_gradient,
        up_second_gradient,
        down_first_gradient,
        down_second_gradient,
    )


def solution(mesh):
    in_specs = (
        P("col", "dp", "row"),
        P("col", "dp", "row"),
        P("dp", None),
        P("dp"),
        P(),
        P("row"),
        P("row"),
        P("row", "col"),
        P("row", "col"),
        P("row", "col"),
        P("col", "row"),
        P("row", "col"),
        P("row", "col"),
        P("col", "row"),
        P("row", None),
        P(None, "col"),
        P("row", None),
        P(None, "col"),
        P("row", None),
        P(None, "col"),
        P("col", None),
        P(None, "row"),
        P("row", None),
        P(None, "col"),
        P("row", None),
        P(None, "col"),
        P("col", None),
        P(None, "row"),
    )
    out_specs = (
        P("col", "dp", "row"),
        P("col", "dp", "row"),
        P("row", None),
        P(None, "col"),
        P("row", None),
        P(None, "col"),
        P("row", None),
        P(None, "col"),
        P("col", None),
        P(None, "row"),
        P("row", None),
        P(None, "col"),
        P("row", None),
        P(None, "col"),
        P("col", None),
        P(None, "row"),
    )
    return jax.shard_map(local, mesh=mesh, in_specs=in_specs, out_specs=out_specs, check_vma=False)
```

```python
import functools, math
import jax, jax.numpy as jnp
from jax import lax
from jax.sharding import PartitionSpec as P
from jax.experimental import pallas as pl
from jax.experimental.pallas import tpu as pltpu

HEAD_DIM = 64
RANK = 16
BLOCKS = 32
EPS = 1e-05
ROPE_BASE = 500000.0
GATHER_ROWS = 128
TILE = 512
REACH = 256
LOG2E = math.log2(math.e)
NEG = -1e30


def nt(a, b):
    return lax.dot_general(a, b, (((1,), (1,)), ((), ())), preferred_element_type=jnp.float32)


def nn(a, b):
    return lax.dot_general(a, b, (((1,), (0,)), ((), ())), preferred_element_type=jnp.float32)


def half_of(x, e):
    lane = lax.broadcasted_iota(jnp.int32, x.shape, 1)
    return jnp.where((lane < 64) if e == 0 else (lane >= 64), x, jnp.zeros_like(x))


def doubled(kv):
    wide = kv.astype(jnp.float32)
    turned = pltpu.roll(wide, 64, 1)
    lane = lax.broadcasted_iota(jnp.int32, wide.shape, 1)
    return jnp.where(lane < 64, wide, turned).astype(jnp.bfloat16), jnp.where(lane < 64, turned, wide).astype(jnp.bfloat16)


def fwd_kernel(heads, factor, end_ref, q_ref, kv_ref, o_ref, lse_ref, acc_ref, m_ref, l_ref, k2_ref, vt_ref):
    i = pl.program_id(0)
    tq = q_ref.shape[0]
    q0 = i * tq
    c = factor * LOG2E

    @pl.when(i == 0)
    def _():
        for t in range(kv_ref.shape[0] // tq):
            rows = slice(t * tq, (t + 1) * tq)
            k2_ref[rows, :] = doubled(kv_ref[rows, :])[0]
            vt_ref[:, rows] = kv_ref[rows, :].astype(jnp.float32).T[64:, :].astype(jnp.bfloat16)

    ends = end_ref[...]
    m_ref[...] = jnp.full_like(m_ref, NEG)
    l_ref[...] = jnp.zeros_like(l_ref)
    acc_ref[...] = jnp.zeros_like(acc_ref)

    def tile(k0, size, masked):
        kk = k2_ref[pl.ds(k0, size), :]
        vv = vt_ref[:, pl.ds(k0, size)]
        if masked:
            allowed = (lax.broadcasted_iota(jnp.int32, (size, tq), 0) + k0) < ends
        for h in range(heads):
            qh = half_of(q_ref[:, (h // 2) * 128:(h // 2 + 1) * 128], h % 2)
            s = nt(kk, qh) * c
            if masked:
                s = jnp.where(allowed, s, NEG)
            m_old = m_ref[h:h + 1, :]
            m_new = jnp.maximum(m_old, jnp.max(s, axis=0, keepdims=True))
            p = jnp.exp2(s - m_new)
            alpha = jnp.exp2(m_old - m_new)
            l_ref[h:h + 1, :] = l_ref[h:h + 1, :] * alpha + jnp.sum(p, axis=0, keepdims=True)
            m_ref[h:h + 1, :] = m_new
            a = pl.ds(h * 64, 64)
            acc_ref[a, :] = acc_ref[a, :] * alpha + nn(vv, p.astype(jnp.bfloat16))

    def body(j, _):
        tile(pl.multiple_of(j * 2 * tq, tq), 2 * tq, False)
        return 0

    lax.fori_loop(0, i // 2, body, 0)
    last = pl.num_programs(0) - 1

    for odd in (False, True):
        for reach in (REACH, 0):

            @pl.when((i % 2 == int(odd)) & ((i < last) if reach else (i == last)))
            def _():
                before = tq if odd else 0
                tile(pl.multiple_of(q0 - before, tq), before + tq + reach, True)

    lse_ref[...] = m_ref[...] + jnp.log2(l_ref[...])
    inv = 1.0 / l_ref[...]
    for p in range(o_ref.shape[1] // 128):
        parts = []
        for h in (2 * p, 2 * p + 1):
            if h < heads:
                parts.append(acc_ref[h * 64:(h + 1) * 64, :] * inv[h:h + 1, :])
            else:
                parts.append(jnp.zeros((64, tq), jnp.float32))
        o_ref[:, p * 128:(p + 1) * 128] = jnp.concatenate(parts, axis=0).T.astype(o_ref.dtype)


def attend(q, kv, ends, heads, factor):
    (q, q_at), (kv, kv_at) = q, kv
    length, width = q.shape[0], 128
    tq = min(TILE, length)
    rows = 8
    return pl.pallas_call(
        functools.partial(fwd_kernel, heads, factor),
        grid=(length // tq,),
        in_specs=[
            pl.BlockSpec((1, tq), lambda i: (0, i)),
            pl.BlockSpec((tq, width), lambda i: (i, q_at)),
            pl.BlockSpec((length, 128), lambda i: (0, kv_at)),
        ],
        out_specs=[
            pl.BlockSpec((tq, width), lambda i: (i, 0)),
            pl.BlockSpec((rows, tq), lambda i: (0, i)),
        ],
        out_shape=[
            jax.ShapeDtypeStruct((length, width), jnp.bfloat16),
            jax.ShapeDtypeStruct((rows, length), jnp.float32),
        ],
        scratch_shapes=[
            pltpu.VMEM((heads * 64, tq), jnp.float32),
            pltpu.VMEM((rows, tq), jnp.float32),
            pltpu.VMEM((rows, tq), jnp.float32),
            pltpu.VMEM((length, 128), jnp.bfloat16),
            pltpu.VMEM((64, length), jnp.bfloat16),
        ],
        compiler_params=pltpu.CompilerParams(vmem_limit_bytes=48 * 2**20),
        cost_estimate=pl.CostEstimate(
            flops=2 * heads * length * length * 64, bytes_accessed=4 * length * width + length * 384, transcendentals=heads * length * length // 2
        ),
        name="attend_forward",
    )(ends, q, kv)


def turn_back(values, cosine, sine):
    high, rest = values[:32, :], values[32:, :]
    return jnp.concatenate([high * cosine + rest * sine, rest * cosine - high * sine], axis=0)


def bwd_kernel(heads, factor, last, end_ref, cos_ref, sin_ref, q_ref, do_ref, o_ref, lse_ref, kv_ref, *refs):
    if last:
        earlier_ref, dq_ref, *refs = refs
    else:
        dq_ref, dkv_ref, *refs = refs
    dqt_ref, delta_ref, dk_ref, dv_ref, k2_ref, v2_ref, kt_ref = refs
    j = pl.program_id(0)
    n = pl.num_programs(0)
    tk = kv_ref.shape[0]
    length, width = q_ref.shape
    c = factor * LOG2E
    k2_ref[...], v2_ref[...] = doubled(kv_ref[...])
    kt_ref[...] = kv_ref[...].astype(jnp.float32).T[:64, :].astype(jnp.bfloat16)

    @pl.when(j == 0)
    def _():
        dqt_ref[...] = jnp.zeros_like(dqt_ref)
        delta_ref[...] = jnp.zeros_like(delta_ref)
        for t in range(length // tk):
            rows = slice(t * tk, (t + 1) * tk)
            for p in range(width // 128):
                prod = do_ref[rows, p * 128:(p + 1) * 128].astype(jnp.float32) * o_ref[rows, p * 128:(p + 1) * 128].astype(jnp.float32)
                turned = prod.T
                for h in (2 * p, 2 * p + 1):
                    if h < heads:
                        delta_ref[h:h + 1, rows] = jnp.sum(turned[(h % 2) * 64:(h % 2 + 1) * 64, :], axis=0, keepdims=True)

    dk_ref[...] = jnp.zeros_like(dk_ref)
    dv_ref[...] = jnp.zeros_like(dv_ref)

    def tile(q0, count, size, masked):
        rows = pl.ds(q0, count)
        kk = k2_ref[:size, :]
        vv = v2_ref[:size, :]
        kt = kt_ref[:, :size]
        if masked:
            allowed = (lax.broadcasted_iota(jnp.int32, (size, count), 0) + j * tk) < end_ref[:, rows]
        for h in range(heads):
            lanes = slice((h // 2) * 128, (h // 2 + 1) * 128)
            qh = half_of(q_ref[rows, lanes], h % 2)
            gh = half_of(do_ref[rows, lanes], h % 2)
            s = nt(kk, qh) * c - lse_ref[h:h + 1, rows]
            if masked:
                s = jnp.where(allowed, s, NEG)
            p = jnp.exp2(s)
            dp = nt(vv, gh)
            ds = (p * (dp - delta_ref[h:h + 1, rows])).astype(jnp.bfloat16)
            dv_ref[:size, :] += nn(p.astype(jnp.bfloat16), gh)
            dk_ref[:size, :] += nn(ds, qh)
            dqt_ref[h * 64:(h + 1) * 64, rows] += nn(kt, ds)

    @pl.when(j > 0)
    def _():
        tile(pl.multiple_of((j - 1) * tk, tk), tk, REACH, True)

    rest = n - 1 - j
    for odd in (False, True):

        @pl.when(rest % 2 == int(odd))
        def _():
            tile(pl.multiple_of(j * tk, tk), 2 * tk if odd else tk, tk, True)

    def body(i, _):
        tile(pl.multiple_of((j + 1 + rest % 2 + 2 * i) * tk, tk), 2 * tk, tk, False)
        return 0

    lax.fori_loop(0, rest // 2, body, 0)

    own = pl.ds(pl.multiple_of(j * tk, tk), tk)
    dk = dk_ref[...].T
    dv = dv_ref[...].T
    dk = turn_back(dk[:64] + dk[64:], cos_ref[:, own], sin_ref[:, own]) * factor
    dkv = jnp.concatenate([dk, dv[:64] + dv[64:]], axis=0).T
    if last:
        dq_ref[own, width:] = (dkv if earlier_ref is None else dkv + earlier_ref[...]).astype(dq_ref.dtype)
    else:
        dkv_ref[...] = dkv

    @pl.when(j == n - 1)
    def _():
        for t in range(length // tk):
            rows = slice(t * tk, (t + 1) * tk)
            for p in range(width // 128):
                parts = []
                for h in (2 * p, 2 * p + 1):
                    if h < heads:
                        parts.append(turn_back(dqt_ref[h * 64:(h + 1) * 64, rows], cos_ref[:, rows], sin_ref[:, rows]) * factor)
                    else:
                        parts.append(jnp.zeros((64, tk), jnp.float32))
                dq_ref[rows, p * 128:(p + 1) * 128] = jnp.concatenate(parts, axis=0).T.astype(dq_ref.dtype)


def attend_back(q, do, o, lse, kv, ends, cosine, sine, heads, factor, earlier=None, last=True):
    (q, q_at), (kv, kv_at) = q, kv
    length, width = o.shape
    tk = min(TILE, length)
    whole = lambda shape, at=0: pl.BlockSpec(shape, lambda j: (0, at))
    by_block = lambda at=0: pl.BlockSpec((tk, 128), lambda j: (j, at))
    if last and earlier is None:
        earlier = jnp.zeros((length, 128), jnp.float32)
    return pl.pallas_call(
        functools.partial(bwd_kernel, heads, factor, last),
        grid=(length // tk,),
        in_specs=[
            whole((1, length)),
            whole((32, length)),
            whole((32, length)),
            whole((length, width), q_at),
            whole((length, width)),
            whole((length, width)),
            whole((8, length)),
            by_block(kv_at),
        ]
        + ([by_block()] if last else []),
        out_specs=[whole((length, width + 128))] if last else [whole((length, width)), by_block()],
        out_shape=[jax.ShapeDtypeStruct((length, width + 128), jnp.bfloat16)]
        if last
        else [jax.ShapeDtypeStruct((length, width), jnp.bfloat16), jax.ShapeDtypeStruct((length, 128), jnp.float32)],
        scratch_shapes=[
            pltpu.VMEM((heads * 64, length), jnp.float32),
            pltpu.VMEM((8, length), jnp.float32),
            pltpu.VMEM((tk, 128), jnp.float32),
            pltpu.VMEM((tk, 128), jnp.float32),
            pltpu.VMEM((tk, 128), jnp.bfloat16),
            pltpu.VMEM((tk, 128), jnp.bfloat16),
            pltpu.VMEM((64, tk), jnp.bfloat16),
        ],
        compiler_params=pltpu.CompilerParams(vmem_limit_bytes=48 * 2**20),
        cost_estimate=pl.CostEstimate(
            flops=5 * heads * length * length * 64,
            bytes_accessed=8 * length * width + length * 512,
            transcendentals=heads * length * length // 2,
        ),
        name="attend_backward",
    )(ends, cosine, sine, q, do, o, lse, kv, *([earlier] if last else []))


def buffered_once(shape, index_map):
    return pl.BlockSpec(shape, index_map, pipeline_mode=pl.Buffered(1))


def normalized(values, gain):
    inverse = lax.rsqrt(jnp.mean(values * values, axis=-1, keepdims=True) + EPS)
    return inverse, (values * inverse * gain).astype(jnp.bfloat16)


def norm_back(values, inverse, gain, upstream):
    scaled = upstream * gain
    weighted = jnp.mean(scaled * values, axis=-1, keepdims=True)
    return inverse * scaled - values * (inverse * inverse * inverse * weighted)


def qkv_kernel(pairs, kv_heads, token_ref, gain_ref, mask_ref, first_ref, second_ref, cos_ref, sin_ref, *refs):
    weight_refs, refs = refs[:3], refs[3:]
    message_refs, low_ref, normed_ref = refs[:pairs], refs[pairs], refs[pairs + 1]
    rows, lanes, chunk = weight_refs[0].shape[1:]
    count = token_ref.shape[0]
    seqs, _, units, part, _ = message_refs[0].shape
    pair_width = message_refs[0].shape[4] - 2 * HEAD_DIM

    @pl.when(pl.program_id(0) == 0)
    def _():
        _, normed = normalized(token_ref[...].astype(jnp.float32), gain_ref[...])
        normed_ref[...] = normed
        low_ref[...] = (nt(normed, first_ref[...]) * mask_ref[...]).astype(jnp.bfloat16)

    raw = jnp.concatenate(
        [nn(normed_ref[...], w[0].reshape(rows * lanes, chunk)) for w in weight_refs], axis=1
    ) + nn(low_ref[...], second_ref[0])
    width = raw.shape[1]
    lane = lax.broadcasted_iota(jnp.int32, raw.shape, 1)
    turned = jnp.where(lane % HEAD_DIM < HEAD_DIM // 2, -pltpu.roll(raw, width - HEAD_DIM // 2, 1), pltpu.roll(raw, HEAD_DIM // 2, 1))
    out = (raw * cos_ref[...] + turned * sin_ref[...]).astype(jnp.bfloat16)
    head_width = width // kv_heads
    for s in range(seqs):
        at = slice(s * part, (s + 1) * part)
        for u in range(units):
            base = u * kv_heads // units * head_width
            inside = u % (units // kv_heads) * pairs * pair_width
            kv = out[at, base + head_width - 2 * HEAD_DIM : base + head_width]
            for p in range(pairs):
                begin = base + inside + p * pair_width
                queries = out[at, begin : begin + pair_width]
                message_refs[p][s, 0, u] = jnp.concatenate([queries, kv], axis=1) if p == 0 else queries


def project_qkv(tokens, gain, mask, first, second, cosine, sine, weight, seqs, units, pairs, pair_width, kv_heads):
    count, features = tokens.shape
    cols, rows, lanes, _ = weight.shape
    width = second.shape[2]
    chunk = width // 3
    part = count // seqs
    whole = lambda shape: pl.BlockSpec(shape, lambda c: (0,) * len(shape))
    message = lambda wide: (seqs, cols, units // (seqs * cols), part, wide)
    widths = [pair_width + 2 * HEAD_DIM] + [pair_width] * (pairs - 1)
    block = lambda wide: pl.BlockSpec((seqs, 1) + message(wide)[2:], lambda c: (0, c, 0, 0, 0))
    weights = lambda at: pl.BlockSpec((1, rows, lanes, chunk), lambda c: (c, 0, 0, at))
    return pl.pallas_call(
        functools.partial(qkv_kernel, pairs, kv_heads),
        grid=(cols,),
        in_specs=[
            whole((count, features)),
            whole((1, features)),
            whole(mask.shape),
            whole(first.shape),
            pl.BlockSpec((1,) + second.shape[1:], lambda c: (c, 0, 0)),
            whole((count, width)),
            whole((count, width)),
            weights(0),
            weights(1),
            weights(2),
        ],
        out_specs=[block(w) for w in widths] + [whole(mask.shape)],
        out_shape=[jax.ShapeDtypeStruct(message(w), jnp.bfloat16) for w in widths]
        + [jax.ShapeDtypeStruct(mask.shape, jnp.bfloat16)],
        scratch_shapes=[pltpu.VMEM((count, features), jnp.bfloat16)],
        compiler_params=pltpu.CompilerParams(vmem_limit_bytes=48 * 2**20),
        cost_estimate=pl.CostEstimate(
            flops=2 * count * features * cols * width,
            bytes_accessed=2 * features * cols * width + 4 * count * features,
            transcendentals=count,
        ),
        name="project_qkv",
    )(tokens, gain, mask, first, second, cosine, sine, weight, weight, weight)


def lanes_of_unit(values, at, wide):
    return pl.BlockSpec((values.shape[0], 1) + values.shape[2:4] + (wide,), lambda c: (0, c, 0, 0, at))


def joined_messages(query_refs, kv_ref):
    seqs, _, kv_heads = kv_ref.shape[:3]
    units = query_refs[0].shape[2]
    parts = []
    for j in range(kv_heads):
        for u in range(j * units // kv_heads, (j + 1) * units // kv_heads):
            parts += [jnp.concatenate([q[s, 0, u] for s in range(seqs)], axis=0) for q in query_refs]
        parts.append(jnp.concatenate([kv_ref[s, 0, j] for s in range(seqs)], axis=0))
    return jnp.concatenate(parts, axis=1)


def qkv_sums_kernel(token_ref, gain_ref, mask_ref, second_ref, low_ref, kv_ref, *refs):
    query_refs, refs = refs[:-5], refs[-5:]
    lowered_out_ref, rows_ref, cols_ref, lowered_ref, low_turned_ref = refs
    c = pl.program_id(0)
    rows, _, lanes = rows_ref.shape
    kv_heads = kv_ref.shape[2]
    rank = mask_ref.shape[1] // 3

    @pl.when(c == 0)
    def _():
        lowered_ref[...] = jnp.zeros_like(lowered_ref)
        low_turned_ref[...] = low_ref[...].astype(jnp.float32).T.astype(jnp.bfloat16)

    e = joined_messages(query_refs, kv_ref)
    lowered_ref[...] += nt(e, second_ref[0])
    sums = nn(low_turned_ref[...], e)
    lane = lax.broadcasted_iota(jnp.int32, (rank, sums.shape[1]), 1) % (sums.shape[1] // kv_heads)
    query_lanes = sums.shape[1] // kv_heads - 2 * HEAD_DIM
    cols_ref[0] = jnp.where(
        lane < query_lanes,
        sums[:rank],
        jnp.where(lane < query_lanes + HEAD_DIM, sums[rank : 2 * rank], sums[2 * rank :]),
    ).astype(cols_ref.dtype)

    @pl.when(c == pl.num_programs(0) - 1)
    def _():
        lowered = lowered_ref[...] * mask_ref[...]
        lowered_out_ref[...] = lowered.astype(jnp.bfloat16)
        _, normed = normalized(token_ref[...].astype(jnp.float32), gain_ref[...])
        turned = nn(lowered.T.astype(jnp.bfloat16), normed)
        for r in range(rows):
            rows_ref[r] = turned[:, r * lanes : (r + 1) * lanes].astype(rows_ref.dtype)


def qkv_grad_sums(tokens, gain, mask, second, low_qkv, kv, queries, rows):
    count, features = tokens.shape
    cols, _, width = second.shape
    rank = mask.shape[1] // 3
    lanes = features // rows
    whole = lambda shape: buffered_once(shape, lambda c: (0,) * len(shape))
    return pl.pallas_call(
        qkv_sums_kernel,
        grid=(cols,),
        in_specs=[
            whole((count, features)),
            whole((1, features)),
            whole(mask.shape),
            pl.BlockSpec((1,) + second.shape[1:], lambda c: (c, 0, 0)),
            whole(low_qkv.shape),
            lanes_of_unit(*kv),
        ]
        + [lanes_of_unit(*q) for q in queries],
        out_specs=[
            pl.BlockSpec(mask.shape, lambda c: (0, 0)),
            pl.BlockSpec((rows, 3 * rank, lanes), lambda c: (0, 0, 0)),
            pl.BlockSpec((1, rank, width), lambda c: (c, 0, 0)),
        ],
        out_shape=[
            jax.ShapeDtypeStruct(mask.shape, jnp.bfloat16),
            jax.ShapeDtypeStruct((rows, 3 * rank, lanes), jnp.bfloat16),
            jax.ShapeDtypeStruct((cols, rank, width), jnp.bfloat16),
        ],
        scratch_shapes=[
            pltpu.VMEM((count, 3 * rank), jnp.float32),
            pltpu.VMEM((3 * rank, count), jnp.bfloat16),
        ],
        compiler_params=pltpu.CompilerParams(vmem_limit_bytes=48 * 2**20),
        cost_estimate=pl.CostEstimate(
            flops=2 * count * features * cols * width,
            bytes_accessed=2 * count * cols * width + 2 * count * features,
            transcendentals=count,
        ),
        name="qkv_grad_sums",
    )(tokens, gain, mask, second, low_qkv, kv[0], *[q[0] for q in queries])


def qkv_back_kernel(token_ref, attended_ref, gain_ref, first_ref, lowered_ref, kv_ref, *refs):
    query_refs, refs = refs[:-5], refs[-5:]
    weight_refs, (out_ref, grad_ref) = refs[:3], refs[3:]
    c = pl.program_id(0)
    rows, lanes, chunk = weight_refs[0].shape[1:]

    @pl.when(c == 0)
    def _():
        grad_ref[...] = nn(lowered_ref[...], first_ref[...])

    e = joined_messages(query_refs, kv_ref)
    for r in range(rows):
        total = nt(e[:, :chunk], weight_refs[0][0, r])
        for i in (1, 2):
            total += nt(e[:, i * chunk : (i + 1) * chunk], weight_refs[i][0, r])
        grad_ref[:, r * lanes : (r + 1) * lanes] += total

    @pl.when(c == pl.num_programs(0) - 1)
    def _():
        values = token_ref[...].astype(jnp.float32)
        inverse = lax.rsqrt(jnp.mean(values * values, axis=-1, keepdims=True) + EPS)
        out = (attended_ref[...] + norm_back(values, inverse, gain_ref[...], grad_ref[...])).astype(jnp.bfloat16)
        for r in range(rows):
            out_ref[r] = out[:, r * lanes : (r + 1) * lanes]


def project_qkv_back(tokens, attended_grad, gain, first, lowered, kv, queries, weight, width):
    count, features = tokens.shape
    cols, rows, lanes, _ = weight.shape
    chunk = width // 3
    whole = lambda shape: buffered_once(shape, lambda c: (0,) * len(shape))
    weights = lambda at: pl.BlockSpec((1, rows, lanes, chunk), lambda c: (c, 0, 0, at))
    return pl.pallas_call(
        qkv_back_kernel,
        grid=(cols,),
        in_specs=[
            whole((count, features)),
            whole((count, features)),
            whole((1, features)),
            whole(first.shape),
            whole(lowered.shape),
            lanes_of_unit(*kv),
        ]
        + [lanes_of_unit(*q) for q in queries]
        + [weights(0), weights(1), weights(2)],
        out_specs=pl.BlockSpec((rows, count, lanes), lambda c: (0, 0, 0)),
        out_shape=jax.ShapeDtypeStruct((rows, count, lanes), jnp.bfloat16),
        scratch_shapes=[pltpu.VMEM((count, features), jnp.float32)],
        compiler_params=pltpu.CompilerParams(vmem_limit_bytes=60 * 2**20),
        cost_estimate=pl.CostEstimate(
            flops=8 * count * features * cols * width,
            bytes_accessed=2 * features * cols * width + 10 * count * features,
            transcendentals=count,
        ),
        name="project_qkv_back",
    )(tokens, attended_grad, gain, first, lowered, kv[0], *[q[0] for q in queries], weight, weight, weight)


def mlp_kernel(fresh, goes_on, block, group_ref, h_ref, e_ref, mask_ref, first_ref, second_ref, gate_ref, up_ref, down_ref, mids_ref, *refs):
    if goes_on:
        sums_in_ref, grad_in_ref = refs[:2]
        refs = refs[2:]
    elif not fresh:
        refs = refs[1:]
    sums_ref, grad_out_ref, hidden_ref, low_down_ref = refs[:4]
    low_refs, turned_refs, sum_refs = refs[4:7], refs[7:10], refs[10:13]
    grad_ref = refs[13] if len(refs) > 13 else grad_out_ref
    c = pl.program_id(0)
    rows, lanes = gate_ref.shape[1], gate_ref.shape[3]
    rank = second_ref.shape[0]

    @pl.when(c == 0)
    def _():
        low_front = nt(h_ref[...], first_ref[...])
        lows = low_front[:, :rank], low_front[:, rank:], nt(e_ref[...], second_ref[...])
        for low, low_ref, turned_ref, sum_ref in zip(lows, low_refs, turned_refs, sum_refs):
            low = low * mask_ref[...]
            low_ref[...] = low.astype(jnp.bfloat16)
            turned_ref[...] = low.T.astype(jnp.bfloat16)
            sum_ref[...] = jnp.zeros_like(sum_ref)
        if goes_on:
            grad_ref[...] = grad_in_ref[...]
            sums_ref[...] = sums_in_ref[...]
        else:
            grad_ref[...] = jnp.zeros_like(grad_ref)
            sums_ref[...] = jnp.zeros_like(sums_ref)

    h = h_ref[...]
    gate_second, up_second, down_first = mids_ref[0, 0, 0], mids_ref[0, 0, 1], mids_ref[0, 0, 2]
    gate = nn(h, gate_ref[0].reshape(rows * lanes, lanes)) + nn(low_refs[0][...], gate_second)
    up = nn(h, up_ref[0].reshape(rows * lanes, lanes)) + nn(low_refs[1][...], up_second)
    upstream = nn(low_refs[2][...], down_first)
    for r in range(rows):
        upstream += nt(e_ref[:, r * lanes : (r + 1) * lanes], down_ref[0, r])
    sigmoid = 1.0 / (1.0 + jnp.exp(-gate))
    swish = gate * sigmoid
    hidden = (swish * up).astype(jnp.bfloat16)
    gate_grad = (upstream * up * (sigmoid + swish * (1.0 - sigmoid))).astype(jnp.bfloat16)
    up_grad = (upstream * swish).astype(jnp.bfloat16)
    for r in range(rows):
        at = slice(r * lanes, (r + 1) * lanes)
        grad_ref[:, at] += nt(gate_grad, gate_ref[0, r]) + nt(up_grad, up_ref[0, r])
    hidden_ref[...] = hidden
    outs = gate_grad, up_grad, hidden
    for out, sum_ref, middle in zip(outs, sum_refs, (gate_second, up_second, down_first)):
        sum_ref[...] += nt(out, middle)
    col_sum = jnp.concatenate([nn(turned_ref[...], out) for turned_ref, out in zip(turned_refs, outs)], axis=0)
    row_share, col_share = 3 * rank // sums_ref.shape[1], 3 * rank // rows
    begin = share_height(row_share) + block * share_height(col_share)
    for r in range(rows):
        sums_ref[r, c, begin : begin + col_share] = col_sum[r * col_share : (r + 1) * col_share]

    @pl.when(c == pl.num_programs(0) - 1)
    def _():
        gate_now, up_now, down_now = (sum_ref[...] * mask_ref[...] for sum_ref in sum_refs)
        front_now = jnp.concatenate([gate_now, up_now], axis=1)
        total = grad_ref[...] + nn(front_now.astype(jnp.bfloat16), first_ref[...])
        grad_out_ref[...] = total.astype(grad_out_ref.dtype)
        low_down_ref[...] = down_now.astype(jnp.bfloat16)
        row_sum = jnp.concatenate(
            [nn(v.T.astype(jnp.bfloat16), w[...]) for v, w in ((front_now, h_ref), (down_now, e_ref))], axis=0
        )
        for r in range(rows):
            now = row_sum[:, r * lanes : (r + 1) * lanes]
            for to in range(sums_ref.shape[1]):
                sums_ref[r, to, :row_share] += now[to * row_share : (to + 1) * row_share]


def share_height(count):
    return -(-count // 8) * 8


def feed_forward(group, block, blocks, h, e, mask, first, second, weight, mids, sums, earlier, dtype):
    count, features = h.shape
    cols, rows, _, lanes = weight.shape
    rank = mids.shape[3]
    groups = mids.shape[1]
    goes_on = earlier is not None
    fresh = sums is None
    whole = lambda shape: buffered_once(shape, lambda c, g: (0,) * len(shape))
    weights = lambda at: pl.BlockSpec((1, rows, lanes, lanes), lambda c, g: (c, 0, at, 0))
    height = share_height(3 * rank // cols) + blocks * share_height(3 * rank // rows)
    sums_shape = (rows, cols, height, lanes)
    anywhere = pl.BlockSpec(memory_space=pl.ANY)
    scratch = [pltpu.VMEM((count, rank), jnp.bfloat16)] * 3
    scratch += [pltpu.VMEM((rank, count), jnp.bfloat16)] * 3
    scratch += [pltpu.VMEM((count, rank), jnp.float32)] * 3
    if dtype != jnp.float32:
        scratch += [pltpu.VMEM((count, features), jnp.float32)]
    return pl.pallas_call(
        functools.partial(mlp_kernel, fresh, goes_on, block),
        grid_spec=pltpu.PrefetchScalarGridSpec(
            num_scalar_prefetch=1,
            grid=(cols,),
            in_specs=[
                whole((count, features)),
                whole((count, features)),
                whole((count, rank)),
                pl.BlockSpec((2 * rank, features), lambda c, g: (g[0], 0)),
                pl.BlockSpec((rank, features), lambda c, g: (g[0], 0)),
                weights(0),
                weights(1),
                weights(2),
                pl.BlockSpec((1, 1, 3, rank, lanes), lambda c, g: (c, g[0], 0, 0, 0)),
            ]
            + ([] if fresh else [buffered_once(sums_shape, lambda c, g: (0, 0, g[0], 0)) if goes_on else anywhere])
            + ([whole((count, features))] if goes_on else []),
            out_specs=[
                pl.BlockSpec(sums_shape, lambda c, g: (0, 0, g[0], 0)),
                pl.BlockSpec((count, features), lambda c, g: (0, 0)),
                pl.BlockSpec((count, lanes), lambda c, g: (0, c)),
                pl.BlockSpec((count, rank), lambda c, g: (0, 0)),
            ],
            scratch_shapes=scratch,
        ),
        out_shape=[
            jax.ShapeDtypeStruct((rows, cols, groups * height, lanes), jnp.float32),
            jax.ShapeDtypeStruct((count, features), dtype),
            jax.ShapeDtypeStruct((count, cols * lanes), jnp.bfloat16),
            jax.ShapeDtypeStruct((count, rank), jnp.bfloat16),
        ],
        input_output_aliases={} if fresh else {10: 0},
        compiler_params=pltpu.CompilerParams(vmem_limit_bytes=60 * 2**20),
        cost_estimate=pl.CostEstimate(
            flops=10 * count * features * cols * lanes,
            bytes_accessed=6 * features * cols * lanes + 12 * count * features,
            transcendentals=count * cols * lanes,
        ),
        name="feed_forward",
    )(group, h, e, mask, first, second, weight, weight, weight, mids, *([] if fresh else [sums]), *([earlier] if goes_on else []))


def down_kernel(second_ref, hidden_ref, low_ref, weight_ref, *refs):
    kept_refs, out_ref = refs[:-1], refs[-1]
    cols, lanes = weight_ref.shape[0], weight_ref.shape[3]
    total = nn(low_ref[...], second_ref[...]) + nn(hidden_ref[...], weight_ref[:, 0].reshape(cols * lanes, lanes))
    for v in kept_refs:
        total += (v[0] if len(v.shape) == 3 else v[...]).astype(jnp.float32)
    out_ref[0] = total.astype(out_ref.dtype)


def project_down(second, hidden, low_down, weight, kept, dtype):
    count = hidden.shape[0]
    cols, rows, _, lanes = weight.shape
    rank = low_down.shape[1]
    whole = lambda v: buffered_once(v.shape, lambda r: (0, 0))
    by_block = pl.BlockSpec((1, count, lanes), lambda r: (r, 0, 0))
    return pl.pallas_call(
        down_kernel,
        grid=(rows,),
        in_specs=[
            pl.BlockSpec((rank, lanes), lambda r: (0, r)),
            whole(hidden),
            whole(low_down),
            pl.BlockSpec((cols, 1, lanes, lanes), lambda r: (0, r, 2, 0)),
        ]
        + [by_block if v.ndim == 3 else pl.BlockSpec((count, lanes), lambda r: (0, r)) for v in kept],
        out_specs=by_block,
        out_shape=jax.ShapeDtypeStruct((rows, count, lanes), dtype),
        compiler_params=pltpu.CompilerParams(vmem_limit_bytes=48 * 2**20),
        cost_estimate=pl.CostEstimate(
            flops=2 * count * rows * lanes * cols * lanes,
            bytes_accessed=2 * rows * lanes * cols * lanes + 8 * count * rows * lanes,
            transcendentals=0,
        ),
        name="project_down",
    )(second, hidden, low_down, weight, *kept)


def lanes_of_part(me_ref, step, copies, r, lanes):
    wide = lanes // copies
    return pl.ds(pl.multiple_of(r * lanes + (me_ref[0] + copies - step) % copies * wide, wide), wide)


def out_kernel(pairs, copies, me_ref, *refs):
    message_refs, refs = refs[:pairs], refs[pairs:]
    residual_ref, gain_ref, mask_ref, first_ref, second_ref = refs[:5]
    weight_refs, (attended_ref, normed_ref, low_ref, heads_ref) = refs[5 : 5 + copies], refs[5 + copies :]
    r = pl.program_id(0)
    cols, lanes = weight_refs[0].shape[0], weight_refs[0].shape[2]

    @pl.when(r == 0)
    def _():
        seqs, _, units, part, width = message_refs[0].shape
        for s in range(seqs):
            for u in range(cols * units):
                for p in range(pairs):
                    begin = (u * pairs + p) * width
                    heads_ref[s * part : (s + 1) * part, begin : begin + width] = message_refs[p][s, u // units, u % units]
        low_ref[...] = (nt(heads_ref[...], first_ref[...]) * mask_ref[...]).astype(jnp.bfloat16)

    for step, weight_ref in enumerate(weight_refs):
        at = lanes_of_part(me_ref, step, copies, r, lanes)
        attended_ref[:, at] = (
            residual_ref[:, at].astype(jnp.float32)
            + nn(heads_ref[...], weight_ref[:, 0].reshape(cols * lanes, lanes // copies))
            + nn(low_ref[...], second_ref[:, at])
        )

    @pl.when(r == pl.num_programs(0) - 1)
    def _():
        normed_ref[...] = normalized(attended_ref[...], gain_ref[...])[1]


def project_out(me, messages, residual, gain, mask, first, second, weights):
    count, features = residual.shape
    cols, rows, lanes, _ = weights[0][0].shape
    copies = len(weights)
    rank = mask.shape[1]
    whole = lambda shape: buffered_once(shape, lambda r, m: (0,) * len(shape))
    part = lambda at: pl.BlockSpec((cols, 1, lanes, lanes // copies), lambda r, m: (0, r, 0, at))
    outs = [(count, features), (count, features), (count, rank)]
    return pl.pallas_call(
        functools.partial(out_kernel, len(messages), copies),
        grid_spec=pltpu.PrefetchScalarGridSpec(
            num_scalar_prefetch=1,
            grid=(rows,),
            in_specs=[whole(m.shape) for m in messages]
            + [whole((count, features)), whole((1, features)), whole((count, rank)), whole(first.shape), whole(second.shape)]
            + [part(at) for _, at in weights],
            out_specs=[pl.BlockSpec(shape, lambda r, m: (0, 0)) for shape in outs],
            scratch_shapes=[pltpu.VMEM((count, cols * lanes), jnp.bfloat16)],
        ),
        out_shape=[jax.ShapeDtypeStruct(s, t) for s, t in zip(outs, (jnp.float32, jnp.bfloat16, jnp.bfloat16))],
        compiler_params=pltpu.CompilerParams(vmem_limit_bytes=48 * 2**20),
        cost_estimate=pl.CostEstimate(
            flops=2 * count * features * cols * lanes,
            bytes_accessed=2 * features * cols * lanes + 10 * count * features,
            transcendentals=count,
        ),
        name="project_out",
    )(me, *messages, residual, gain, mask, first, second, *[w for w, _ in weights])


def out_back_kernel(
    pairs, copies, pair_width, me_ref, own_ref, other_ref, upstream_ref, attended_ref, gain_ref, mask_ref, first_ref, second_ref, low_ref, *refs
):
    weight_refs, refs = refs[:copies], refs[copies:]
    heads_refs, refs = refs[:pairs], refs[pairs:]
    attended_grad_ref, rows_ref, cols_ref, *refs = refs
    message_refs = refs[:pairs]
    e_ref, lowered_ref, lowered_turned_ref = refs[pairs:]
    c = pl.program_id(0)
    rows, lanes = weight_refs[0].shape[1:3]
    seqs, _, units, part, _ = message_refs[0].shape

    @pl.when(c == 0)
    def _():
        values = attended_ref[...]
        inverse = lax.rsqrt(jnp.mean(values * values, axis=-1, keepdims=True) + EPS)
        upstream = own_ref[...] + other_ref[...].astype(jnp.float32)
        total = upstream_ref[...].astype(jnp.float32) + norm_back(values, inverse, gain_ref[...], upstream)
        attended_grad_ref[...] = total
        e = total.astype(jnp.bfloat16)
        e_ref[...] = e
        lowered = nt(e, second_ref[...]) * mask_ref[...]
        lowered_ref[...] = lowered.astype(jnp.bfloat16)
        lowered_turned_ref[...] = lowered.T.astype(jnp.bfloat16)
        turned = nn(low_ref[...].astype(jnp.float32).T.astype(jnp.bfloat16), e)
        for r in range(rows):
            rows_ref[r] = turned[:, r * lanes : (r + 1) * lanes].astype(rows_ref.dtype)

    grad = nn(lowered_ref[...], first_ref[...])
    for r in range(rows):
        for step, weight_ref in enumerate(weight_refs):
            grad += nt(e_ref[:, lanes_of_part(me_ref, step, copies, r, lanes)], weight_ref[0, r])
    grad = grad.astype(jnp.bfloat16)
    for s in range(seqs):
        for u in range(units):
            for p in range(pairs):
                begin = (u * pairs + p) * pair_width
                message_refs[p][s, 0, u] = grad[s * part : (s + 1) * part, begin : begin + pair_width]
    heads = [jnp.concatenate([h[s, 0, u] for s in range(seqs)], axis=0) for u in range(units) for h in heads_refs]
    cols_ref[0] = nn(lowered_turned_ref[...], jnp.concatenate(heads, axis=1)).astype(cols_ref.dtype)


def project_out_back(me, own, other, upstream, attended, gain, mask, first, second, heads, low_out, weights, seqs, units, pair_width):
    count, features = attended.shape
    cols, rows, lanes, _ = weights[0][0].shape
    copies, pairs = len(weights), len(heads)
    rank = mask.shape[1]
    whole = lambda shape: buffered_once(shape, lambda c, m: (0,) * len(shape))
    message = (seqs, cols, units // (seqs * cols), count // seqs, pair_width)
    by_unit = pl.BlockSpec((seqs, 1) + message[2:], lambda c, m: (0, c, 0, 0, 0))
    return pl.pallas_call(
        functools.partial(out_back_kernel, pairs, copies, pair_width),
        grid_spec=pltpu.PrefetchScalarGridSpec(
            num_scalar_prefetch=1,
            grid=(cols,),
            in_specs=[whole((count, features))] * 4
            + [
                whole((1, features)),
                whole((count, rank)),
                pl.BlockSpec((rank, lanes), lambda c, m: (0, c)),
                whole((rank, features)),
                whole((count, rank)),
            ]
            + [
                pl.BlockSpec((1, rows, lanes, lanes // copies), functools.partial(lambda at, c, m: (c, 0, 0, at), at))
                for _, at in weights
            ]
            + [by_unit] * pairs,
            out_specs=[
                pl.BlockSpec((count, features), lambda c, m: (0, 0)),
                pl.BlockSpec((rows, rank, lanes), lambda c, m: (0, 0, 0)),
                pl.BlockSpec((1, rank, lanes), lambda c, m: (c, 0, 0)),
            ]
            + [by_unit] * pairs,
            scratch_shapes=[
                pltpu.VMEM((count, features), jnp.bfloat16),
                pltpu.VMEM((count, rank), jnp.bfloat16),
                pltpu.VMEM((rank, count), jnp.bfloat16),
            ],
        ),
        out_shape=[
            jax.ShapeDtypeStruct((count, features), jnp.float32),
            jax.ShapeDtypeStruct((rows, rank, lanes), jnp.bfloat16),
            jax.ShapeDtypeStruct((cols, rank, lanes), jnp.bfloat16),
        ]
        + [jax.ShapeDtypeStruct(message, jnp.bfloat16)] * pairs,
        compiler_params=pltpu.CompilerParams(vmem_limit_bytes=60 * 2**20),
        cost_estimate=pl.CostEstimate(
            flops=2 * count * features * cols * lanes,
            bytes_accessed=2 * features * cols * lanes + 18 * count * features,
            transcendentals=count,
        ),
        name="project_out_back",
    )(me, own, other, upstream, attended, gain, mask, first, second, low_out, *[w for w, _ in weights], *heads)


def dot(left, right):
    return lax.dot_general(left, right, (((1,), (0,)), ((), ())), preferred_element_type=jnp.float32)


def over_tokens(left, right):
    return lax.dot_general(left, right, (((0,), (0,)), ((), ())), preferred_element_type=jnp.float32)


def low(values):
    return values.astype(jnp.bfloat16)


ordered = lax.optimization_barrier


def to_tokens(values):
    rows = lax.axis_size("row")
    part, seqs, features = values.shape
    cut = values.reshape(rows, part // rows, seqs, features).transpose(0, 2, 1, 3)
    moved = lax.all_to_all(cut, "row", 0, 0, tiled=True)
    return moved.transpose(1, 2, 0, 3).reshape(seqs * (part // rows), rows * features)


def send_features(*terms):
    rows = terms[0].shape[0]
    me = lax.axis_index("row")
    parts = []
    for step in range(rows):
        blocks = [lax.dynamic_index_in_dim(v, (me + step) % rows, 0, keepdims=False) for v in terms]
        block = low(sum(v.astype(jnp.float32) for v in blocks)) if len(blocks) > 1 else blocks[0]
        if step:
            block = lax.ppermute(block, "row", [(i, (i + step) % rows) for i in range(rows)])
        parts.append(block)
    return parts


def join_features(parts, seqs):
    rows, width = len(parts), parts[0].shape[1]
    me = lax.axis_index("row")
    stacked = jnp.stack(parts)
    moved = jnp.stack(
        [lax.dynamic_index_in_dim(stacked, (me - source) % rows, 0, keepdims=False) for source in range(rows)]
    ).reshape(rows, seqs, -1, width)
    return moved.transpose(0, 2, 1, 3).reshape(-1, seqs, width)


def rope_tables(positions):
    half = HEAD_DIM // 2
    frequency = ROPE_BASE ** (-(jnp.arange(half).astype(jnp.float32) * 2.0) / HEAD_DIM)
    angles = positions.astype(jnp.float32)[:, None] * frequency[None, :]
    return lax.optimization_barrier((jnp.cos(angles), jnp.sin(angles)))


def diagonal(blocks):
    total = sum(b.shape[1] for b in blocks)
    out, at = [], 0
    for b in blocks:
        out.append(jnp.pad(b, ((0, 0), (at, total - at - b.shape[1]))))
        at += b.shape[1]
    return jnp.concatenate(out, axis=0)


def local(
    tokens,
    cotangent,
    block_labels,
    adapter_selection,
    adapter_scale,
    attention_norm_gain,
    feedforward_norm_gain,
    query_weight,
    key_weight,
    value_weight,
    output_weight,
    gate_weight,
    up_weight,
    down_weight,
    query_first_factor,
    query_second_factor,
    key_first_factor,
    key_second_factor,
    value_first_factor,
    value_second_factor,
    output_first_factor,
    output_second_factor,
    gate_first_factor,
    gate_second_factor,
    up_first_factor,
    up_second_factor,
    down_first_factor,
    down_second_factor,
):
    copies, rows, cols = lax.axis_size("dp"), lax.axis_size("row"), lax.axis_size("col")
    me = lax.axis_index("dp")
    units = rows * cols
    both, turned_both = ("row", "col"), ("col", "row")
    seqs = tokens.shape[1]
    part = tokens.shape[0] // rows
    length = part * units
    lanes = tokens.shape[2]
    scale = adapter_scale[0]
    width_q, width_kv = query_weight.shape[1], key_weight.shape[1]
    width_ff = gate_weight.shape[1] // copies
    blocks_ff = width_ff // lanes
    kv_heads = width_kv // HEAD_DIM
    heads = width_q * cols // HEAD_DIM * seqs // units
    pairs = -(-heads // 2)
    pair_heads = heads // pairs
    pair_width = pair_heads * HEAD_DIM
    pair_pad = -pair_width % 128
    kv_copies = max(1, units // (seqs * kv_heads * cols))
    adapter_cols = query_first_factor.shape[1]
    rank = seqs * RANK
    factor = HEAD_DIM ** (-0.5)
    head_q = width_q // kv_heads

    picked = lax.all_gather(adapter_selection, "dp", axis=0, tiled=True)
    owner = jnp.arange(adapter_cols)
    slot = jnp.arange(copies * rank)
    choose = (owner[:, None] // RANK == picked[slot // RANK][None, :]) & (owner[:, None] % RANK == slot[None, :] % RANK)
    choose_low = choose.astype(jnp.bfloat16)
    choose_wide = choose.astype(jnp.float32)
    choose_own = lax.dynamic_slice_in_dim(choose_low, me * rank, rank, 1)

    def first_of(matrix, chosen):
        return low(lax.dot_general(chosen, matrix, (((0,), (1,)), ((), ())), preferred_element_type=jnp.float32))

    def second_of(matrix, chosen):
        return low(over_tokens(chosen, matrix))

    def pack(by_row, by_col):
        shares = []
        for group, count, at in zip((by_row, by_col), (cols, rows), ("col", "row")):
            if not group:
                shares.append(jnp.zeros((0, lanes), jnp.bfloat16))
                continue
            joined = jnp.concatenate([v.reshape(-1, lanes) for v in group], axis=0)
            joined = jnp.pad(joined, ((0, -joined.shape[0] % count), (0, 0)))
            piece = joined.shape[0] // count
            shares.append(lax.dynamic_slice_in_dim(joined, lax.axis_index(at) * piece, piece, 0))
        return jnp.concatenate(shares, axis=0), shares[0].shape[0]

    def unpack(moved, share, by_row, by_col):
        of_rows = moved[:, :, :share].transpose(1, 0, 2, 3).reshape(rows, -1, lanes)
        count = -(-sum(v.size for v in by_col) // (lanes * rows))
        of_cols = moved[:, :, share : share + count].reshape(cols, -1, lanes)
        outs = []
        for group, source in zip((by_row, by_col), (of_rows, of_cols)):
            at, out = 0, []
            for v in group:
                size = v.size // lanes
                out.append(source[:, at : at + size].reshape((source.shape[0],) + v.shape))
                at += size
            outs.append(out)
        return outs

    def joined_rows(values):
        return values.transpose(1, 0, 2).reshape(values.shape[1], -1)

    def by_head(query, key, value):
        parts = []
        for j in range(kv_heads):
            at = slice(j * HEAD_DIM, (j + 1) * HEAD_DIM)
            parts += [query[:, j * head_q : (j + 1) * head_q], key[:, at], value[:, at]]
        return jnp.concatenate(parts, axis=1)

    half = me * width_ff
    width_qkv = width_q + 2 * width_kv
    gate_half = lax.dynamic_slice_in_dim(gate_weight, half, width_ff, 1)
    up_half = lax.dynamic_slice_in_dim(up_weight, half, width_ff, 1)
    down_half = lax.dynamic_slice_in_dim(down_weight, half, width_ff, 0)
    gate_second_half = lax.dynamic_slice_in_dim(gate_second_factor, half, width_ff, 1)
    up_second_half = lax.dynamic_slice_in_dim(up_second_factor, half, width_ff, 1)
    down_first_half = lax.dynamic_slice_in_dim(down_first_factor, half, width_ff, 0)

    attn_small = (
        [
            jnp.concatenate([first_of(m, choose_own) for m in (query_first_factor, key_first_factor, value_first_factor)]),
            jnp.stack([attention_norm_gain, feedforward_norm_gain]),
            second_of(output_second_factor, choose_own),
        ],
        [
            second_of(query_second_factor, choose_own),
            second_of(key_second_factor, choose_own),
            second_of(value_second_factor, choose_own),
            first_of(output_first_factor, choose_own),
        ],
    )
    packed, share = pack(*attn_small)
    (qkv_first, gains, out_second), (query_second, key_second, value_second, out_first) = unpack(
        lax.all_gather(packed, turned_both).reshape(cols, rows, -1, lanes), share, *attn_small
    )
    qkv_first = joined_rows(qkv_first)
    gains = joined_rows(gains).astype(jnp.float32)
    out_first = joined_rows(out_first)
    nothing = lambda m: jnp.zeros_like(m)
    qkv_second = jnp.stack(
        [
            jnp.concatenate(
                [
                    by_head(query_second[c], nothing(key_second[c]), nothing(value_second[c])),
                    by_head(nothing(query_second[c]), key_second[c], nothing(value_second[c])),
                    by_head(nothing(query_second[c]), nothing(key_second[c]), value_second[c]),
                ],
                axis=0,
            )
            for c in range(cols)
        ]
    )

    first_parts = [first_of(m, choose_low) for m in (gate_first_factor, up_first_factor)]
    hidden_parts = [
        second_of(gate_second_half, choose_low),
        second_of(up_second_half, choose_low),
        first_of(down_first_half, choose_low),
    ]
    of_group = lambda values, g: values[g * rank : (g + 1) * rank]
    mlp_small = [
        jnp.concatenate([of_group(m, g) for g in range(copies) for m in first_parts]),
        second_of(down_second_factor, choose_low),
    ]

    def middle(n):
        at = slice(n * lanes, (n + 1) * lanes)
        return jnp.stack(
            [
                jnp.stack([of_group(m, g)[:, at] for m in hidden_parts])
                for g in range(copies)
            ]
        )

    middles = [middle(n) for n in range(blocks_ff)]
    packed, mlp_share = pack(mlp_small, middles)
    packed = jnp.pad(packed, ((0, -packed.shape[0] % 16), (0, 0)))
    part_lanes = lanes // copies
    attn_weight = lax.all_gather(
        jnp.concatenate(
            [
                by_head(query_weight, key_weight, value_weight),
                lax.dynamic_slice_in_dim(output_weight, me * part_lanes, part_lanes, 1),
                jnp.zeros((lanes, 128), jnp.bfloat16),
            ],
            axis=1,
        ),
        turned_both,
        axis=0,
        tiled=True,
    ).reshape(cols, rows, lanes, -1)
    mlp_shards = [
        jnp.concatenate(
            [
                gate_half[:, n * lanes : (n + 1) * lanes],
                up_half[:, n * lanes : (n + 1) * lanes],
                down_half[n * lanes : (n + 1) * lanes],
            ]
            + ([packed] if n == 0 else []),
            axis=0,
        )
        for n in range(blocks_ff)
    ]

    row_seq = jnp.arange(seqs * part) // part
    mask = (row_seq[:, None] == jnp.arange(rank)[None, :] // RANK).astype(jnp.float32) * scale
    mask_thrice = jnp.tile(mask, (1, 3))

    positions = (lax.axis_index("col") * rows + lax.axis_index("row")) * part + jnp.arange(part)
    cosine, sine = rope_tables(jnp.tile(positions, seqs))
    flat, none = jnp.ones((seqs * part, HEAD_DIM), jnp.float32), jnp.zeros((seqs * part, HEAD_DIM), jnp.float32)
    turning = head_q // HEAD_DIM + 1
    cosine, sine = (
        jnp.tile(jnp.concatenate([jnp.tile(table, (1, 2 * turning)), rest], axis=1), (1, kv_heads))
        for table, rest in ((cosine, flat), (sine, none))
    )
    tokens, gains = ordered((tokens, gains))
    residual = to_tokens(tokens)
    cotangent, residual, mlp_shards, qkv_first, qkv_second, cosine, sine, mask_thrice, gains = ordered(
        (cotangent, residual, mlp_shards, qkv_first, qkv_second, cosine, sine, mask_thrice, gains)
    )
    upstream = to_tokens(cotangent)
    residual, upstream, mlp_shards[0] = ordered((residual, upstream, mlp_shards[0]))
    *messages, low_qkv = project_qkv(
        residual, gains[0:1], mask_thrice, qkv_first, qkv_second, cosine, sine, attn_weight, seqs, units, pairs, pair_width, kv_heads
    )

    def exchange(values):
        return lax.all_to_all(values.reshape(units, part, -1), turned_both, 0, 0, tiled=True)

    def to_messages(parts):
        return [v.reshape(seqs, cols, -1, part, pair_width) for v in parts]

    def padded(values):
        return jnp.pad(values, ((0, 0), (0, pair_pad)))

    first_in = exchange(messages[0]).reshape(length, -1)
    first_in, messages[1:], mlp_shards[1:] = ordered((first_in, messages[1:], mlp_shards[1:]))
    mlp_weights = [lax.all_gather(v, turned_both).reshape(cols, rows, -1, lanes) for v in mlp_shards]
    if pair_pad:
        unit_kv = (first_in[:, pair_width:], 0)
        unit_queries = [(padded(first_in[:, :pair_width]), 0)]
    else:
        unit_kv = (first_in, 1)
        unit_queries = [(first_in, 0)]
    unit_queries += [(padded(exchange(v).reshape(length, -1)), 0) for v in messages[1:]]
    unit_seq = (lax.axis_index("col") * rows + lax.axis_index("row")) * seqs // units
    labels = lax.dynamic_index_in_dim(block_labels, unit_seq, 0, keepdims=True)
    numbers = jnp.arange(BLOCKS)[:, None]
    ends_of = jnp.sum((labels <= numbers).astype(jnp.int32), axis=1, keepdims=True)
    ends = jnp.sum(jnp.where(labels == numbers, ends_of, 0), axis=0, keepdims=True)
    unit_outs, log_sums = [], []
    for p in range(pairs):
        out, log_sum = attend(unit_queries[p], unit_kv, ends, pair_heads, factor)
        unit_outs.append(out)
        log_sums.append(log_sum)
    heads_out = to_messages([exchange(v[:, :pair_width]) for v in unit_outs])
    (front_first, down_second), middles = unpack(
        mlp_weights[0][:, :, 3 * lanes :], mlp_share, mlp_small, middles
    )
    front_first, down_second = joined_rows(front_first), joined_rows(down_second)
    out_second = joined_rows(out_second)

    def swap(values, step):
        return lax.ppermute(values, "dp", [(i, (i + step) % copies) for i in range(copies)])

    out_weight = attn_weight[..., width_qkv : width_qkv + part_lanes]
    out_weights = [(attn_weight, width_qkv // part_lanes)] + [(swap(out_weight, step), 0) for step in range(1, copies)]
    this_copy = me.reshape(1)
    heads_out, front_first, down_second, middles = ordered((heads_out, front_first, down_second, middles))
    attended, normed_mlp, low_out = project_out(
        this_copy, heads_out, residual, gains[1:2], mask, out_first, out_second, out_weights
    )

    tokens_of = [(normed_mlp, upstream)]
    for step in range(1, copies):
        tokens_of.append((swap(normed_mlp, step), swap(upstream, step)))
    def second_of_group(step):
        return lax.dynamic_slice_in_dim(down_second, (me - step) % copies * rank, rank, 0)

    adapter_sums, grads, mixed = None, [None] * copies, [()] * copies
    for n in range(blocks_ff):
        last = n == blocks_ff - 1
        order = list(range(copies))
        hidden, low_down = [None] * copies, [None] * copies
        for step in order[1:] + order[:1] if last else order:
            adapter_sums, grads[step], hidden[step], low_down[step] = feed_forward(
                ((me - step) % copies).reshape(1),
                n,
                blocks_ff,
                *tokens_of[step],
                mask,
                front_first,
                down_second,
                mlp_weights[n],
                middles[n],
                adapter_sums,
                grads[step],
                jnp.float32 if not last or step == 0 else jnp.bfloat16,
            )
        if not last:
            mixed = [
                (project_down(second_of_group(step), hidden[step], low_down[step], mlp_weights[n], mixed[step], jnp.float32),)
                for step in range(copies)
            ]
            mlp_weights[n + 1], mixed = ordered((mlp_weights[n + 1], mixed))
    grad_part = grads[0]
    for step in range(1, copies):
        grad_back = swap(grads[step], -step)
        grad_other = grad_back if step == 1 else grad_other + grad_back

    attended_grad, out_rows, out_cols, *grad_messages = project_out_back(
        this_copy,
        grad_part,
        grad_other,
        upstream,
        attended,
        gains[1:2],
        mask,
        out_first,
        out_second,
        heads_out,
        low_out,
        out_weights,
        seqs,
        units,
        pair_width,
    )
    out_share, out_row, out_col = adapter_sums.shape[2], rank // cols, rank // rows
    shares = jnp.concatenate(
        [
            low(adapter_sums),
            out_rows.reshape(rows, cols, out_row, lanes),
            out_cols.reshape(cols, rows, out_col, lanes).transpose(1, 0, 2, 3),
        ],
        axis=2,
    )
    row_share, col_share = 3 * rank // cols, 3 * rank // rows
    row_height, col_height = share_height(row_share), share_height(col_share)
    grad_messages, hidden = ordered((grad_messages, hidden))
    mixed_own, *mixed_others = [
        project_down(
            second_of_group(step),
            hidden[step],
            low_down[step],
            mlp_weights[-1],
            mixed[step] + (() if step else (attended,)),
            jnp.bfloat16 if step else jnp.float32,
        )
        for step in range(copies)
    ]
    unit_grads = [padded(exchange(grad_messages[0]).reshape(length, -1))]
    ends, mixed_own, mixed_others, shares, unit_grads[0] = ordered((ends, mixed_own, mixed_others, shares, unit_grads[0]))
    shares = lax.psum_scatter(shares.reshape(units, -1, lanes), both, scatter_dimension=0)
    mixed_backs = [swap(v, -step) for step, v in enumerate(mixed_others, 1)]
    unit_grads[0], grad_messages[1:] = ordered((unit_grads[0], grad_messages[1:]))
    unit_grads += [padded(exchange(v).reshape(length, -1)) for v in grad_messages[1:]]
    full_cosine, full_sine = (table.T for table in rope_tables(jnp.arange(length)))
    query_moved, kv_grad = [], None
    for p in range(pairs):
        last = p == pairs - 1
        if last:
            if p > 0:
                shares, mixed_backs, kv_grad = ordered((shares, mixed_backs, kv_grad))
            mixed_parts = send_features(mixed_own, *mixed_backs)
            out_shares = shares[out_share:]
            shares = shares[:out_share].reshape(copies, -1, lanes)
            parts = (
                jnp.concatenate([shares[:, :row_share].reshape(-1, lanes), out_shares[:out_row]], axis=0),
                jnp.concatenate(
                    [
                        shares[:, row_height:].reshape(copies, blocks_ff, col_height, lanes)[:, :, :col_share].reshape(-1, lanes),
                        out_shares[out_row:],
                    ],
                    axis=0,
                ),
            )
            counts = [v.shape[0] for v in parts]
            parts = [jnp.pad(low(v), ((0, -v.shape[0] % GATHER_ROWS), (0, 0))) for v in parts]
            row_total = lax.all_gather(parts[0], ("dp", "col")).reshape(copies, cols, -1, lanes)
            col_total = lax.all_gather(parts[1], ("dp", "row")).reshape(copies, rows, -1, lanes)
        query_now, *kv_now = attend_back(
            unit_queries[p],
            unit_grads[p],
            unit_outs[p],
            log_sums[p],
            unit_kv,
            ends,
            full_cosine,
            full_sine,
            pair_heads,
            factor,
            kv_grad,
            last,
        )
        if last:
            query_now, mixed_parts, row_total, col_total, query_moved = ordered(
                (query_now, mixed_parts, row_total, col_total, query_moved)
            )
            if pair_pad:
                query_now = jnp.concatenate([query_now[:, :pair_width], query_now[:, -2 * HEAD_DIM :]], axis=1)
        else:
            kv_grad = kv_now[0]
            query_now = query_now[:, :pair_width]
        query_moved.append(exchange(query_now))
    mixed_out = join_features(mixed_parts, seqs)
    last_moved = query_moved[-1].reshape(seqs, cols, -1, part, pair_width + 2 * HEAD_DIM)
    if kv_copies > 1 or pair_pad:
        kv_moved = last_moved[..., pair_width:].reshape(seqs, cols, kv_heads, kv_copies, part, -1)
        kv_moved = (low(kv_moved.astype(jnp.float32).sum(axis=3)), 0, 2 * HEAD_DIM)
        last_moved = last_moved[..., :pair_width]
    else:
        kv_moved = (last_moved, pair_width // (2 * HEAD_DIM), 2 * HEAD_DIM)
    query_moved = [(v, 0, pair_width) for v in (*to_messages(query_moved[:-1]), last_moved)]
    lowered_qkv, qkv_rows, qkv_cols = qkv_grad_sums(
        residual, gains[0:1], mask_thrice, qkv_second, low_qkv, kv_moved, query_moved, rows
    )

    def everywhere(values, axes, count):
        copied = jnp.broadcast_to(low(values)[None], (count,) + values.shape)
        return lax.all_to_all(copied, axes, 0, 0, tiled=True).astype(jnp.float32).reshape(copies, -1, lanes)

    def wide_second(values):
        return lax.dot_general(
            choose_wide, values, (((1,), (0,)), ((), ())), precision=lax.Precision.HIGHEST, preferred_element_type=jnp.float32
        )

    def wide_first(values):
        return lax.dot_general(
            values, choose_wide, (((0,), (1,)), ((), ())), precision=lax.Precision.HIGHEST, preferred_element_type=jnp.float32
        )

    out_rows = row_total[:, :, counts[0] - out_row : counts[0]].astype(jnp.float32).reshape(-1, lanes)
    out_cols = col_total[:, :, counts[1] - out_col : counts[1]].astype(jnp.float32).reshape(-1, lanes)
    row_total = row_total[:, :, : counts[0] - out_row].astype(jnp.float32)
    row_total = row_total.reshape(copies, cols, copies, row_share, lanes).sum(axis=0)
    row_total = row_total.transpose(1, 0, 2, 3).reshape(copies, 3, rank, lanes)
    gate_first_gradient, up_first_gradient = (wide_first(row_total[:, i].reshape(-1, lanes)) for i in range(2))
    down_second_gradient = wide_second(row_total[:, 2].reshape(-1, lanes))
    col_total = col_total[:, :, : counts[1] - out_col].astype(jnp.float32)
    col_total = col_total.reshape(copies, rows, copies, blocks_ff, col_share, lanes)
    col_total = col_total.transpose(0, 2, 3, 1, 4, 5).reshape(copies, copies, blocks_ff, 3, rank, lanes)
    pieces = [
        [col_total[x, :, n, i].reshape(-1, lanes) for x in range(copies) for n in range(blocks_ff)] for i in range(3)
    ]
    gate_second_gradient, up_second_gradient = (
        jnp.concatenate([wide_second(v) for v in pieces[i]], axis=1) for i in range(2)
    )
    down_first_gradient = jnp.concatenate([wide_first(v) for v in pieces[2]], axis=0)

    row_cut = qkv_rows.reshape(rows, cols, -1, lanes)
    col_cut = qkv_cols.reshape(cols, rows, -1, lanes).transpose(1, 0, 2, 3)
    cut = row_cut.shape[2]
    attn_shares = jnp.concatenate([row_cut, col_cut], axis=2).reshape(units, -1, lanes)
    attn_shares, lowered_qkv = ordered((attn_shares, lowered_qkv))
    token_grad = project_qkv_back(
        residual, attended_grad, gains[0:1], qkv_first, lowered_qkv, kv_moved, query_moved, attn_weight, width_qkv
    )
    attn_sums = jnp.sum(lax.all_to_all(attn_shares, both, 0, 0, tiled=True).astype(jnp.float32), axis=0)
    token_parts = send_features(token_grad)
    attn_rows, token_parts[0] = ordered((attn_sums[:cut], token_parts[0]))
    attn_rows = everywhere(attn_rows, ("dp", "col"), copies * cols)
    attn_cols, attn_rows = ordered((attn_sums[cut:], attn_rows))
    attn_rows = attn_rows.reshape(copies, 3, rank, lanes)
    attn_cols = everywhere(attn_cols, ("dp", "row"), copies * rows)
    query_first_gradient, key_first_gradient, value_first_gradient = (
        wide_first(attn_rows[:, i].reshape(-1, lanes)) for i in range(3)
    )
    output_second_gradient = wide_second(out_rows)
    output_first_gradient = wide_first(out_cols)
    qkv_second_gradient = wide_second(attn_cols.reshape(copies * rank, -1)).reshape(
        adapter_cols, kv_heads, -1
    )
    query_second_gradient = qkv_second_gradient[..., :head_q].reshape(adapter_cols, -1)
    key_second_gradient = qkv_second_gradient[..., head_q : head_q + HEAD_DIM].reshape(adapter_cols, -1)
    value_second_gradient = qkv_second_gradient[..., head_q + HEAD_DIM :].reshape(adapter_cols, -1)

    return (
        mixed_out,
        join_features(token_parts, seqs),
        query_first_gradient,
        query_second_gradient,
        key_first_gradient,
        key_second_gradient,
        value_first_gradient,
        value_second_gradient,
        output_first_gradient,
        output_second_gradient,
        gate_first_gradient,
        gate_second_gradient,
        up_first_gradient,
        up_second_gradient,
        down_first_gradient,
        down_second_gradient,
    )


def solution(mesh):
    in_specs = (
        P("col", "dp", "row"),
        P("col", "dp", "row"),
        P("dp", None),
        P("dp"),
        P(),
        P("row"),
        P("row"),
        P("row", "col"),
        P("row", "col"),
        P("row", "col"),
        P("col", "row"),
        P("row", "col"),
        P("row", "col"),
        P("col", "row"),
        P("row", None),
        P(None, "col"),
        P("row", None),
        P(None, "col"),
        P("row", None),
        P(None, "col"),
        P("col", None),
        P(None, "row"),
        P("row", None),
        P(None, "col"),
        P("row", None),
        P(None, "col"),
        P("col", None),
        P(None, "row"),
    )
    out_specs = (
        P("col", "dp", "row"),
        P("col", "dp", "row"),
        P("row", None),
        P(None, "col"),
        P("row", None),
        P(None, "col"),
        P("row", None),
        P(None, "col"),
        P("col", None),
        P(None, "row"),
        P("row", None),
        P(None, "col"),
        P("row", None),
        P(None, "col"),
        P("col", None),
        P(None, "row"),
    )
    return jax.shard_map(local, mesh=mesh, in_specs=in_specs, out_specs=out_specs, check_vma=False)
```

```python
import functools, math
import jax, jax.numpy as jnp
from jax import lax
from jax.sharding import PartitionSpec as P
from jax.experimental import pallas as pl
from jax.experimental.pallas import tpu as pltpu

HEAD_DIM = 64
RANK = 16
BLOCKS = 32
EPS = 1e-05
ROPE_BASE = 500000.0
GATHER_ROWS = 128
TILE = 512
REACH = 256
LOG2E = math.log2(math.e)
NEG = -1e30


def nt(a, b):
    return lax.dot_general(a, b, (((1,), (1,)), ((), ())), preferred_element_type=jnp.float32)


def nn(a, b):
    return lax.dot_general(a, b, (((1,), (0,)), ((), ())), preferred_element_type=jnp.float32)


def half_of(x, e):
    lane = lax.broadcasted_iota(jnp.int32, x.shape, 1)
    return jnp.where((lane < 64) if e == 0 else (lane >= 64), x, jnp.zeros_like(x))


def doubled(kv):
    wide = kv.astype(jnp.float32)
    turned = pltpu.roll(wide, 64, 1)
    lane = lax.broadcasted_iota(jnp.int32, wide.shape, 1)
    return jnp.where(lane < 64, wide, turned).astype(jnp.bfloat16), jnp.where(lane < 64, turned, wide).astype(jnp.bfloat16)


def fwd_kernel(heads, factor, end_ref, q_ref, kv_ref, o_ref, lse_ref, acc_ref, m_ref, l_ref, k2_ref, vt_ref):
    i = pl.program_id(0)
    tq = q_ref.shape[0]
    q0 = i * tq
    c = factor * LOG2E

    @pl.when(i == 0)
    def _():
        for t in range(kv_ref.shape[0] // tq):
            rows = slice(t * tq, (t + 1) * tq)
            k2_ref[rows, :] = doubled(kv_ref[rows, :])[0]
            vt_ref[:, rows] = kv_ref[rows, :].astype(jnp.float32).T[64:, :].astype(jnp.bfloat16)

    ends = end_ref[...]
    m_ref[...] = jnp.full_like(m_ref, NEG)
    l_ref[...] = jnp.zeros_like(l_ref)
    acc_ref[...] = jnp.zeros_like(acc_ref)

    def tile(k0, size, masked):
        kk = k2_ref[pl.ds(k0, size), :]
        vv = vt_ref[:, pl.ds(k0, size)]
        if masked:
            allowed = (lax.broadcasted_iota(jnp.int32, (size, tq), 0) + k0) < ends
        for h in range(heads):
            qh = half_of(q_ref[:, (h // 2) * 128:(h // 2 + 1) * 128], h % 2)
            s = nt(kk, qh) * c
            if masked:
                s = jnp.where(allowed, s, NEG)
            m_old = m_ref[h:h + 1, :]
            m_new = jnp.maximum(m_old, jnp.max(s, axis=0, keepdims=True))
            p = jnp.exp2(s - m_new)
            alpha = jnp.exp2(m_old - m_new)
            l_ref[h:h + 1, :] = l_ref[h:h + 1, :] * alpha + jnp.sum(p, axis=0, keepdims=True)
            m_ref[h:h + 1, :] = m_new
            a = pl.ds(h * 64, 64)
            acc_ref[a, :] = acc_ref[a, :] * alpha + nn(vv, p.astype(jnp.bfloat16))

    def body(j, _):
        tile(pl.multiple_of(j * 2 * tq, tq), 2 * tq, False)
        return 0

    lax.fori_loop(0, i // 2, body, 0)
    last = pl.num_programs(0) - 1

    for odd in (False, True):
        for reach in (REACH, 0):

            @pl.when((i % 2 == int(odd)) & ((i < last) if reach else (i == last)))
            def _():
                before = tq if odd else 0
                tile(pl.multiple_of(q0 - before, tq), before + tq + reach, True)

    lse_ref[...] = m_ref[...] + jnp.log2(l_ref[...])
    inv = 1.0 / l_ref[...]
    for p in range(o_ref.shape[1] // 128):
        parts = []
        for h in (2 * p, 2 * p + 1):
            if h < heads:
                parts.append(acc_ref[h * 64:(h + 1) * 64, :] * inv[h:h + 1, :])
            else:
                parts.append(jnp.zeros((64, tq), jnp.float32))
        o_ref[:, p * 128:(p + 1) * 128] = jnp.concatenate(parts, axis=0).T.astype(o_ref.dtype)


def attend(q, kv, ends, heads, factor):
    (q, q_at), (kv, kv_at) = q, kv
    length, width = q.shape[0], 128
    tq = min(TILE, length)
    rows = 8
    return pl.pallas_call(
        functools.partial(fwd_kernel, heads, factor),
        grid=(length // tq,),
        in_specs=[
            pl.BlockSpec((1, tq), lambda i: (0, i)),
            pl.BlockSpec((tq, width), lambda i: (i, q_at)),
            pl.BlockSpec((length, 128), lambda i: (0, kv_at)),
        ],
        out_specs=[
            pl.BlockSpec((tq, width), lambda i: (i, 0)),
            pl.BlockSpec((rows, tq), lambda i: (0, i)),
        ],
        out_shape=[
            jax.ShapeDtypeStruct((length, width), jnp.bfloat16),
            jax.ShapeDtypeStruct((rows, length), jnp.float32),
        ],
        scratch_shapes=[
            pltpu.VMEM((heads * 64, tq), jnp.float32),
            pltpu.VMEM((rows, tq), jnp.float32),
            pltpu.VMEM((rows, tq), jnp.float32),
            pltpu.VMEM((length, 128), jnp.bfloat16),
            pltpu.VMEM((64, length), jnp.bfloat16),
        ],
        compiler_params=pltpu.CompilerParams(vmem_limit_bytes=48 * 2**20),
        cost_estimate=pl.CostEstimate(
            flops=2 * heads * length * length * 64, bytes_accessed=4 * length * width + length * 384, transcendentals=heads * length * length // 2
        ),
        name="attend_forward",
    )(ends, q, kv)


def turn_back(values, cosine, sine):
    high, rest = values[:32, :], values[32:, :]
    return jnp.concatenate([high * cosine + rest * sine, rest * cosine - high * sine], axis=0)


def bwd_kernel(heads, factor, last, end_ref, cos_ref, sin_ref, q_ref, do_ref, o_ref, lse_ref, kv_ref, *refs):
    if last:
        earlier_ref, dq_ref, *refs = refs
    else:
        dq_ref, dkv_ref, *refs = refs
    dqt_ref, delta_ref, dk_ref, dv_ref, k2_ref, v2_ref, kt_ref = refs
    j = pl.program_id(0)
    n = pl.num_programs(0)
    tk = kv_ref.shape[0]
    length, width = q_ref.shape
    c = factor * LOG2E
    k2_ref[...], v2_ref[...] = doubled(kv_ref[...])
    kt_ref[...] = kv_ref[...].astype(jnp.float32).T[:64, :].astype(jnp.bfloat16)

    @pl.when(j == 0)
    def _():
        dqt_ref[...] = jnp.zeros_like(dqt_ref)
        delta_ref[...] = jnp.zeros_like(delta_ref)
        for t in range(length // tk):
            rows = slice(t * tk, (t + 1) * tk)
            for p in range(width // 128):
                prod = do_ref[rows, p * 128:(p + 1) * 128].astype(jnp.float32) * o_ref[rows, p * 128:(p + 1) * 128].astype(jnp.float32)
                turned = prod.T
                for h in (2 * p, 2 * p + 1):
                    if h < heads:
                        delta_ref[h:h + 1, rows] = jnp.sum(turned[(h % 2) * 64:(h % 2 + 1) * 64, :], axis=0, keepdims=True)

    dk_ref[...] = jnp.zeros_like(dk_ref)
    dv_ref[...] = jnp.zeros_like(dv_ref)

    def tile(q0, count, size, masked):
        rows = pl.ds(q0, count)
        kk = k2_ref[:size, :]
        vv = v2_ref[:size, :]
        kt = kt_ref[:, :size]
        if masked:
            allowed = (lax.broadcasted_iota(jnp.int32, (size, count), 0) + j * tk) < end_ref[:, rows]
        for h in range(heads):
            lanes = slice((h // 2) * 128, (h // 2 + 1) * 128)
            qh = half_of(q_ref[rows, lanes], h % 2)
            gh = half_of(do_ref[rows, lanes], h % 2)
            s = nt(kk, qh) * c - lse_ref[h:h + 1, rows]
            if masked:
                s = jnp.where(allowed, s, NEG)
            p = jnp.exp2(s)
            dp = nt(vv, gh)
            ds = (p * (dp - delta_ref[h:h + 1, rows])).astype(jnp.bfloat16)
            dv_ref[:size, :] += nn(p.astype(jnp.bfloat16), gh)
            dk_ref[:size, :] += nn(ds, qh)
            dqt_ref[h * 64:(h + 1) * 64, rows] += nn(kt, ds)

    @pl.when(j > 0)
    def _():
        tile(pl.multiple_of((j - 1) * tk, tk), tk, REACH, True)

    rest = n - 1 - j
    for odd in (False, True):

        @pl.when(rest % 2 == int(odd))
        def _():
            tile(pl.multiple_of(j * tk, tk), 2 * tk if odd else tk, tk, True)

    def body(i, _):
        tile(pl.multiple_of((j + 1 + rest % 2 + 2 * i) * tk, tk), 2 * tk, tk, False)
        return 0

    lax.fori_loop(0, rest // 2, body, 0)

    own = pl.ds(pl.multiple_of(j * tk, tk), tk)
    dk = dk_ref[...].T
    dv = dv_ref[...].T
    dk = turn_back(dk[:64] + dk[64:], cos_ref[:, own], sin_ref[:, own]) * factor
    dkv = jnp.concatenate([dk, dv[:64] + dv[64:]], axis=0).T
    if last:
        dq_ref[own, width:] = (dkv if earlier_ref is None else dkv + earlier_ref[...]).astype(dq_ref.dtype)
    else:
        dkv_ref[...] = dkv

    @pl.when(j == n - 1)
    def _():
        for t in range(length // tk):
            rows = slice(t * tk, (t + 1) * tk)
            for p in range(width // 128):
                parts = []
                for h in (2 * p, 2 * p + 1):
                    if h < heads:
                        parts.append(turn_back(dqt_ref[h * 64:(h + 1) * 64, rows], cos_ref[:, rows], sin_ref[:, rows]) * factor)
                    else:
                        parts.append(jnp.zeros((64, tk), jnp.float32))
                dq_ref[rows, p * 128:(p + 1) * 128] = jnp.concatenate(parts, axis=0).T.astype(dq_ref.dtype)


def attend_back(q, do, o, lse, kv, ends, cosine, sine, heads, factor, earlier=None, last=True):
    (q, q_at), (kv, kv_at) = q, kv
    length, width = o.shape
    tk = min(TILE, length)
    whole = lambda shape, at=0: pl.BlockSpec(shape, lambda j: (0, at))
    by_block = lambda at=0: pl.BlockSpec((tk, 128), lambda j: (j, at))
    if last and earlier is None:
        earlier = jnp.zeros((length, 128), jnp.float32)
    return pl.pallas_call(
        functools.partial(bwd_kernel, heads, factor, last),
        grid=(length // tk,),
        in_specs=[
            whole((1, length)),
            whole((32, length)),
            whole((32, length)),
            whole((length, width), q_at),
            whole((length, width)),
            whole((length, width)),
            whole((8, length)),
            by_block(kv_at),
        ]
        + ([by_block()] if last else []),
        out_specs=[whole((length, width + 128))] if last else [whole((length, width)), by_block()],
        out_shape=[jax.ShapeDtypeStruct((length, width + 128), jnp.bfloat16)]
        if last
        else [jax.ShapeDtypeStruct((length, width), jnp.bfloat16), jax.ShapeDtypeStruct((length, 128), jnp.float32)],
        scratch_shapes=[
            pltpu.VMEM((heads * 64, length), jnp.float32),
            pltpu.VMEM((8, length), jnp.float32),
            pltpu.VMEM((tk, 128), jnp.float32),
            pltpu.VMEM((tk, 128), jnp.float32),
            pltpu.VMEM((tk, 128), jnp.bfloat16),
            pltpu.VMEM((tk, 128), jnp.bfloat16),
            pltpu.VMEM((64, tk), jnp.bfloat16),
        ],
        compiler_params=pltpu.CompilerParams(vmem_limit_bytes=48 * 2**20),
        cost_estimate=pl.CostEstimate(
            flops=5 * heads * length * length * 64,
            bytes_accessed=8 * length * width + length * 512,
            transcendentals=heads * length * length // 2,
        ),
        name="attend_backward",
    )(ends, cosine, sine, q, do, o, lse, kv, *([earlier] if last else []))


def buffered_once(shape, index_map):
    return pl.BlockSpec(shape, index_map, pipeline_mode=pl.Buffered(1))


def normalized(values, gain):
    inverse = lax.rsqrt(jnp.mean(values * values, axis=-1, keepdims=True) + EPS)
    return inverse, (values * inverse * gain).astype(jnp.bfloat16)


def norm_back(values, inverse, gain, upstream):
    scaled = upstream * gain
    weighted = jnp.mean(scaled * values, axis=-1, keepdims=True)
    return inverse * scaled - values * (inverse * inverse * inverse * weighted)


def qkv_kernel(pairs, kv_heads, token_ref, gain_ref, mask_ref, first_ref, second_ref, cos_ref, sin_ref, *refs):
    weight_refs, refs = refs[:3], refs[3:]
    message_refs, low_ref, normed_ref = refs[:pairs], refs[pairs], refs[pairs + 1]
    rows, lanes, chunk = weight_refs[0].shape[1:]
    count = token_ref.shape[0]
    seqs, _, units, part, _ = message_refs[0].shape
    pair_width = message_refs[0].shape[4] - 2 * HEAD_DIM

    @pl.when(pl.program_id(0) == 0)
    def _():
        _, normed = normalized(token_ref[...].astype(jnp.float32), gain_ref[...])
        normed_ref[...] = normed
        low_ref[...] = (nt(normed, first_ref[...]) * mask_ref[...]).astype(jnp.bfloat16)

    raw = jnp.concatenate(
        [nn(normed_ref[...], w[0].reshape(rows * lanes, chunk)) for w in weight_refs], axis=1
    ) + nn(low_ref[...], second_ref[0])
    width = raw.shape[1]
    lane = lax.broadcasted_iota(jnp.int32, raw.shape, 1)
    turned = jnp.where(lane % HEAD_DIM < HEAD_DIM // 2, -pltpu.roll(raw, width - HEAD_DIM // 2, 1), pltpu.roll(raw, HEAD_DIM // 2, 1))
    out = (raw * cos_ref[...] + turned * sin_ref[...]).astype(jnp.bfloat16)
    head_width = width // kv_heads
    for s in range(seqs):
        at = slice(s * part, (s + 1) * part)
        for u in range(units):
            base = u * kv_heads // units * head_width
            inside = u % (units // kv_heads) * pairs * pair_width
            kv = out[at, base + head_width - 2 * HEAD_DIM : base + head_width]
            for p in range(pairs):
                begin = base + inside + p * pair_width
                queries = out[at, begin : begin + pair_width]
                message_refs[p][s, 0, u] = jnp.concatenate([queries, kv], axis=1) if p == 0 else queries


def project_qkv(tokens, gain, mask, first, second, cosine, sine, weight, seqs, units, pairs, pair_width, kv_heads):
    count, features = tokens.shape
    cols, rows, lanes, _ = weight.shape
    width = second.shape[2]
    chunk = width // 3
    part = count // seqs
    whole = lambda shape: pl.BlockSpec(shape, lambda c: (0,) * len(shape))
    message = lambda wide: (seqs, cols, units // (seqs * cols), part, wide)
    widths = [pair_width + 2 * HEAD_DIM] + [pair_width] * (pairs - 1)
    block = lambda wide: pl.BlockSpec((seqs, 1) + message(wide)[2:], lambda c: (0, c, 0, 0, 0))
    weights = lambda at: pl.BlockSpec((1, rows, lanes, chunk), lambda c: (c, 0, 0, at))
    return pl.pallas_call(
        functools.partial(qkv_kernel, pairs, kv_heads),
        grid=(cols,),
        in_specs=[
            whole((count, features)),
            whole((1, features)),
            whole(mask.shape),
            whole(first.shape),
            pl.BlockSpec((1,) + second.shape[1:], lambda c: (c, 0, 0)),
            whole((count, width)),
            whole((count, width)),
            weights(0),
            weights(1),
            weights(2),
        ],
        out_specs=[block(w) for w in widths] + [whole(mask.shape)],
        out_shape=[jax.ShapeDtypeStruct(message(w), jnp.bfloat16) for w in widths]
        + [jax.ShapeDtypeStruct(mask.shape, jnp.bfloat16)],
        scratch_shapes=[pltpu.VMEM((count, features), jnp.bfloat16)],
        compiler_params=pltpu.CompilerParams(vmem_limit_bytes=48 * 2**20),
        cost_estimate=pl.CostEstimate(
            flops=2 * count * features * cols * width,
            bytes_accessed=2 * features * cols * width + 4 * count * features,
            transcendentals=count,
        ),
        name="project_qkv",
    )(tokens, gain, mask, first, second, cosine, sine, weight, weight, weight)


def lanes_of_unit(values, at, wide):
    return pl.BlockSpec((values.shape[0], 1) + values.shape[2:4] + (wide,), lambda c: (0, c, 0, 0, at))


def joined_messages(query_refs, kv_ref):
    seqs, _, kv_heads = kv_ref.shape[:3]
    units = query_refs[0].shape[2]
    parts = []
    for j in range(kv_heads):
        for u in range(j * units // kv_heads, (j + 1) * units // kv_heads):
            parts += [jnp.concatenate([q[s, 0, u] for s in range(seqs)], axis=0) for q in query_refs]
        parts.append(jnp.concatenate([kv_ref[s, 0, j] for s in range(seqs)], axis=0))
    return jnp.concatenate(parts, axis=1)


def qkv_sums_kernel(token_ref, gain_ref, mask_ref, second_ref, low_ref, kv_ref, *refs):
    query_refs, refs = refs[:-5], refs[-5:]
    lowered_out_ref, rows_ref, cols_ref, lowered_ref, low_turned_ref = refs
    c = pl.program_id(0)
    rows, _, lanes = rows_ref.shape
    kv_heads = kv_ref.shape[2]
    rank = mask_ref.shape[1] // 3

    @pl.when(c == 0)
    def _():
        lowered_ref[...] = jnp.zeros_like(lowered_ref)
        low_turned_ref[...] = low_ref[...].astype(jnp.float32).T.astype(jnp.bfloat16)

    e = joined_messages(query_refs, kv_ref)
    lowered_ref[...] += nt(e, second_ref[0])
    sums = nn(low_turned_ref[...], e)
    lane = lax.broadcasted_iota(jnp.int32, (rank, sums.shape[1]), 1) % (sums.shape[1] // kv_heads)
    query_lanes = sums.shape[1] // kv_heads - 2 * HEAD_DIM
    cols_ref[0] = jnp.where(
        lane < query_lanes,
        sums[:rank],
        jnp.where(lane < query_lanes + HEAD_DIM, sums[rank : 2 * rank], sums[2 * rank :]),
    ).astype(cols_ref.dtype)

    @pl.when(c == pl.num_programs(0) - 1)
    def _():
        lowered = lowered_ref[...] * mask_ref[...]
        lowered_out_ref[...] = lowered.astype(jnp.bfloat16)
        _, normed = normalized(token_ref[...].astype(jnp.float32), gain_ref[...])
        turned = nn(lowered.T.astype(jnp.bfloat16), normed)
        for r in range(rows):
            rows_ref[r] = turned[:, r * lanes : (r + 1) * lanes].astype(rows_ref.dtype)


def qkv_grad_sums(tokens, gain, mask, second, low_qkv, kv, queries, rows):
    count, features = tokens.shape
    cols, _, width = second.shape
    rank = mask.shape[1] // 3
    lanes = features // rows
    whole = lambda shape: buffered_once(shape, lambda c: (0,) * len(shape))
    return pl.pallas_call(
        qkv_sums_kernel,
        grid=(cols,),
        in_specs=[
            whole((count, features)),
            whole((1, features)),
            whole(mask.shape),
            pl.BlockSpec((1,) + second.shape[1:], lambda c: (c, 0, 0)),
            whole(low_qkv.shape),
            lanes_of_unit(*kv),
        ]
        + [lanes_of_unit(*q) for q in queries],
        out_specs=[
            pl.BlockSpec(mask.shape, lambda c: (0, 0)),
            pl.BlockSpec((rows, 3 * rank, lanes), lambda c: (0, 0, 0)),
            pl.BlockSpec((1, rank, width), lambda c: (c, 0, 0)),
        ],
        out_shape=[
            jax.ShapeDtypeStruct(mask.shape, jnp.bfloat16),
            jax.ShapeDtypeStruct((rows, 3 * rank, lanes), jnp.bfloat16),
            jax.ShapeDtypeStruct((cols, rank, width), jnp.bfloat16),
        ],
        scratch_shapes=[
            pltpu.VMEM((count, 3 * rank), jnp.float32),
            pltpu.VMEM((3 * rank, count), jnp.bfloat16),
        ],
        compiler_params=pltpu.CompilerParams(vmem_limit_bytes=48 * 2**20),
        cost_estimate=pl.CostEstimate(
            flops=2 * count * features * cols * width,
            bytes_accessed=2 * count * cols * width + 2 * count * features,
            transcendentals=count,
        ),
        name="qkv_grad_sums",
    )(tokens, gain, mask, second, low_qkv, kv[0], *[q[0] for q in queries])


def qkv_back_kernel(token_ref, attended_ref, gain_ref, first_ref, lowered_ref, kv_ref, *refs):
    query_refs, refs = refs[:-5], refs[-5:]
    weight_refs, (out_ref, grad_ref) = refs[:3], refs[3:]
    c = pl.program_id(0)
    rows, lanes, chunk = weight_refs[0].shape[1:]

    @pl.when(c == 0)
    def _():
        grad_ref[...] = nn(lowered_ref[...], first_ref[...])

    e = joined_messages(query_refs, kv_ref)
    for r in range(rows):
        total = nt(e[:, :chunk], weight_refs[0][0, r])
        for i in (1, 2):
            total += nt(e[:, i * chunk : (i + 1) * chunk], weight_refs[i][0, r])
        grad_ref[:, r * lanes : (r + 1) * lanes] += total

    @pl.when(c == pl.num_programs(0) - 1)
    def _():
        values = token_ref[...].astype(jnp.float32)
        inverse = lax.rsqrt(jnp.mean(values * values, axis=-1, keepdims=True) + EPS)
        out = (attended_ref[...] + norm_back(values, inverse, gain_ref[...], grad_ref[...])).astype(jnp.bfloat16)
        for r in range(rows):
            out_ref[r] = out[:, r * lanes : (r + 1) * lanes]


def project_qkv_back(tokens, attended_grad, gain, first, lowered, kv, queries, weight, width):
    count, features = tokens.shape
    cols, rows, lanes, _ = weight.shape
    chunk = width // 3
    whole = lambda shape: buffered_once(shape, lambda c: (0,) * len(shape))
    weights = lambda at: pl.BlockSpec((1, rows, lanes, chunk), lambda c: (c, 0, 0, at))
    return pl.pallas_call(
        qkv_back_kernel,
        grid=(cols,),
        in_specs=[
            whole((count, features)),
            whole((count, features)),
            whole((1, features)),
            whole(first.shape),
            whole(lowered.shape),
            lanes_of_unit(*kv),
        ]
        + [lanes_of_unit(*q) for q in queries]
        + [weights(0), weights(1), weights(2)],
        out_specs=pl.BlockSpec((rows, count, lanes), lambda c: (0, 0, 0)),
        out_shape=jax.ShapeDtypeStruct((rows, count, lanes), jnp.bfloat16),
        scratch_shapes=[pltpu.VMEM((count, features), jnp.float32)],
        compiler_params=pltpu.CompilerParams(vmem_limit_bytes=60 * 2**20),
        cost_estimate=pl.CostEstimate(
            flops=8 * count * features * cols * width,
            bytes_accessed=2 * features * cols * width + 10 * count * features,
            transcendentals=count,
        ),
        name="project_qkv_back",
    )(tokens, attended_grad, gain, first, lowered, kv[0], *[q[0] for q in queries], weight, weight, weight)


def mlp_kernel(fresh, goes_on, block, group_ref, h_ref, e_ref, mask_ref, first_ref, second_ref, gate_ref, up_ref, down_ref, mids_ref, *refs):
    if goes_on:
        sums_in_ref, grad_in_ref = refs[:2]
        refs = refs[2:]
    elif not fresh:
        refs = refs[1:]
    sums_ref, grad_out_ref, hidden_ref, low_down_ref = refs[:4]
    low_refs, turned_refs, sum_refs, arrived = refs[4:7], refs[7:10], refs[10:13], refs[13]
    grad_ref = refs[14] if len(refs) > 14 else grad_out_ref
    c = pl.program_id(0)
    rows, lanes = gate_ref.shape[1], gate_ref.shape[3]
    rank = second_ref.shape[0]

    def earlier(which):
        if which == 0:
            return pltpu.make_async_copy(grad_in_ref, grad_ref, arrived.at[0])
        height = sums_ref.shape[2]
        at = pl.ds(pl.multiple_of(group_ref[0] * height, 8), height)
        return pltpu.make_async_copy(sums_in_ref.at[:, :, at, :], sums_ref, arrived.at[1])

    def arrive(which):
        if goes_on:

            @pl.when(c == 0)
            def _():
                earlier(which).wait()

    @pl.when(c == 0)
    def _():
        if goes_on:
            earlier(0).start()
            earlier(1).start()
        low_front = nt(h_ref[...], first_ref[...])
        lows = low_front[:, :rank], low_front[:, rank:], nt(e_ref[...], second_ref[...])
        for low, low_ref, turned_ref, sum_ref in zip(lows, low_refs, turned_refs, sum_refs):
            low = low * mask_ref[...]
            low_ref[...] = low.astype(jnp.bfloat16)
            turned_ref[...] = low.T.astype(jnp.bfloat16)
            sum_ref[...] = jnp.zeros_like(sum_ref)
        if not goes_on:
            grad_ref[...] = jnp.zeros_like(grad_ref)
            sums_ref[...] = jnp.zeros_like(sums_ref)

    h = h_ref[...]
    gate_second, up_second, down_first = mids_ref[0, 0, 0], mids_ref[0, 0, 1], mids_ref[0, 0, 2]
    gate = nn(h, gate_ref[0].reshape(rows * lanes, lanes)) + nn(low_refs[0][...], gate_second)
    up = nn(h, up_ref[0].reshape(rows * lanes, lanes)) + nn(low_refs[1][...], up_second)
    upstream = nn(low_refs[2][...], down_first)
    for r in range(rows):
        upstream += nt(e_ref[:, r * lanes : (r + 1) * lanes], down_ref[0, r])
    sigmoid = 1.0 / (1.0 + jnp.exp(-gate))
    swish = gate * sigmoid
    hidden = (swish * up).astype(jnp.bfloat16)
    gate_grad = (upstream * up * (sigmoid + swish * (1.0 - sigmoid))).astype(jnp.bfloat16)
    up_grad = (upstream * swish).astype(jnp.bfloat16)
    arrive(0)
    for r in range(rows):
        at = slice(r * lanes, (r + 1) * lanes)
        grad_ref[:, at] += nt(gate_grad, gate_ref[0, r]) + nt(up_grad, up_ref[0, r])
    hidden_ref[...] = hidden
    outs = gate_grad, up_grad, hidden
    for out, sum_ref, middle in zip(outs, sum_refs, (gate_second, up_second, down_first)):
        sum_ref[...] += nt(out, middle)
    col_sum = jnp.concatenate([nn(turned_ref[...], out) for turned_ref, out in zip(turned_refs, outs)], axis=0)
    row_share, col_share = 3 * rank // sums_ref.shape[1], 3 * rank // rows
    begin = share_height(row_share) + block * share_height(col_share)
    arrive(1)
    for r in range(rows):
        sums_ref[r, c, begin : begin + col_share] = col_sum[r * col_share : (r + 1) * col_share]

    @pl.when(c == pl.num_programs(0) - 1)
    def _():
        gate_now, up_now, down_now = (sum_ref[...] * mask_ref[...] for sum_ref in sum_refs)
        front_now = jnp.concatenate([gate_now, up_now], axis=1)
        total = grad_ref[...] + nn(front_now.astype(jnp.bfloat16), first_ref[...])
        grad_out_ref[...] = total.astype(grad_out_ref.dtype)
        low_down_ref[...] = down_now.astype(jnp.bfloat16)
        row_sum = jnp.concatenate(
            [nn(v.T.astype(jnp.bfloat16), w[...]) for v, w in ((front_now, h_ref), (down_now, e_ref))], axis=0
        )
        for r in range(rows):
            now = row_sum[:, r * lanes : (r + 1) * lanes]
            for to in range(sums_ref.shape[1]):
                sums_ref[r, to, :row_share] += now[to * row_share : (to + 1) * row_share]


def share_height(count):
    return -(-count // 8) * 8


def feed_forward(group, block, blocks, h, e, mask, first, second, weight, mids, sums, earlier, dtype):
    count, features = h.shape
    cols, rows, _, lanes = weight.shape
    rank = mids.shape[3]
    groups = mids.shape[1]
    goes_on = earlier is not None
    fresh = sums is None
    whole = lambda shape: buffered_once(shape, lambda c, g: (0,) * len(shape))
    weights = lambda at: pl.BlockSpec((1, rows, lanes, lanes), lambda c, g: (c, 0, at, 0))
    height = share_height(3 * rank // cols) + blocks * share_height(3 * rank // rows)
    sums_shape = (rows, cols, height, lanes)
    anywhere = pl.BlockSpec(memory_space=pl.ANY)
    scratch = [pltpu.VMEM((count, rank), jnp.bfloat16)] * 3
    scratch += [pltpu.VMEM((rank, count), jnp.bfloat16)] * 3
    scratch += [pltpu.VMEM((count, rank), jnp.float32)] * 3
    scratch += [pltpu.SemaphoreType.DMA((2,))]
    if dtype != jnp.float32:
        scratch += [pltpu.VMEM((count, features), jnp.float32)]
    return pl.pallas_call(
        functools.partial(mlp_kernel, fresh, goes_on, block),
        grid_spec=pltpu.PrefetchScalarGridSpec(
            num_scalar_prefetch=1,
            grid=(cols,),
            in_specs=[
                whole((count, features)),
                whole((count, features)),
                whole((count, rank)),
                pl.BlockSpec((2 * rank, features), lambda c, g: (g[0], 0)),
                pl.BlockSpec((rank, features), lambda c, g: (g[0], 0)),
                weights(0),
                weights(1),
                weights(2),
                pl.BlockSpec((1, 1, 3, rank, lanes), lambda c, g: (c, g[0], 0, 0, 0)),
            ]
            + ([] if fresh else [anywhere])
            + ([anywhere] if goes_on else []),
            out_specs=[
                pl.BlockSpec(sums_shape, lambda c, g: (0, 0, g[0], 0)),
                pl.BlockSpec((count, features), lambda c, g: (0, 0)),
                pl.BlockSpec((count, lanes), lambda c, g: (0, c)),
                pl.BlockSpec((count, rank), lambda c, g: (0, 0)),
            ],
            scratch_shapes=scratch,
        ),
        out_shape=[
            jax.ShapeDtypeStruct((rows, cols, groups * height, lanes), jnp.float32),
            jax.ShapeDtypeStruct((count, features), dtype),
            jax.ShapeDtypeStruct((count, cols * lanes), jnp.bfloat16),
            jax.ShapeDtypeStruct((count, rank), jnp.bfloat16),
        ],
        input_output_aliases={} if fresh else {10: 0},
        compiler_params=pltpu.CompilerParams(vmem_limit_bytes=60 * 2**20),
        cost_estimate=pl.CostEstimate(
            flops=10 * count * features * cols * lanes,
            bytes_accessed=6 * features * cols * lanes + 12 * count * features,
            transcendentals=count * cols * lanes,
        ),
        name="feed_forward",
    )(group, h, e, mask, first, second, weight, weight, weight, mids, *([] if fresh else [sums]), *([earlier] if goes_on else []))


def down_kernel(second_ref, hidden_ref, low_ref, weight_ref, *refs):
    kept_refs, out_ref = refs[:-1], refs[-1]
    cols, lanes = weight_ref.shape[0], weight_ref.shape[3]
    total = nn(low_ref[...], second_ref[...]) + nn(hidden_ref[...], weight_ref[:, 0].reshape(cols * lanes, lanes))
    for v in kept_refs:
        total += (v[0] if len(v.shape) == 3 else v[...]).astype(jnp.float32)
    out_ref[0] = total.astype(out_ref.dtype)


def project_down(second, hidden, low_down, weight, kept, dtype):
    count = hidden.shape[0]
    cols, rows, _, lanes = weight.shape
    rank = low_down.shape[1]
    whole = lambda v: buffered_once(v.shape, lambda r: (0, 0))
    by_block = pl.BlockSpec((1, count, lanes), lambda r: (r, 0, 0))
    return pl.pallas_call(
        down_kernel,
        grid=(rows,),
        in_specs=[
            pl.BlockSpec((rank, lanes), lambda r: (0, r)),
            whole(hidden),
            whole(low_down),
            pl.BlockSpec((cols, 1, lanes, lanes), lambda r: (0, r, 2, 0)),
        ]
        + [by_block if v.ndim == 3 else pl.BlockSpec((count, lanes), lambda r: (0, r)) for v in kept],
        out_specs=by_block,
        out_shape=jax.ShapeDtypeStruct((rows, count, lanes), dtype),
        compiler_params=pltpu.CompilerParams(vmem_limit_bytes=48 * 2**20),
        cost_estimate=pl.CostEstimate(
            flops=2 * count * rows * lanes * cols * lanes,
            bytes_accessed=2 * rows * lanes * cols * lanes + 8 * count * rows * lanes,
            transcendentals=0,
        ),
        name="project_down",
    )(second, hidden, low_down, weight, *kept)


def lanes_of_part(me_ref, step, copies, r, lanes):
    wide = lanes // copies
    return pl.ds(pl.multiple_of(r * lanes + (me_ref[0] + copies - step) % copies * wide, wide), wide)


def out_kernel(pairs, copies, me_ref, *refs):
    message_refs, refs = refs[:pairs], refs[pairs:]
    residual_ref, gain_ref, mask_ref, first_ref, second_ref = refs[:5]
    weight_refs, (attended_ref, normed_ref, low_ref, heads_ref) = refs[5 : 5 + copies], refs[5 + copies :]
    r = pl.program_id(0)
    cols, lanes = weight_refs[0].shape[0], weight_refs[0].shape[2]

    @pl.when(r == 0)
    def _():
        seqs, _, units, part, width = message_refs[0].shape
        for s in range(seqs):
            for u in range(cols * units):
                for p in range(pairs):
                    begin = (u * pairs + p) * width
                    heads_ref[s * part : (s + 1) * part, begin : begin + width] = message_refs[p][s, u // units, u % units]
        low_ref[...] = (nt(heads_ref[...], first_ref[...]) * mask_ref[...]).astype(jnp.bfloat16)

    for step, weight_ref in enumerate(weight_refs):
        at = lanes_of_part(me_ref, step, copies, r, lanes)
        attended_ref[:, at] = (
            residual_ref[:, at].astype(jnp.float32)
            + nn(heads_ref[...], weight_ref[:, 0].reshape(cols * lanes, lanes // copies))
            + nn(low_ref[...], second_ref[:, at])
        )

    @pl.when(r == pl.num_programs(0) - 1)
    def _():
        normed_ref[...] = normalized(attended_ref[...], gain_ref[...])[1]


def project_out(me, messages, residual, gain, mask, first, second, weights):
    count, features = residual.shape
    cols, rows, lanes, _ = weights[0][0].shape
    copies = len(weights)
    rank = mask.shape[1]
    whole = lambda shape: buffered_once(shape, lambda r, m: (0,) * len(shape))
    part = lambda at: pl.BlockSpec((cols, 1, lanes, lanes // copies), lambda r, m: (0, r, 0, at))
    outs = [(count, features), (count, features), (count, rank)]
    return pl.pallas_call(
        functools.partial(out_kernel, len(messages), copies),
        grid_spec=pltpu.PrefetchScalarGridSpec(
            num_scalar_prefetch=1,
            grid=(rows,),
            in_specs=[whole(m.shape) for m in messages]
            + [whole((count, features)), whole((1, features)), whole((count, rank)), whole(first.shape), whole(second.shape)]
            + [part(at) for _, at in weights],
            out_specs=[pl.BlockSpec(shape, lambda r, m: (0, 0)) for shape in outs],
            scratch_shapes=[pltpu.VMEM((count, cols * lanes), jnp.bfloat16)],
        ),
        out_shape=[jax.ShapeDtypeStruct(s, t) for s, t in zip(outs, (jnp.float32, jnp.bfloat16, jnp.bfloat16))],
        compiler_params=pltpu.CompilerParams(vmem_limit_bytes=48 * 2**20),
        cost_estimate=pl.CostEstimate(
            flops=2 * count * features * cols * lanes,
            bytes_accessed=2 * features * cols * lanes + 10 * count * features,
            transcendentals=count,
        ),
        name="project_out",
    )(me, *messages, residual, gain, mask, first, second, *[w for w, _ in weights])


def out_back_kernel(
    pairs, copies, pair_width, me_ref, own_ref, other_ref, upstream_ref, attended_ref, gain_ref, mask_ref, first_ref, second_ref, low_ref, *refs
):
    weight_refs, refs = refs[:copies], refs[copies:]
    heads_refs, refs = refs[:pairs], refs[pairs:]
    attended_grad_ref, rows_ref, cols_ref, *refs = refs
    message_refs = refs[:pairs]
    e_ref, lowered_ref, lowered_turned_ref = refs[pairs:]
    c = pl.program_id(0)
    rows, lanes = weight_refs[0].shape[1:3]
    seqs, _, units, part, _ = message_refs[0].shape

    @pl.when(c == 0)
    def _():
        values = attended_ref[...]
        inverse = lax.rsqrt(jnp.mean(values * values, axis=-1, keepdims=True) + EPS)
        upstream = own_ref[...] + other_ref[...].astype(jnp.float32)
        total = upstream_ref[...].astype(jnp.float32) + norm_back(values, inverse, gain_ref[...], upstream)
        attended_grad_ref[...] = total
        e = total.astype(jnp.bfloat16)
        e_ref[...] = e
        lowered = nt(e, second_ref[...]) * mask_ref[...]
        lowered_ref[...] = lowered.astype(jnp.bfloat16)
        lowered_turned_ref[...] = lowered.T.astype(jnp.bfloat16)
        turned = nn(low_ref[...].astype(jnp.float32).T.astype(jnp.bfloat16), e)
        for r in range(rows):
            rows_ref[r] = turned[:, r * lanes : (r + 1) * lanes].astype(rows_ref.dtype)

    grad = nn(lowered_ref[...], first_ref[...])
    for r in range(rows):
        for step, weight_ref in enumerate(weight_refs):
            grad += nt(e_ref[:, lanes_of_part(me_ref, step, copies, r, lanes)], weight_ref[0, r])
    grad = grad.astype(jnp.bfloat16)
    for s in range(seqs):
        for u in range(units):
            for p in range(pairs):
                begin = (u * pairs + p) * pair_width
                message_refs[p][s, 0, u] = grad[s * part : (s + 1) * part, begin : begin + pair_width]
    heads = [jnp.concatenate([h[s, 0, u] for s in range(seqs)], axis=0) for u in range(units) for h in heads_refs]
    cols_ref[0] = nn(lowered_turned_ref[...], jnp.concatenate(heads, axis=1)).astype(cols_ref.dtype)


def project_out_back(me, own, other, upstream, attended, gain, mask, first, second, heads, low_out, weights, seqs, units, pair_width):
    count, features = attended.shape
    cols, rows, lanes, _ = weights[0][0].shape
    copies, pairs = len(weights), len(heads)
    rank = mask.shape[1]
    whole = lambda shape: buffered_once(shape, lambda c, m: (0,) * len(shape))
    message = (seqs, cols, units // (seqs * cols), count // seqs, pair_width)
    by_unit = pl.BlockSpec((seqs, 1) + message[2:], lambda c, m: (0, c, 0, 0, 0))
    return pl.pallas_call(
        functools.partial(out_back_kernel, pairs, copies, pair_width),
        grid_spec=pltpu.PrefetchScalarGridSpec(
            num_scalar_prefetch=1,
            grid=(cols,),
            in_specs=[whole((count, features))] * 4
            + [
                whole((1, features)),
                whole((count, rank)),
                pl.BlockSpec((rank, lanes), lambda c, m: (0, c)),
                whole((rank, features)),
                whole((count, rank)),
            ]
            + [
                pl.BlockSpec((1, rows, lanes, lanes // copies), functools.partial(lambda at, c, m: (c, 0, 0, at), at))
                for _, at in weights
            ]
            + [by_unit] * pairs,
            out_specs=[
                pl.BlockSpec((count, features), lambda c, m: (0, 0)),
                pl.BlockSpec((rows, rank, lanes), lambda c, m: (0, 0, 0)),
                pl.BlockSpec((1, rank, lanes), lambda c, m: (c, 0, 0)),
            ]
            + [by_unit] * pairs,
            scratch_shapes=[
                pltpu.VMEM((count, features), jnp.bfloat16),
                pltpu.VMEM((count, rank), jnp.bfloat16),
                pltpu.VMEM((rank, count), jnp.bfloat16),
            ],
        ),
        out_shape=[
            jax.ShapeDtypeStruct((count, features), jnp.float32),
            jax.ShapeDtypeStruct((rows, rank, lanes), jnp.bfloat16),
            jax.ShapeDtypeStruct((cols, rank, lanes), jnp.bfloat16),
        ]
        + [jax.ShapeDtypeStruct(message, jnp.bfloat16)] * pairs,
        compiler_params=pltpu.CompilerParams(vmem_limit_bytes=60 * 2**20),
        cost_estimate=pl.CostEstimate(
            flops=2 * count * features * cols * lanes,
            bytes_accessed=2 * features * cols * lanes + 18 * count * features,
            transcendentals=count,
        ),
        name="project_out_back",
    )(me, own, other, upstream, attended, gain, mask, first, second, low_out, *[w for w, _ in weights], *heads)


def dot(left, right):
    return lax.dot_general(left, right, (((1,), (0,)), ((), ())), preferred_element_type=jnp.float32)


def over_tokens(left, right):
    return lax.dot_general(left, right, (((0,), (0,)), ((), ())), preferred_element_type=jnp.float32)


def low(values):
    return values.astype(jnp.bfloat16)


ordered = lax.optimization_barrier


def to_tokens(values):
    rows = lax.axis_size("row")
    part, seqs, features = values.shape
    cut = values.reshape(rows, part // rows, seqs, features).transpose(0, 2, 1, 3)
    moved = lax.all_to_all(cut, "row", 0, 0, tiled=True)
    return moved.transpose(1, 2, 0, 3).reshape(seqs * (part // rows), rows * features)


def send_features(*terms):
    rows = terms[0].shape[0]
    me = lax.axis_index("row")
    parts = []
    for step in range(rows):
        blocks = [lax.dynamic_index_in_dim(v, (me + step) % rows, 0, keepdims=False) for v in terms]
        block = low(sum(v.astype(jnp.float32) for v in blocks)) if len(blocks) > 1 else blocks[0]
        if step:
            block = lax.ppermute(block, "row", [(i, (i + step) % rows) for i in range(rows)])
        parts.append(block)
    return parts


def join_features(parts, seqs):
    rows, width = len(parts), parts[0].shape[1]
    me = lax.axis_index("row")
    stacked = jnp.stack(parts)
    moved = jnp.stack(
        [lax.dynamic_index_in_dim(stacked, (me - source) % rows, 0, keepdims=False) for source in range(rows)]
    ).reshape(rows, seqs, -1, width)
    return moved.transpose(0, 2, 1, 3).reshape(-1, seqs, width)


def rope_tables(positions):
    half = HEAD_DIM // 2
    frequency = ROPE_BASE ** (-(jnp.arange(half).astype(jnp.float32) * 2.0) / HEAD_DIM)
    angles = positions.astype(jnp.float32)[:, None] * frequency[None, :]
    return lax.optimization_barrier((jnp.cos(angles), jnp.sin(angles)))


def diagonal(blocks):
    total = sum(b.shape[1] for b in blocks)
    out, at = [], 0
    for b in blocks:
        out.append(jnp.pad(b, ((0, 0), (at, total - at - b.shape[1]))))
        at += b.shape[1]
    return jnp.concatenate(out, axis=0)


def local(
    tokens,
    cotangent,
    block_labels,
    adapter_selection,
    adapter_scale,
    attention_norm_gain,
    feedforward_norm_gain,
    query_weight,
    key_weight,
    value_weight,
    output_weight,
    gate_weight,
    up_weight,
    down_weight,
    query_first_factor,
    query_second_factor,
    key_first_factor,
    key_second_factor,
    value_first_factor,
    value_second_factor,
    output_first_factor,
    output_second_factor,
    gate_first_factor,
    gate_second_factor,
    up_first_factor,
    up_second_factor,
    down_first_factor,
    down_second_factor,
):
    copies, rows, cols = lax.axis_size("dp"), lax.axis_size("row"), lax.axis_size("col")
    me = lax.axis_index("dp")
    units = rows * cols
    both, turned_both = ("row", "col"), ("col", "row")
    seqs = tokens.shape[1]
    part = tokens.shape[0] // rows
    length = part * units
    lanes = tokens.shape[2]
    scale = adapter_scale[0]
    width_q, width_kv = query_weight.shape[1], key_weight.shape[1]
    width_ff = gate_weight.shape[1] // copies
    blocks_ff = width_ff // lanes
    kv_heads = width_kv // HEAD_DIM
    heads = width_q * cols // HEAD_DIM * seqs // units
    pairs = -(-heads // 2)
    pair_heads = heads // pairs
    pair_width = pair_heads * HEAD_DIM
    pair_pad = -pair_width % 128
    kv_copies = max(1, units // (seqs * kv_heads * cols))
    adapter_cols = query_first_factor.shape[1]
    rank = seqs * RANK
    factor = HEAD_DIM ** (-0.5)
    head_q = width_q // kv_heads

    picked = lax.all_gather(adapter_selection, "dp", axis=0, tiled=True)
    owner = jnp.arange(adapter_cols)
    slot = jnp.arange(copies * rank)
    choose = (owner[:, None] // RANK == picked[slot // RANK][None, :]) & (owner[:, None] % RANK == slot[None, :] % RANK)
    choose_low = choose.astype(jnp.bfloat16)
    choose_wide = choose.astype(jnp.float32)
    choose_own = lax.dynamic_slice_in_dim(choose_low, me * rank, rank, 1)

    def first_of(matrix, chosen):
        return low(lax.dot_general(chosen, matrix, (((0,), (1,)), ((), ())), preferred_element_type=jnp.float32))

    def second_of(matrix, chosen):
        return low(over_tokens(chosen, matrix))

    def pack(by_row, by_col):
        shares = []
        for group, count, at in zip((by_row, by_col), (cols, rows), ("col", "row")):
            if not group:
                shares.append(jnp.zeros((0, lanes), jnp.bfloat16))
                continue
            joined = jnp.concatenate([v.reshape(-1, lanes) for v in group], axis=0)
            joined = jnp.pad(joined, ((0, -joined.shape[0] % count), (0, 0)))
            piece = joined.shape[0] // count
            shares.append(lax.dynamic_slice_in_dim(joined, lax.axis_index(at) * piece, piece, 0))
        return jnp.concatenate(shares, axis=0), shares[0].shape[0]

    def unpack(moved, share, by_row, by_col):
        of_rows = moved[:, :, :share].transpose(1, 0, 2, 3).reshape(rows, -1, lanes)
        count = -(-sum(v.size for v in by_col) // (lanes * rows))
        of_cols = moved[:, :, share : share + count].reshape(cols, -1, lanes)
        outs = []
        for group, source in zip((by_row, by_col), (of_rows, of_cols)):
            at, out = 0, []
            for v in group:
                size = v.size // lanes
                out.append(source[:, at : at + size].reshape((source.shape[0],) + v.shape))
                at += size
            outs.append(out)
        return outs

    def joined_rows(values):
        return values.transpose(1, 0, 2).reshape(values.shape[1], -1)

    def by_head(query, key, value):
        parts = []
        for j in range(kv_heads):
            at = slice(j * HEAD_DIM, (j + 1) * HEAD_DIM)
            parts += [query[:, j * head_q : (j + 1) * head_q], key[:, at], value[:, at]]
        return jnp.concatenate(parts, axis=1)

    half = me * width_ff
    width_qkv = width_q + 2 * width_kv
    gate_half = lax.dynamic_slice_in_dim(gate_weight, half, width_ff, 1)
    up_half = lax.dynamic_slice_in_dim(up_weight, half, width_ff, 1)
    down_half = lax.dynamic_slice_in_dim(down_weight, half, width_ff, 0)
    gate_second_half = lax.dynamic_slice_in_dim(gate_second_factor, half, width_ff, 1)
    up_second_half = lax.dynamic_slice_in_dim(up_second_factor, half, width_ff, 1)
    down_first_half = lax.dynamic_slice_in_dim(down_first_factor, half, width_ff, 0)

    attn_small = (
        [
            jnp.concatenate([first_of(m, choose_own) for m in (query_first_factor, key_first_factor, value_first_factor)]),
            jnp.stack([attention_norm_gain, feedforward_norm_gain]),
            second_of(output_second_factor, choose_own),
        ],
        [
            second_of(query_second_factor, choose_own),
            second_of(key_second_factor, choose_own),
            second_of(value_second_factor, choose_own),
            first_of(output_first_factor, choose_own),
        ],
    )
    packed, share = pack(*attn_small)
    (qkv_first, gains, out_second), (query_second, key_second, value_second, out_first) = unpack(
        lax.all_gather(packed, turned_both).reshape(cols, rows, -1, lanes), share, *attn_small
    )
    qkv_first = joined_rows(qkv_first)
    gains = joined_rows(gains).astype(jnp.float32)
    out_first = joined_rows(out_first)
    nothing = lambda m: jnp.zeros_like(m)
    qkv_second = jnp.stack(
        [
            jnp.concatenate(
                [
                    by_head(query_second[c], nothing(key_second[c]), nothing(value_second[c])),
                    by_head(nothing(query_second[c]), key_second[c], nothing(value_second[c])),
                    by_head(nothing(query_second[c]), nothing(key_second[c]), value_second[c]),
                ],
                axis=0,
            )
            for c in range(cols)
        ]
    )

    first_parts = [first_of(m, choose_low) for m in (gate_first_factor, up_first_factor)]
    hidden_parts = [
        second_of(gate_second_half, choose_low),
        second_of(up_second_half, choose_low),
        first_of(down_first_half, choose_low),
    ]
    of_group = lambda values, g: values[g * rank : (g + 1) * rank]
    mlp_small = [
        jnp.concatenate([of_group(m, g) for g in range(copies) for m in first_parts]),
        second_of(down_second_factor, choose_low),
    ]

    def middle(n):
        at = slice(n * lanes, (n + 1) * lanes)
        return jnp.stack(
            [
                jnp.stack([of_group(m, g)[:, at] for m in hidden_parts])
                for g in range(copies)
            ]
        )

    middles = [middle(n) for n in range(blocks_ff)]
    packed, mlp_share = pack(mlp_small, middles)
    packed = jnp.pad(packed, ((0, -packed.shape[0] % 16), (0, 0)))
    part_lanes = lanes // copies
    attn_weight = lax.all_gather(
        jnp.concatenate(
            [
                by_head(query_weight, key_weight, value_weight),
                lax.dynamic_slice_in_dim(output_weight, me * part_lanes, part_lanes, 1),
                jnp.zeros((lanes, 128), jnp.bfloat16),
            ],
            axis=1,
        ),
        turned_both,
        axis=0,
        tiled=True,
    ).reshape(cols, rows, lanes, -1)
    mlp_shards = [
        jnp.concatenate(
            [
                gate_half[:, n * lanes : (n + 1) * lanes],
                up_half[:, n * lanes : (n + 1) * lanes],
                down_half[n * lanes : (n + 1) * lanes],
            ]
            + ([packed] if n == 0 else []),
            axis=0,
        )
        for n in range(blocks_ff)
    ]

    row_seq = jnp.arange(seqs * part) // part
    mask = (row_seq[:, None] == jnp.arange(rank)[None, :] // RANK).astype(jnp.float32) * scale
    mask_thrice = jnp.tile(mask, (1, 3))

    positions = (lax.axis_index("col") * rows + lax.axis_index("row")) * part + jnp.arange(part)
    cosine, sine = rope_tables(jnp.tile(positions, seqs))
    flat, none = jnp.ones((seqs * part, HEAD_DIM), jnp.float32), jnp.zeros((seqs * part, HEAD_DIM), jnp.float32)
    turning = head_q // HEAD_DIM + 1
    cosine, sine = (
        jnp.tile(jnp.concatenate([jnp.tile(table, (1, 2 * turning)), rest], axis=1), (1, kv_heads))
        for table, rest in ((cosine, flat), (sine, none))
    )
    tokens, gains = ordered((tokens, gains))
    residual = to_tokens(tokens)
    cotangent, residual, mlp_shards, qkv_first, qkv_second, cosine, sine, mask_thrice, gains = ordered(
        (cotangent, residual, mlp_shards, qkv_first, qkv_second, cosine, sine, mask_thrice, gains)
    )
    upstream = to_tokens(cotangent)
    residual, upstream, mlp_shards[0] = ordered((residual, upstream, mlp_shards[0]))
    *messages, low_qkv = project_qkv(
        residual, gains[0:1], mask_thrice, qkv_first, qkv_second, cosine, sine, attn_weight, seqs, units, pairs, pair_width, kv_heads
    )

    def exchange(values):
        return lax.all_to_all(values.reshape(units, part, -1), turned_both, 0, 0, tiled=True)

    def to_messages(parts):
        return [v.reshape(seqs, cols, -1, part, pair_width) for v in parts]

    def padded(values):
        return jnp.pad(values, ((0, 0), (0, pair_pad)))

    first_in = exchange(messages[0]).reshape(length, -1)
    first_in, messages[1:], mlp_shards[1:] = ordered((first_in, messages[1:], mlp_shards[1:]))
    mlp_weights = [lax.all_gather(v, turned_both).reshape(cols, rows, -1, lanes) for v in mlp_shards]
    if pair_pad:
        unit_kv = (first_in[:, pair_width:], 0)
        unit_queries = [(padded(first_in[:, :pair_width]), 0)]
    else:
        unit_kv = (first_in, 1)
        unit_queries = [(first_in, 0)]
    unit_queries += [(padded(exchange(v).reshape(length, -1)), 0) for v in messages[1:]]
    unit_seq = (lax.axis_index("col") * rows + lax.axis_index("row")) * seqs // units
    labels = lax.dynamic_index_in_dim(block_labels, unit_seq, 0, keepdims=True)
    numbers = jnp.arange(BLOCKS)[:, None]
    ends_of = jnp.sum((labels <= numbers).astype(jnp.int32), axis=1, keepdims=True)
    ends = jnp.sum(jnp.where(labels == numbers, ends_of, 0), axis=0, keepdims=True)
    unit_outs, log_sums = [], []
    for p in range(pairs):
        out, log_sum = attend(unit_queries[p], unit_kv, ends, pair_heads, factor)
        unit_outs.append(out)
        log_sums.append(log_sum)
    heads_out = to_messages([exchange(v[:, :pair_width]) for v in unit_outs])
    (front_first, down_second), middles = unpack(
        mlp_weights[0][:, :, 3 * lanes :], mlp_share, mlp_small, middles
    )
    front_first, down_second = joined_rows(front_first), joined_rows(down_second)
    out_second = joined_rows(out_second)

    def swap(values, step):
        return lax.ppermute(values, "dp", [(i, (i + step) % copies) for i in range(copies)])

    out_weight = attn_weight[..., width_qkv : width_qkv + part_lanes]
    out_weights = [(attn_weight, width_qkv // part_lanes)] + [(swap(out_weight, step), 0) for step in range(1, copies)]
    this_copy = me.reshape(1)
    heads_out, front_first, down_second, middles = ordered((heads_out, front_first, down_second, middles))
    attended, normed_mlp, low_out = project_out(
        this_copy, heads_out, residual, gains[1:2], mask, out_first, out_second, out_weights
    )

    tokens_of = [(normed_mlp, upstream)]
    for step in range(1, copies):
        tokens_of.append((swap(normed_mlp, step), swap(upstream, step)))
    def second_of_group(step):
        return lax.dynamic_slice_in_dim(down_second, (me - step) % copies * rank, rank, 0)

    adapter_sums, grads, mixed = None, [None] * copies, [()] * copies
    for n in range(blocks_ff):
        last = n == blocks_ff - 1
        order = list(range(copies))
        hidden, low_down = [None] * copies, [None] * copies
        for step in order[1:] + order[:1] if last else order:
            adapter_sums, grads[step], hidden[step], low_down[step] = feed_forward(
                ((me - step) % copies).reshape(1),
                n,
                blocks_ff,
                *tokens_of[step],
                mask,
                front_first,
                down_second,
                mlp_weights[n],
                middles[n],
                adapter_sums,
                grads[step],
                jnp.float32 if not last or step == 0 else jnp.bfloat16,
            )
        if not last:
            mixed = [
                (project_down(second_of_group(step), hidden[step], low_down[step], mlp_weights[n], mixed[step], jnp.float32),)
                for step in range(copies)
            ]
            mlp_weights[n + 1], mixed = ordered((mlp_weights[n + 1], mixed))
    grad_part = grads[0]
    for step in range(1, copies):
        grad_back = swap(grads[step], -step)
        grad_other = grad_back if step == 1 else grad_other + grad_back

    attended_grad, out_rows, out_cols, *grad_messages = project_out_back(
        this_copy,
        grad_part,
        grad_other,
        upstream,
        attended,
        gains[1:2],
        mask,
        out_first,
        out_second,
        heads_out,
        low_out,
        out_weights,
        seqs,
        units,
        pair_width,
    )
    out_share, out_row, out_col = adapter_sums.shape[2], rank // cols, rank // rows
    shares = jnp.concatenate(
        [
            low(adapter_sums),
            out_rows.reshape(rows, cols, out_row, lanes),
            out_cols.reshape(cols, rows, out_col, lanes).transpose(1, 0, 2, 3),
        ],
        axis=2,
    )
    row_share, col_share = 3 * rank // cols, 3 * rank // rows
    row_height, col_height = share_height(row_share), share_height(col_share)
    grad_messages, hidden = ordered((grad_messages, hidden))
    mixed_own, *mixed_others = [
        project_down(
            second_of_group(step),
            hidden[step],
            low_down[step],
            mlp_weights[-1],
            mixed[step] + (() if step else (attended,)),
            jnp.bfloat16 if step else jnp.float32,
        )
        for step in range(copies)
    ]
    unit_grads = [padded(exchange(grad_messages[0]).reshape(length, -1))]
    ends, mixed_own, mixed_others, shares, unit_grads[0] = ordered((ends, mixed_own, mixed_others, shares, unit_grads[0]))
    shares = lax.psum_scatter(shares.reshape(units, -1, lanes), both, scatter_dimension=0)
    mixed_backs = [swap(v, -step) for step, v in enumerate(mixed_others, 1)]
    unit_grads[0], grad_messages[1:] = ordered((unit_grads[0], grad_messages[1:]))
    unit_grads += [padded(exchange(v).reshape(length, -1)) for v in grad_messages[1:]]
    full_cosine, full_sine = (table.T for table in rope_tables(jnp.arange(length)))
    query_moved, kv_grad = [], None
    for p in range(pairs):
        last = p == pairs - 1
        if last:
            if p > 0:
                shares, mixed_backs, kv_grad = ordered((shares, mixed_backs, kv_grad))
            mixed_parts = send_features(mixed_own, *mixed_backs)
            out_shares = shares[out_share:]
            shares = shares[:out_share].reshape(copies, -1, lanes)
            parts = (
                jnp.concatenate([shares[:, :row_share].reshape(-1, lanes), out_shares[:out_row]], axis=0),
                jnp.concatenate(
                    [
                        shares[:, row_height:].reshape(copies, blocks_ff, col_height, lanes)[:, :, :col_share].reshape(-1, lanes),
                        out_shares[out_row:],
                    ],
                    axis=0,
                ),
            )
            counts = [v.shape[0] for v in parts]
            parts = [jnp.pad(low(v), ((0, -v.shape[0] % GATHER_ROWS), (0, 0))) for v in parts]
            row_total = lax.all_gather(parts[0], ("dp", "col")).reshape(copies, cols, -1, lanes)
            col_total = lax.all_gather(parts[1], ("dp", "row")).reshape(copies, rows, -1, lanes)
        query_now, *kv_now = attend_back(
            unit_queries[p],
            unit_grads[p],
            unit_outs[p],
            log_sums[p],
            unit_kv,
            ends,
            full_cosine,
            full_sine,
            pair_heads,
            factor,
            kv_grad,
            last,
        )
        if last:
            query_now, mixed_parts, query_moved = ordered((query_now, mixed_parts, query_moved))
            if pair_pad:
                query_now = jnp.concatenate([query_now[:, :pair_width], query_now[:, -2 * HEAD_DIM :]], axis=1)
        else:
            kv_grad = kv_now[0]
            query_now = query_now[:, :pair_width]
        query_moved.append(exchange(query_now))
    mixed_out = join_features(mixed_parts, seqs)
    last_moved = query_moved[-1].reshape(seqs, cols, -1, part, pair_width + 2 * HEAD_DIM)
    if kv_copies > 1 or pair_pad:
        kv_moved = last_moved[..., pair_width:].reshape(seqs, cols, kv_heads, kv_copies, part, -1)
        kv_moved = (low(kv_moved.astype(jnp.float32).sum(axis=3)), 0, 2 * HEAD_DIM)
        last_moved = last_moved[..., :pair_width]
    else:
        kv_moved = (last_moved, pair_width // (2 * HEAD_DIM), 2 * HEAD_DIM)
    query_moved = [(v, 0, pair_width) for v in (*to_messages(query_moved[:-1]), last_moved)]
    lowered_qkv, qkv_rows, qkv_cols = qkv_grad_sums(
        residual, gains[0:1], mask_thrice, qkv_second, low_qkv, kv_moved, query_moved, rows
    )

    def everywhere(values, axes, count):
        copied = jnp.broadcast_to(low(values)[None], (count,) + values.shape)
        return lax.all_to_all(copied, axes, 0, 0, tiled=True).astype(jnp.float32).reshape(copies, -1, lanes)

    def wide_second(values):
        return lax.dot_general(
            choose_wide, values, (((1,), (0,)), ((), ())), precision=lax.Precision.HIGHEST, preferred_element_type=jnp.float32
        )

    def wide_first(values):
        return lax.dot_general(
            values, choose_wide, (((0,), (1,)), ((), ())), precision=lax.Precision.HIGHEST, preferred_element_type=jnp.float32
        )

    out_rows = row_total[:, :, counts[0] - out_row : counts[0]].astype(jnp.float32).reshape(-1, lanes)
    out_cols = col_total[:, :, counts[1] - out_col : counts[1]].astype(jnp.float32).reshape(-1, lanes)
    row_total = row_total[:, :, : counts[0] - out_row].astype(jnp.float32)
    row_total = row_total.reshape(copies, cols, copies, row_share, lanes).sum(axis=0)
    row_total = row_total.transpose(1, 0, 2, 3).reshape(copies, 3, rank, lanes)
    gate_first_gradient, up_first_gradient = (wide_first(row_total[:, i].reshape(-1, lanes)) for i in range(2))
    down_second_gradient = wide_second(row_total[:, 2].reshape(-1, lanes))
    col_total = col_total[:, :, : counts[1] - out_col].astype(jnp.float32)
    col_total = col_total.reshape(copies, rows, copies, blocks_ff, col_share, lanes)
    col_total = col_total.transpose(0, 2, 3, 1, 4, 5).reshape(copies, copies, blocks_ff, 3, rank, lanes)
    pieces = [
        [col_total[x, :, n, i].reshape(-1, lanes) for x in range(copies) for n in range(blocks_ff)] for i in range(3)
    ]
    gate_second_gradient, up_second_gradient = (
        jnp.concatenate([wide_second(v) for v in pieces[i]], axis=1) for i in range(2)
    )
    down_first_gradient = jnp.concatenate([wide_first(v) for v in pieces[2]], axis=0)

    row_cut = qkv_rows.reshape(rows, cols, -1, lanes)
    col_cut = qkv_cols.reshape(cols, rows, -1, lanes).transpose(1, 0, 2, 3)
    cut = row_cut.shape[2]
    attn_shares = jnp.concatenate([row_cut, col_cut], axis=2).reshape(units, -1, lanes)
    attn_shares, lowered_qkv = ordered((attn_shares, lowered_qkv))
    token_grad = project_qkv_back(
        residual, attended_grad, gains[0:1], qkv_first, lowered_qkv, kv_moved, query_moved, attn_weight, width_qkv
    )
    attn_sums = jnp.sum(lax.all_to_all(attn_shares, both, 0, 0, tiled=True).astype(jnp.float32), axis=0)
    token_parts = send_features(token_grad)
    attn_sums, row_total, col_total = ordered((attn_sums, row_total, col_total))
    attn_rows, token_parts[0] = ordered((attn_sums[:cut], token_parts[0]))
    attn_rows = everywhere(attn_rows, ("dp", "col"), copies * cols)
    attn_cols, attn_rows = ordered((attn_sums[cut:], attn_rows))
    attn_rows = attn_rows.reshape(copies, 3, rank, lanes)
    attn_cols = everywhere(attn_cols, ("dp", "row"), copies * rows)
    query_first_gradient, key_first_gradient, value_first_gradient = (
        wide_first(attn_rows[:, i].reshape(-1, lanes)) for i in range(3)
    )
    output_second_gradient = wide_second(out_rows)
    output_first_gradient = wide_first(out_cols)
    qkv_second_gradient = wide_second(attn_cols.reshape(copies * rank, -1)).reshape(
        adapter_cols, kv_heads, -1
    )
    query_second_gradient = qkv_second_gradient[..., :head_q].reshape(adapter_cols, -1)
    key_second_gradient = qkv_second_gradient[..., head_q : head_q + HEAD_DIM].reshape(adapter_cols, -1)
    value_second_gradient = qkv_second_gradient[..., head_q + HEAD_DIM :].reshape(adapter_cols, -1)

    return (
        mixed_out,
        join_features(token_parts, seqs),
        query_first_gradient,
        query_second_gradient,
        key_first_gradient,
        key_second_gradient,
        value_first_gradient,
        value_second_gradient,
        output_first_gradient,
        output_second_gradient,
        gate_first_gradient,
        gate_second_gradient,
        up_first_gradient,
        up_second_gradient,
        down_first_gradient,
        down_second_gradient,
    )


def solution(mesh):
    in_specs = (
        P("col", "dp", "row"),
        P("col", "dp", "row"),
        P("dp", None),
        P("dp"),
        P(),
        P("row"),
        P("row"),
        P("row", "col"),
        P("row", "col"),
        P("row", "col"),
        P("col", "row"),
        P("row", "col"),
        P("row", "col"),
        P("col", "row"),
        P("row", None),
        P(None, "col"),
        P("row", None),
        P(None, "col"),
        P("row", None),
        P(None, "col"),
        P("col", None),
        P(None, "row"),
        P("row", None),
        P(None, "col"),
        P("row", None),
        P(None, "col"),
        P("col", None),
        P(None, "row"),
    )
    out_specs = (
        P("col", "dp", "row"),
        P("col", "dp", "row"),
        P("row", None),
        P(None, "col"),
        P("row", None),
        P(None, "col"),
        P("row", None),
        P(None, "col"),
        P("col", None),
        P(None, "row"),
        P("row", None),
        P(None, "col"),
        P("row", None),
        P(None, "col"),
        P("col", None),
        P(None, "row"),
    )
    return jax.shard_map(local, mesh=mesh, in_specs=in_specs, out_specs=out_specs, check_vma=False)
```
